32 devices in a mesh: cells: 4 (over y, x), genes: 8 (over z, core).
Axes of the slice: x: 2, y: 2, z: 4, core: 2. Of those that a mesh axis runs over, the one named last changes fastest.
Arguments:
- counts: int32 [8192, 20480], P('cells', 'genes'), may hold values from 0 to 22, as said below
- batch_ids: int32 [8192], P('cells'), may hold values from 0 to 63
- dataset_ids: int32 [8192], P('cells'), may hold values from 0 to 7
- variable_mask: int32 [8, 20480], P(None, 'genes'), may hold values 0 or 1
- latent_noise: float32 [8192, 10], P('cells'), may hold values from -4 to 4
- encoder_weight: bfloat16 [20480, 128], P('genes'), may hold values from -0.0390625 to 0.0390625
- encoder_batch: float32 [64, 128], replicated, may hold values from -5 to 5
- encoder_gain: float32 [128], replicated, may hold values from 0.5 to 1.5
- encoder_shift: float32 [128], replicated, may hold values from -3 to 3
- mean_weight: float32 [128, 10], replicated, may hold values from -0.5 to 0.5
- mean_bias: float32 [10], replicated, may hold values from -3 to 3
- logvar_weight: float32 [128, 10], replicated, may hold values from -0.5 to 0.5
- logvar_bias: float32 [10], replicated, may hold values from -3 to 3
- decoder_latent: float32 [10, 128], replicated, may hold values from -2 to 2
- decoder_batch: float32 [64, 128], replicated, may hold values from -5 to 5
- decoder_gain: float32 [128], replicated, may hold values from 0.5 to 1.5
- decoder_shift: float32 [128], replicated, may hold values from -3 to 3
- scale_weight: bfloat16 [128, 20480], P(None, 'genes'), may hold values from -0.5 to 0.5
- scale_bias: float32 [20480], P('genes'), may hold values from -4 to 4
- dropout_weight: bfloat16 [128, 20480], P(None, 'genes'), may hold values from -0.5 to 0.5
- dropout_bias: float32 [20480], P('genes'), may hold values from -4 to 4
- log_theta: float32 [20480], P('genes'), may hold values from -1 to 2
Outputs:
- mean_loss: float32 [], replicated
- input_gradient: float32 [8192, 20480], P('cells', 'genes')
- encoder_weight_grad: float32 [20480, 128], P('genes')
- encoder_batch_grad: float32 [64, 128], replicated
- encoder_gain_grad: float32 [128], replicated
- encoder_shift_grad: float32 [128], replicated
- mean_weight_grad: float32 [128, 10], replicated
- mean_bias_grad: float32 [10], replicated
- logvar_weight_grad: float32 [128, 10], replicated
- logvar_bias_grad: float32 [10], replicated
- decoder_latent_grad: float32 [10, 128], replicated
- decoder_batch_grad: float32 [64, 128], replicated
- decoder_gain_grad: float32 [128], replicated
- decoder_shift_grad: float32 [128], replicated
- scale_weight_grad: float32 [128, 20480], P(None, 'genes')
- scale_bias_grad: float32 [20480], P('genes')
- dropout_weight_grad: float32 [128, 20480], P(None, 'genes')
- dropout_bias_grad: float32 [20480], P('genes')
- log_theta_grad: float32 [20480], P('genes')
The draws below stay inside these ranges and needn't reach their ends.
Inputs may be any that keep to these rules, and one draw needn't show every extreme that they name: counts of each cell and gene, zero in most entries.
All inputs are finite; a program needn't handle non-finite values. No bound on the sum of `variable_mask` on one device may be relied on, other than what follows from the above.
Results may differ from the reference program's by a relative error of at most 0.0064.
Values may be sent and summed in bfloat16 or wider, within the bound.
No kernel may reach another device: no remote copies, remote signals or barrier semaphores. Data moves between devices by JAX's collectives and lax.ppermute only.
A program may use at most 256 MiB of HBM per device.

```python
import math
import jax
import jax.numpy as jnp
from jax import lax

G = 20480
H = 128
L = 10
NB = 64
ND = 8
TOKENS = 8192


def draw_counts(key, part):
    key = jax.random.fold_in(key, 11)
    first_key, second_key, third_key = jax.random.split(key, 3)
    row_limit = jax.random.randint(first_key, (TOKENS, 1), 2, 24)
    values = jax.random.randint(second_key, (TOKENS, G), 0, 1 << 20) % row_limit
    keeper = jax.random.randint(third_key, (TOKENS, G), 0, 5)
    result = jnp.where(keeper < 2, values, 0)
    corner = (jnp.arange(TOKENS)[:, None] == 0) & (jnp.arange(G)[None, :] == 0)
    return jnp.where(corner, 22, result).astype(jnp.int32)


def set_ends(entries, key, low, top_value):
    index_at = [jax.random.randint(jax.random.fold_in(key, axis), (), 0, length) for axis, length in enumerate(entries.shape)]
    main_axis = entries.shape.index(max(entries.shape))
    beside = index_at[:main_axis] + [(index_at[main_axis] + 1) % entries.shape[main_axis]] + index_at[main_axis + 1:]
    return entries.at[tuple(index_at)].set(low).at[tuple(beside)].set(top_value)


def steps_of(key, dims, pieces, smallest, largest):
    loudness = 1.0
    for dim, parts in pieces:
        heights = jax.random.uniform(jax.random.fold_in(jax.random.fold_in(key, 6), dim), (parts,), jnp.float32, smallest / len(pieces), largest / len(pieces))
        loudness = loudness * jnp.repeat(jnp.exp(heights), dims[dim] // parts).reshape((-1,) + (1,) * (len(dims) - 1 - dim))
    return loudness


def noise(rng, shape, width, bound, cuts=(), kind=jnp.bfloat16):
    gain = steps_of(rng, shape, cuts, -0.22, 0.18) if cuts else 1.0
    drawn = jax.random.normal(rng, shape, jnp.float32) * width * gain
    return jnp.minimum(jnp.maximum(drawn, -bound), bound).astype(kind)


def setup_inputs(seed: int = 0) -> dict:
    keys = jax.random.split(jax.random.key(seed), 23)
    return {
        "counts": draw_counts(jax.random.fold_in(keys[22], 71), 0),
        "batch_ids": set_ends(jax.random.randint(keys[1], (TOKENS,), 0, NB), jax.random.fold_in(keys[1], 1), 0, NB - 1).astype(jnp.int32),
        "dataset_ids": set_ends(jax.random.randint(keys[2], (TOKENS,), 0, ND), jax.random.fold_in(keys[2], 1), 0, ND - 1).astype(jnp.int32),
        "variable_mask": set_ends((jax.random.randint(keys[3], (ND, G), 0, 8) < 1).astype(jnp.int32), jax.random.fold_in(keys[3], 1), 0, 1),
        "latent_noise": noise(keys[4], (TOKENS, L), 1.0, 4.0, ((0, 4),), jnp.float32),
        "encoder_weight": noise(keys[5], (G, H), G ** -0.5, 0.0390625, ((0, 8),)),
        "encoder_batch": noise(keys[6], (NB, H), 1.0, 5.0, (), jnp.float32),
        "encoder_gain": jnp.clip(1.0 + 0.1 * jax.random.normal(keys[7], (H,), jnp.float32), 0.5, 1.5),
        "encoder_shift": noise(keys[8], (H,), 0.5, 3.0, (), jnp.float32),
        "mean_weight": noise(keys[9], (H, L), H ** -0.5, 0.5, (), jnp.float32),
        "mean_bias": noise(keys[10], (L,), 0.5, 3.0, (), jnp.float32),
        "logvar_weight": noise(keys[11], (H, L), H ** -0.5, 0.5, (), jnp.float32),
        "logvar_bias": noise(keys[12], (L,), 0.5, 3.0, (), jnp.float32),
        "decoder_latent": noise(keys[13], (L, H), L ** -0.5, 2.0, (), jnp.float32),
        "decoder_batch": noise(keys[14], (NB, H), 1.0, 5.0, (), jnp.float32),
        "decoder_gain": jnp.clip(1.0 + 0.1 * jax.random.normal(keys[15], (H,), jnp.float32), 0.5, 1.5),
        "decoder_shift": noise(keys[16], (H,), 0.5, 3.0, (), jnp.float32),
        "scale_weight": noise(keys[17], (H, G), H ** -0.5, 0.5, ((1, 8),)),
        "scale_bias": noise(keys[18], (G,), 1.0, 4.0, ((0, 8),), jnp.float32),
        "dropout_weight": noise(keys[19], (H, G), H ** -0.5, 0.5, ((1, 8),)),
        "dropout_bias": noise(keys[20], (G,), 1.0, 4.0, ((0, 8),), jnp.float32),
        "log_theta": jnp.clip(-1.0 + 3.0 * jax.random.uniform(keys[21], (G,), jnp.float32) ** steps_of(keys[21], (G,), ((0, 8),), -0.2, 0.2), -1.0, 2.0),
    }


@jax.custom_vjp
def low(v):
    return lax.optimization_barrier(v.astype(jnp.bfloat16)).astype(jnp.float32)

@jax.custom_vjp
def low_back(v):
    return v

def low_keep(v):
    return (low(v), None)

def low_pass(kept, grad):
    return (grad,)

def back_keep(v):
    return (v, None)

def back_low(kept, grad):
    return (low(grad),)
low.defvjp(low_keep, low_pass)
low_back.defvjp(back_keep, back_low)
highest = lax.Precision.HIGHEST
norm_eps = 0.001
log_eps = 1e-08

def batch_norm(pre_norm, norm_gain, norm_shift):
    center = lax.optimization_barrier(jnp.mean(pre_norm, axis=0))
    variance = lax.optimization_barrier(jnp.mean((pre_norm - center) ** 2, axis=0))
    gated = (pre_norm - center) * lax.rsqrt(variance + norm_eps) * norm_gain + norm_shift
    return gated * jax.nn.sigmoid(gated)

def zinb_terms(count_rows, is_zero, expected, dropout, dispersion):
    log_disp = jnp.log(dispersion + log_eps)
    log_both = jnp.log(dispersion + expected + log_eps)
    soft_dropout = jax.nn.softplus(-dropout)
    joint_term = -dropout + dispersion * (log_disp - log_both)
    zero_case = jax.nn.softplus(joint_term) - soft_dropout
    other_case = joint_term - soft_dropout + count_rows * (jnp.log(expected + log_eps) - log_both) + lax.lgamma(count_rows + dispersion) - lax.lgamma(dispersion) - lax.lgamma(count_rows + 1.0)
    return jnp.where(is_zero, zero_case, other_case)

def reference(counts, batch_ids, dataset_ids, variable_mask, latent_noise, encoder_weight, encoder_batch, encoder_gain, encoder_shift, mean_weight, mean_bias, logvar_weight, logvar_bias, decoder_latent, decoder_batch, decoder_gain, decoder_shift, scale_weight, scale_bias, dropout_weight, dropout_bias, log_theta):
    block_rows = math.gcd(TOKENS, 512)
    block_count = TOKENS // block_rows
    expression = jnp.log1p(counts.astype(jnp.float32))
    batch_hot = (batch_ids[:, None] == jnp.arange(NB)[None, :]).astype(jnp.float32)
    mask_float = variable_mask.astype(jnp.float32)
    params = tuple((weight_item.astype(jnp.float32) for weight_item in (encoder_weight, encoder_batch, encoder_gain, encoder_shift, mean_weight, mean_bias, logvar_weight, logvar_bias, decoder_latent, decoder_batch, decoder_gain, decoder_shift, scale_weight, scale_bias, dropout_weight, dropout_bias, log_theta)))

    def forward(expr_input, weights):
        enc_weight, enc_batch, enc_gain, enc_shift, head_mean, bias_mean, head_logvar, bias_logvar, dec_latent, dec_batch, dec_gain, dec_shift, gene_scale, bias_scale, gene_dropout, bias_dropout, theta_log = weights

        def encode_block(piece):
            return jnp.dot(low(piece), enc_weight, precision=highest)
        pre_genes = lax.map(jax.checkpoint(encode_block), expr_input.reshape(block_count, block_rows, G)).reshape(TOKENS, H)
        encoder_pre = low_back(pre_genes + jnp.dot(batch_hot, enc_batch, precision=highest))
        encoder_act = batch_norm(encoder_pre, enc_gain, enc_shift)
        latent_mean = jnp.dot(encoder_act, head_mean, precision=highest) + bias_mean
        latent_logvar = jnp.dot(encoder_act, head_logvar, precision=highest) + bias_logvar
        latent = latent_mean + jnp.exp(0.5 * latent_logvar) * latent_noise
        kl_total = 0.5 * jnp.sum(jnp.exp(latent_logvar) + latent_mean * latent_mean - 1.0 - latent_logvar)
        decoder_pre = jnp.dot(latent, dec_latent, precision=highest) + jnp.dot(batch_hot, dec_batch, precision=highest)
        hidden = low(batch_norm(decoder_pre, dec_gain, dec_shift))
        dispersion = jnp.exp(theta_log)

        def decode_block(carry, block):
            hidden_rows, count_rows, data_rows = block
            scale_logit = low_back(jnp.dot(hidden_rows, gene_scale, precision=highest) + bias_scale)
            dropout_logit = low_back(jnp.dot(hidden_rows, gene_dropout, precision=highest) + bias_dropout)
            row_top = lax.optimization_barrier(jnp.max(scale_logit, axis=1, keepdims=True))
            exponent = jnp.exp(scale_logit - row_top)
            count_float = count_rows.astype(jnp.float32)
            library = lax.optimization_barrier(jnp.sum(count_float, axis=1, keepdims=True))
            expected = library * exponent / lax.optimization_barrier(jnp.sum(exponent, axis=1, keepdims=True))
            data_hot = (data_rows[:, None] == jnp.arange(ND)[None, :]).astype(jnp.float32)
            gene_weight = jnp.dot(data_hot, mask_float, precision=highest)
            terms = zinb_terms(count_float, count_rows == 0, expected, dropout_logit, dispersion)
            return (carry - jnp.sum(gene_weight * terms), None)
        recon, unused_out = lax.scan(jax.checkpoint(decode_block), jnp.zeros((), jnp.float32), (hidden.reshape(block_count, block_rows, H), counts.reshape(block_count, block_rows, G), dataset_ids.reshape(block_count, block_rows)))
        return (recon + kl_total) / TOKENS
    mean_loss, pullback = jax.vjp(forward, expression, params)
    input_cot, param_cot = pullback(jnp.ones_like(mean_loss))
    return (mean_loss, input_cot * TOKENS, param_cot[0], param_cot[1], param_cot[2], param_cot[3], param_cot[4], param_cot[5], param_cot[6], param_cot[7], param_cot[8], param_cot[9], param_cot[10], param_cot[11], param_cot[12], param_cot[13], param_cot[14], param_cot[15], param_cot[16])
```

```python
import jax
import jax.numpy as jnp
from jax import lax
from jax.experimental import pallas as pl
from jax.experimental.pallas import tpu as pltpu
from jax.sharding import PartitionSpec as P

highest = lax.Precision.HIGHEST
norm_eps = 0.001
log_eps = 1e-08
f32 = jnp.float32
bf16 = jnp.bfloat16
i32 = jnp.int32
LANE = 128
ALIGN = 16
CAP = 384
RB = 320
TOP = 24
WIRE = bf16
VMEM_MB = 1 << 20
by_last = (((1,), (1,)), ((), ()))
by_first = (((0,), (0,)), ((), ()))


def cuts(total, width):
    return [(i, min(width, total - i)) for i in range(0, total, width)]


def fit(v, width=LANE):
    return v if v.shape[1] == width else jnp.pad(v, ((0, 0), (0, width - v.shape[1])))


def vmem():
    return pl.BlockSpec(memory_space=pltpu.VMEM)


def smem():
    return pl.BlockSpec(memory_space=pltpu.SMEM)


def anywhere():
    return pl.BlockSpec(memory_space=pl.ANY)


def params(mib):
    return pltpu.CompilerParams(vmem_limit_bytes=mib * VMEM_MB)


def cost(micros):
    return pl.CostEstimate(
        flops=int(micros * 1.1e9), bytes_accessed=int(micros * 3.6e6), transcendentals=0
    )


def split3(v):
    high = lax.reduce_precision(v, 8, 7)
    rest = v - high
    middle = lax.reduce_precision(rest, 8, 7)
    return high.astype(bf16), middle.astype(bf16), (rest - middle).astype(bf16)


def swap(v, axis, bits):
    n = lax.axis_size(axis)
    return lax.ppermute(v, axis, [(i, i ^ bits) for i in range(n)])


def tree_sum(parts):
    while len(parts) > 1:
        parts = [parts[i] + parts[i + 1] for i in range(0, len(parts), 2)]
    return parts[0]


def total_direct(v, axis, unit=1):
    n = lax.axis_size(axis)
    return tree_sum([v] + [swap(v, axis, s) for s in range(unit, n, unit)])


def total_genes(v):
    return total_direct(v + swap(v, "genes", 1), "genes", 2)


def piece_of(v, i, size, axis):
    return lax.dynamic_slice_in_dim(v, i * size, size, axis)


def pieces_for(v, axis, dim, wire, unit=1):
    groups = lax.axis_size(axis) // unit
    spot = lax.axis_index(axis) // unit
    size = v.shape[dim] // groups
    low = v.astype(wire)
    own = piece_of(v, spot, size, dim).astype(f32)
    return [own] + [piece_of(low, spot ^ s, size, dim) for s in range(1, groups)]


def exchange(pieces, axis, unit=1):
    return pieces[:1] + [swap(piece, axis, unit * s) for s, piece in enumerate(pieces) if s]


def axis_scatter(v, axis, dim, wire, unit=1):
    return exchange(pieces_for(v, axis, dim, wire, unit), axis, unit)


def join(parts, wire):
    return tree_sum([part.astype(f32) for part in parts]).astype(wire)


def spread_out(own, axis, unit=1):
    groups = lax.axis_size(axis) // unit
    return [own] + [swap(own, axis, unit * s) for s in range(1, groups)]


def assemble(pieces, axis, dim, unit=1):
    spot = lax.axis_index(axis) // unit
    size = pieces[0].shape[dim]
    shape = list(pieces[0].shape)
    shape[dim] = size * len(pieces)
    whole = jnp.zeros(shape, pieces[0].dtype)
    for s, piece in enumerate(pieces):
        whole = lax.dynamic_update_slice_in_dim(whole, piece, (spot ^ s) * size, dim)
    return whole


def rows_pieces(v, wire):
    core = lax.axis_index("genes") % 2
    half = v.shape[0] // 2
    mine = piece_of(v, core, half, 0)
    other = piece_of(v, 1 - core, half, 0)
    summed = mine + swap(other.astype(wire), "genes", 1).astype(f32)
    return pieces_for(summed, "genes", 0, wire, 2)


def rows_whole(block):
    core = lax.axis_index("genes") % 2
    far = swap(block, "genes", 1)
    first = jnp.where(core == 0, block, far)
    second = jnp.where(core == 0, far, block)
    return jnp.concatenate([first, second], axis=0).astype(f32)


def after(value, *earlier):
    return lax.optimization_barrier((value, *earlier))


def pack_width(genes, pieces):
    return -(-genes // pieces // LANE) * LANE


def encode_kernel(
    blocks, pieces, counts_hbm, weight_ref, part_ref, lib_ref, pack_hbm,
    counts_ref, pack_ref, arrived, left,
):
    cells, genes = counts_ref.shape
    block = cells // blocks
    quarter = genes // pieces
    rows = [pl.ds(i * block, block) for i in range(blocks)]
    copies = [
        pltpu.make_async_copy(counts_hbm.at[rows[i], :], counts_ref.at[rows[i], :], arrived.at[i])
        for i in range(blocks)
    ]
    leaving = [
        pltpu.make_async_copy(pack_ref.at[rows[i], :], pack_hbm.at[rows[i], :], left.at[i])
        for i in range(blocks)
    ]
    for copy in copies:
        copy.start()
    for i in range(blocks):
        copies[i].wait()
        lib = jnp.zeros((block, LANE), f32)
        part = jnp.zeros((block, part_ref.shape[1]), f32)
        for start, width in cuts(quarter, LANE):
            packed = None
            for piece in range(pieces):
                at = pl.ds(piece * quarter + start, width)
                raw = counts_ref[rows[i], at]
                real = raw.astype(f32)
                lib = lib + fit(real)
                expr = jnp.log(1.0 + real).astype(bf16)
                part = part + jnp.dot(expr, weight_ref[at, :], preferred_element_type=f32)
                packed = raw if piece == 0 else packed | (raw << (8 * piece))
            pack_ref[rows[i], pl.ds(start, width)] = packed
        part_ref[rows[i], :] = part
        lib_ref[rows[i], :] = lib
        leaving[i].start()
    for copy in leaving:
        copy.wait()


def encode(counts, weight, pieces):
    cells, genes = counts.shape
    hidden = weight.shape[1]
    blocks = 8
    narrow = pack_width(genes, pieces)
    return pl.pallas_call(
        lambda *refs: encode_kernel(blocks, pieces, *refs),
        in_specs=[anywhere(), vmem()],
        out_specs=[vmem(), vmem(), anywhere()],
        out_shape=[
            jax.ShapeDtypeStruct((cells, hidden), f32),
            jax.ShapeDtypeStruct((cells, LANE), f32),
            jax.ShapeDtypeStruct((cells, narrow), i32),
        ],
        scratch_shapes=[
            pltpu.VMEM((cells, genes), i32),
            pltpu.VMEM((cells, narrow), i32),
            pltpu.SemaphoreType.DMA((blocks,)),
            pltpu.SemaphoreType.DMA((blocks,)),
        ],
        compiler_params=params(56),
        cost_estimate=cost(9),
        name="encode",
    )(counts, weight)


def express_kernel(pieces, pack_ref, expr_ref):
    genes = expr_ref.shape[1]
    quarter = genes // pieces
    for start, width in cuts(quarter, LANE):
        raw = pack_ref[:, pl.ds(start, width)]
        for piece in range(pieces):
            part = raw if pieces == 1 else (raw >> (8 * piece)) & 255
            expr_ref[:, pl.ds(piece * quarter + start, width)] = jnp.log(
                1.0 + part.astype(f32)
            ).astype(bf16)


def express(packed, genes, pieces):
    cells, narrow = packed.shape
    block = cells // 4
    return pl.pallas_call(
        lambda *refs: express_kernel(pieces, *refs),
        grid=(cells // block,),
        in_specs=[pl.BlockSpec((block, narrow), lambda i: (i, 0))],
        out_specs=pl.BlockSpec((block, genes), lambda i: (i, 0)),
        out_shape=jax.ShapeDtypeStruct((cells, genes), bf16),
        compiler_params=params(40),
        cost_estimate=cost(8),
        name="express",
    )(packed)


def order_kernel(mask_ref, data_ref, pos_ref, rank_ref, meta_ref):
    groups, genes = mask_ref.shape
    cells = data_ref.shape[1]
    row = lax.broadcasted_iota(i32, (LANE, LANE), 0)
    col = lax.broadcasted_iota(i32, (LANE, LANE), 1)
    upto = (row <= col).astype(bf16)
    group = lax.broadcasted_iota(i32, (groups, LANE), 0)

    def running(hot, so_far, width):
        inside = jnp.dot(hot.astype(bf16), upto[:width, :width], preferred_element_type=f32)
        return so_far + inside, so_far + jnp.sum(hot, axis=1, keepdims=True)

    so_far = jnp.zeros((groups, 1), f32)
    for start, width in cuts(genes, LANE):
        hot = mask_ref[:, pl.ds(start, width)].astype(f32)
        count, so_far = running(hot, so_far, width)
        place = jnp.where(hot > 0.5, count - 1.0, -1.0).astype(i32)
        if width < LANE:
            place = jnp.pad(place, ((0, 0), (0, LANE - width)), constant_values=-1)
        pos_ref[:, pl.ds(start, LANE)] = place
    gene_count = so_far

    so_far = jnp.zeros((groups, 1), f32)
    kept = []
    for start, width in cuts(cells, LANE):
        data = data_ref[:, pl.ds(start, width)]
        hot = (group[:, :width] == data).astype(f32)
        count, so_far = running(hot, so_far, width)
        kept.append((start, width, hot, count))
    cell_count = so_far
    padded = jnp.floor((cell_count + (ALIGN - 1)) * (1.0 / ALIGN))
    before = lax.broadcasted_iota(i32, (groups, groups), 1) < lax.broadcasted_iota(
        i32, (groups, groups), 0
    )
    spread = jnp.broadcast_to(padded, (groups, LANE))
    begin = ALIGN * jnp.dot(
        before.astype(f32), spread, precision=highest, preferred_element_type=f32
    )
    for start, width, hot, count in kept:
        place = hot * (begin[:, :width] + count - 1.0)
        rank_ref[:, pl.ds(start, width)] = jnp.sum(place, axis=0, keepdims=True).astype(i32)
    lane = lax.broadcasted_iota(i32, (groups, LANE), 1)
    meta = jnp.where(lane == 0, cell_count, jnp.where(lane == 1, begin, gene_count))
    meta_ref[...] = meta.astype(i32)


def order_cells(mask, data):
    groups, genes = mask.shape
    cells = data.shape[0]
    pos, rank, meta = pl.pallas_call(
        order_kernel,
        in_specs=[vmem(), vmem()],
        out_specs=[vmem(), vmem(), vmem()],
        out_shape=[
            jax.ShapeDtypeStruct((groups, -(-genes // LANE) * LANE), i32),
            jax.ShapeDtypeStruct((1, cells), i32),
            jax.ShapeDtypeStruct((groups, LANE), i32),
        ],
        cost_estimate=cost(2),
        name="order_cells",
    )(mask, data.reshape(1, cells))
    return pos, rank, meta[:, :3].reshape(-1)


def pass_count(meta_ref, groups):
    most = meta_ref[2]
    for d in range(1, groups):
        most = jnp.maximum(most, meta_ref[3 * d + 2])
    return jnp.maximum((most + CAP - 1) // CAP, 1)


def chunk_of(meta_ref, d, i, rows_all):
    count = meta_ref[3 * d]
    begin = meta_ref[3 * d + 1]
    low = begin + i * RB
    first = pl.multiple_of(jnp.minimum(low, rows_all - RB), ALIGN)
    return first, low, begin + count


def sort_kernel(rank_ref, pack_ref, sorted_hbm, sorted_ref, done):
    cells = pack_ref.shape[0]
    unroll = 16

    def move(i, carry):
        for u in range(unroll):
            c = i * unroll + u
            sorted_ref[pl.ds(rank_ref[c], 1), :] = pack_ref[pl.ds(c, 1), :]
        return carry

    lax.fori_loop(0, cells // unroll, move, 0)
    rows_all = sorted_ref.shape[0]
    copy = pltpu.make_async_copy(sorted_ref, sorted_hbm.at[pl.ds(0, rows_all), :], done)
    copy.start()
    copy.wait()


def sort_rows(rank, packed, rows_all):
    narrow = packed.shape[1]
    return pl.pallas_call(
        sort_kernel,
        in_specs=[smem(), vmem()],
        out_specs=anywhere(),
        out_shape=jax.ShapeDtypeStruct((rows_all + RB, narrow), i32),
        scratch_shapes=[pltpu.VMEM((rows_all, narrow), i32), pltpu.SemaphoreType.DMA],
        compiler_params=params(40),
        cost_estimate=cost(9),
        name="sort_rows",
    )(rank, packed)


def compact_kernel(
    pieces, genes, members, first_call, meta_ref, sorted_hbm, pos_ref, scale_ref, dropout_ref,
    extra_ref, *rest,
):
    if not first_call:
        rest = rest[3:]
    y_hbm, w_hbm, c_hbm, rows_ref, stack_ref, pick_ref, found_ref, table_ref, y_ref, w_ref, c_ref, came, gone = rest
    both = w_ref.shape[1]
    quarter = genes // pieces
    groups = pos_ref.shape[0]
    stack_ref[RB : RB + both // 2, :] = scale_ref[...]
    stack_ref[RB + both // 2 : RB + both, :] = dropout_ref[...] * jnp.asarray(0.5, bf16)
    stack_ref[RB + both :, :] = extra_ref[...]

    def rows_of(d, i):
        low = pl.multiple_of(meta_ref[3 * d + 1] + i * RB, ALIGN)
        return low, meta_ref[3 * d + 1] + meta_ref[3 * d]

    def bring(n, d, i):
        low, _ = rows_of(d, i)
        return pltpu.make_async_copy(sorted_hbm.at[pl.ds(low, RB), :], rows_ref.at[n], came.at[n])

    def widen(n):
        for start, width in cuts(quarter, LANE):
            raw = rows_ref[n, :, pl.ds(start, width)]
            for piece in range(pieces):
                part = raw if pieces == 1 else (raw >> (8 * piece)) & 255
                stack_ref[:RB, pl.ds(piece * quarter + start, width)] = part.astype(f32).astype(bf16)

    def look(n, d, i, k, sums):
        low, high = rows_of(d, i)

        def step(j, sums):
            gamma_in, digamma_in = sums
            src = pl.ds(pl.multiple_of(j * 16, 16), 16)
            row = lax.broadcasted_iota(i32, (16, CAP), 0) + (low + j * 16)
            col = lax.broadcasted_iota(i32, (16, CAP), 1) + k * CAP
            own = (row < high) & (col < meta_ref[3 * d + 2])
            value = jnp.where(own, found_ref[src, :], -1.0)
            y_ref[n, src, :] = value.astype(bf16)
            index = jnp.maximum(value, 0.0).astype(i32)
            for h in (0, 8):
                here = index[h : h + 8]
                inner = here & 7
                got = []
                for base in (0, TOP):
                    g0 = jnp.take_along_axis(table_ref[base : base + 8, :], inner, axis=0)
                    g1 = jnp.take_along_axis(table_ref[base + 8 : base + 16, :], inner, axis=0)
                    g2 = jnp.take_along_axis(table_ref[base + 16 : base + 24, :], inner, axis=0)
                    got.append(jnp.where(here < 8, g0, jnp.where(here < 16, g1, g2)))
                gamma_in = gamma_in + got[0]
                digamma_in = digamma_in + got[1]
            return gamma_in, digamma_in

        return lax.fori_loop(0, RB // 16, step, sums, unroll=2)

    def leave(n, d, i, k):
        low, _ = rows_of(d, i)
        return pltpu.make_async_copy(y_ref.at[n], y_hbm.at[k, pl.ds(low, RB), :], gone.at[3 * n])

    def one_pass(k, carry):
        for n, d in enumerate(members):
            bring(n, d, 0).start()
        pending = []
        for n, d in enumerate(members):
            column = lax.broadcasted_iota(i32, (CAP, 1), 0) + k * CAP
            for start, width in cuts(genes, 2 * LANE):
                place = pos_ref[d : d + 1, pl.ds(start, -(-width // LANE) * LANE)]
                pick = (column == place).astype(f32).astype(bf16)
                pick_ref[:, pl.ds(start, width)] = pick[:, :width]
            bring(n, d, 0).wait()
            widen(n)
            found_ref[...] = lax.dot_general(
                stack_ref[...], pick_ref[...], by_last, preferred_element_type=f32
            )
            w_ref[n] = found_ref[RB : RB + both, :].astype(bf16)
            side = [found_ref[RB + both + j : RB + both + j + 1, :] for j in range(9)]
            scale_bias = side[0] + side[1] + side[2]
            dropout_bias = side[3] + side[4] + side[5]
            log_theta = side[6] + side[7] + side[8]
            used = lax.broadcasted_iota(i32, (1, CAP), 1) + k * CAP < meta_ref[3 * d + 2]
            scale_bias = jnp.where(used, scale_bias, -1e30)
            theta = jnp.exp(log_theta)
            gamma_sum = jnp.zeros((1, CAP), f32)
            digamma_sum = jnp.zeros((1, CAP), f32)
            table_ref[...] = jnp.zeros_like(table_ref)
            for x in range(1, TOP):
                base = theta + float(x - 1)
                gamma_sum = gamma_sum + jnp.log(base * (1.0 / x))
                digamma_sum = digamma_sum + 1.0 / base
                table_ref[x : x + 1, :] = gamma_sum
                table_ref[TOP + x : TOP + x + 1, :] = digamma_sum
            zero = jnp.zeros((8, CAP), f32)
            sums = look(n, d, 0, k, (zero, zero))
            if pending:
                pending[-1].wait()
                pending.pop()
            last = leave(n, d, 0, k)
            last.start()

            def more(i, sums):
                leave(n, d, i - 1, k).wait()
                bring(n, d, i).start()
                bring(n, d, i).wait()
                widen(n)
                found_ref[:RB, :] = lax.dot_general(
                    stack_ref[:RB, :], pick_ref[...], by_last, preferred_element_type=f32
                )
                sums = look(n, d, i, k, sums)
                leave(n, d, i, k).start()
                return sums

            chunks = (meta_ref[3 * d] + RB - 1) // RB
            gammas, digammas = lax.fori_loop(1, chunks, more, sums)
            pending.append(last)
            c_ref[n] = jnp.zeros((8, CAP), f32)
            c_ref[n, 0:1, :] = scale_bias
            c_ref[n, 1:2, :] = dropout_bias
            c_ref[n, 2:3, :] = theta
            c_ref[n, 3:4, :] = jnp.sum(gammas, axis=0, keepdims=True)
            c_ref[n, 4:5, :] = jnp.sum(digammas, axis=0, keepdims=True)
            for copy in sides(n, d, k):
                copy.start()
        pending.pop().wait()
        for n, d in enumerate(members):
            for copy in sides(n, d, k):
                copy.wait()
        return carry

    def sides(n, d, k):
        return [
            pltpu.make_async_copy(w_ref.at[n], w_hbm.at[k, d], gone.at[3 * n + 1]),
            pltpu.make_async_copy(c_ref.at[n], c_hbm.at[k, d], gone.at[3 * n + 2]),
        ]

    lax.fori_loop(0, pass_count(meta_ref, groups), one_pass, 0)


def compact(members, meta, sorted_rows, pos, scale_weight, dropout_weight, extra, genes, pieces, before):
    groups = pos.shape[0]
    tall, narrow = sorted_rows.shape
    passes = -(-genes // CAP)
    both = 2 * scale_weight.shape[0]
    count = len(members)
    first_call = before is None
    return pl.pallas_call(
        lambda *refs: compact_kernel(pieces, genes, members, first_call, *refs),
        in_specs=[smem(), anywhere(), vmem(), vmem(), vmem(), vmem()]
        + ([] if first_call else [anywhere()] * 3),
        out_specs=[anywhere()] * 3,
        out_shape=[
            jax.ShapeDtypeStruct((passes, tall, CAP), bf16),
            jax.ShapeDtypeStruct((passes, groups, both, CAP), bf16),
            jax.ShapeDtypeStruct((passes, groups, 8, CAP), f32),
        ],
        input_output_aliases={} if first_call else {6: 0, 7: 1, 8: 2},
        scratch_shapes=[
            pltpu.VMEM((count, RB, narrow), i32),
            pltpu.VMEM((RB + both + 16, genes), bf16),
            pltpu.VMEM((CAP, genes), bf16),
            pltpu.VMEM((RB + both + 16, CAP), f32),
            pltpu.VMEM((2 * TOP, CAP), f32),
            pltpu.VMEM((count, RB, CAP), bf16),
            pltpu.VMEM((count, both, CAP), bf16),
            pltpu.VMEM((count, 8, CAP), f32),
            pltpu.SemaphoreType.DMA((count,)),
            pltpu.SemaphoreType.DMA((3 * count,)),
        ],
        compiler_params=params(48),
        cost_estimate=cost(4 * count),
        name="compact",
    )(meta, sorted_rows, pos, scale_weight, dropout_weight, extra, *(before or ()))


def softmax_kernel(
    hidden_ref, lib_ref, weight_ref, bias_ref, exp_ref, stat_ref, logit_ref, column_ref
):
    rows, genes = logit_ref.shape
    hidden = hidden_ref[...]
    top = jnp.full((rows, LANE), -jnp.inf, f32)
    for start, width in cuts(genes, 2 * LANE):
        at = pl.ds(start, width)
        logit = jnp.dot(hidden, weight_ref[:, at], preferred_element_type=f32) + bias_ref[:, at]
        logit_ref[:, at] = logit
        for first, wide in cuts(width, LANE):
            piece = logit[:, first : first + wide]
            if wide < LANE:
                piece = jnp.broadcast_to(jnp.max(piece, axis=1, keepdims=True), (rows, LANE))
            top = jnp.maximum(top, piece)
    top = jnp.max(top, axis=1, keepdims=True)
    total = jnp.zeros((rows, LANE), f32)
    for start, width in cuts(genes, LANE):
        at = pl.ds(start, width)
        value = jnp.exp(logit_ref[:, at] - top)
        exp_ref[:, at] = value.astype(bf16)
        total = total + fit(value)
    total = jnp.sum(total, axis=1, keepdims=True)
    lane = lax.broadcasted_iota(i32, (rows, LANE), 1)
    turn = pl.program_id(0)
    stat = jnp.where(lane == 0, top, jnp.where(lane == 1, total, lib_ref[...]))
    column_ref[pl.ds(pl.multiple_of(turn * rows, ALIGN), rows), :] = stat

    @pl.when(turn == pl.num_programs(0) - 1)
    def _():
        stat_ref[...] = jnp.zeros_like(stat_ref)
        for i in range(column_ref.shape[0] // LANE):
            tile = column_ref[i * LANE : (i + 1) * LANE, :].T
            for j in range(3):
                stat_ref[j, i : i + 1, :] = tile[j : j + 1, :]


def row_block(rows_all):
    return rows_all // 8 if rows_all % 128 == 0 else rows_all


def softmax_part(hidden, lib, weight, bias):
    rows_all, width = hidden.shape
    genes = weight.shape[1]
    block = row_block(rows_all)
    tall = -(-rows_all // LANE // 8) * 8
    return pl.pallas_call(
        softmax_kernel,
        grid=(rows_all // block,),
        in_specs=[
            pl.BlockSpec((block, width), lambda i: (i, 0)),
            pl.BlockSpec((block, LANE), lambda i: (i, 0)),
            pl.BlockSpec((width, genes), lambda i: (0, 0)),
            pl.BlockSpec((1, genes), lambda i: (0, 0)),
        ],
        out_specs=[
            pl.BlockSpec((block, genes), lambda i: (i, 0)),
            pl.BlockSpec((3, tall, LANE), lambda i: (0, 0, 0)),
        ],
        out_shape=[
            jax.ShapeDtypeStruct((rows_all, genes), bf16),
            jax.ShapeDtypeStruct((3, tall, LANE), f32),
        ],
        scratch_shapes=[pltpu.VMEM((block, genes), f32), pltpu.VMEM((rows_all, LANE), f32)],
        compiler_params=params(40),
        cost_estimate=cost(10),
        name="softmax_part",
    )(hidden, lib, weight, bias)


def exp_back_kernel(exp_ref, weight_ref, back_ref):
    back_ref[...] = lax.dot_general(
        exp_ref[...], weight_ref[...], by_last, preferred_element_type=f32
    )


def exp_times_weight(exps, weight):
    rows_all, genes = exps.shape
    width = weight.shape[0]
    block = row_block(rows_all)
    return pl.pallas_call(
        exp_back_kernel,
        grid=(rows_all // block,),
        in_specs=[
            pl.BlockSpec((block, genes), lambda i: (i, 0)),
            pl.BlockSpec((width, genes), lambda i: (0, 0)),
        ],
        out_specs=pl.BlockSpec((block, width), lambda i: (i, 0)),
        out_shape=jax.ShapeDtypeStruct((rows_all, width), f32),
        compiler_params=params(40),
        cost_estimate=cost(4),
        name="exp_times_weight",
    )(exps, weight)


def likelihood_kernel(
    meta_ref, hidden_ref, shift_ref, y_hbm, w_hbm, c_hbm,
    back_ref, inner_ref, loss_ref, g_hbm,
    row_sum_ref, y_ref, w_ref, c_ref, logit_ref, grad_ref, g_ref,
):
    rows_all, width = hidden_ref.shape
    groups = w_ref.shape[0]
    both = 2 * width
    step = 32
    back_ref[...] = jnp.zeros_like(back_ref)
    row_sum_ref[...] = jnp.zeros_like(row_sum_ref)
    inner_ref[...] = jnp.zeros_like(inner_ref)
    loss_ref[...] = jnp.zeros_like(loss_ref)

    def one_pass(k, carry):
        pltpu.sync_copy(c_hbm.at[k], c_ref)
        pltpu.sync_copy(w_hbm.at[k], w_ref)
        pltpu.sync_copy(y_hbm.at[k, pl.ds(0, rows_all), :], y_ref)

        def one_group(d, carry):
            scale_w = w_ref[d, :width, :]
            dropout_w = w_ref[d, width:, :]
            const = c_ref[d]
            at = pl.ds(pl.multiple_of(d * CAP, LANE), CAP)
            g_ref[:, at] = jnp.zeros((both + 16, CAP), f32)

            def one_chunk(i, sums):
                first, low, high = chunk_of(meta_ref, d, i, rows_all)
                rows = pl.ds(first, RB)
                hidden = hidden_ref[rows, :]
                logit_ref[:, :CAP] = jnp.dot(hidden, scale_w, preferred_element_type=f32)
                logit_ref[:, CAP:] = jnp.dot(hidden, dropout_w, preferred_element_type=f32)

                def element(j, sums):
                    src = pl.ds(pl.multiple_of(j * step, step), step)
                    row = pl.ds(pl.multiple_of(first + j * step, 16), step)
                    shift = shift_ref[row, :]
                    loss, num, den = sums[:3]
                    place = lax.broadcasted_iota(i32, (step, LANE), 0) + (first + j * step)
                    inside = (place >= low) & (place < high)
                    columns = []
                    for n, (start, wide) in enumerate(cuts(CAP, LANE)):
                        here = pl.ds(start, wide)
                        there = pl.ds(CAP + start, wide)
                        scale_bias = const[0:1, start : start + wide]
                        dropout_bias = const[1:2, start : start + wide]
                        theta = const[2:3, start : start + wide]
                        theta_e = theta + log_eps
                        log_e = jnp.log(theta_e)
                        ratio = theta / theta_e
                        y = jnp.where(inside[:, :wide], y_ref[row, here].astype(f32), -1.0)
                        mean = jnp.exp(logit_ref[src, here] + scale_bias + shift)
                        half = logit_ref[src, there] + dropout_bias
                        t = mean + theta_e
                        log_t = jnp.log(t)
                        inv_t = 1.0 / t
                        down = log_e - log_t
                        weighted_in = y >= 0.0
                        count = jnp.maximum(y, 0.0)
                        half = jnp.where(weighted_in, half, 0.0)
                        joint = jnp.where(y == 0.0, (0.5 * theta) * down - half, 32.0 * count)
                        tan_drop = jnp.tanh(half)
                        tan_joint = jnp.tanh(joint)
                        one = jnp.where(weighted_in, 1.0, 0.0)
                        chance = 0.5 * (one + tan_joint)
                        pull = (theta * chance + count) * inv_t
                        me = mean + log_eps
                        drift = pull * mean - count * (mean / me)
                        twice = tan_joint + tan_drop
                        grad_ref[src, here] = drift.astype(bf16)
                        grad_ref[src, there] = twice.astype(bf16)
                        slope = chance * (down + ratio) - pull
                        fold = lambda v: jnp.sum(v.reshape(step // 8, 8, wide), axis=0)
                        old = sums[3 + n]
                        columns.append(
                            (old[0] + fold(slope), old[1] + fold(drift), old[2] + fold(twice))
                        )
                        loss = loss + (
                            one * theta * down
                            + 2.0 * (jnp.maximum(-joint, 0.0) - jnp.maximum(half, 0.0))
                            + count * (jnp.log(me) - log_t)
                        )
                        num = num * (1.0 + jnp.abs(tan_drop))
                        den = den * (1.0 + jnp.abs(tan_joint))
                    return (loss, num, den, *columns)

                def clear(j, carry):
                    src = pl.ds(pl.multiple_of(j * step, step), step)
                    grad_ref[src, :] = jnp.zeros((step, 2 * CAP), bf16)
                    return carry

                steps = jnp.minimum((high - first + step - 1) // step, RB // step)
                one_rows = jnp.ones((step, LANE), f32)
                got = lax.fori_loop(0, steps, element, (sums[0], one_rows, one_rows, *sums[1:]))
                lax.fori_loop(steps, RB // step, clear, 0)
                loss, num, den = got[:3]
                loss = loss + (jnp.log(num) - jnp.log(den))
                grads = grad_ref[...]
                g_ref[:width, at] += lax.dot_general(
                    hidden, grads[:, :CAP], by_first, preferred_element_type=f32
                )
                g_ref[width:both, at] += lax.dot_general(
                    hidden, grads[:, CAP:], by_first, preferred_element_type=f32
                )
                ones = jnp.ones((width, CAP), bf16)
                both_sums = lax.dot_general(
                    grads[:, :CAP],
                    jnp.concatenate([scale_w, ones], axis=0),
                    by_last,
                    preferred_element_type=f32,
                )
                row_sum_ref[rows, :] += both_sums[:, width:]
                back_ref[rows, :] += both_sums[:, :width] + lax.dot_general(
                    grads[:, CAP:], dropout_w, by_last, preferred_element_type=f32
                )
                return (loss, *got[3:])

            zero = jnp.zeros((8, LANE), f32)
            start_sums = (jnp.zeros((step, LANE), f32),) + tuple(
                (zero, zero, zero) for _ in cuts(CAP, LANE)
            )
            chunks = (meta_ref[3 * d] + RB - 1) // RB
            got = lax.fori_loop(0, chunks, one_chunk, start_sums)
            count_sum = const[3:4, :LANE]
            for start, wide in cuts(CAP, LANE)[1:]:
                count_sum = count_sum + const[3:4, start : start + wide]
            loss_ref[...] += jnp.sum(got[0].reshape(step // 8, 8, LANE), axis=0) + jnp.where(
                lax.broadcasted_iota(i32, (8, LANE), 0) == 0, count_sum, 0.0
            )
            for n, (start, wide) in enumerate(cuts(CAP, LANE)):
                here = pl.ds(pl.multiple_of(d * CAP + start, LANE), wide)
                slope, drift, twice = (jnp.sum(v, axis=0, keepdims=True) for v in got[1 + n])
                g_ref[both : both + 1, here] = drift
                g_ref[both + 1 : both + 2, here] = twice
                g_ref[both + 2 : both + 3, here] = slope + const[4:5, start : start + wide]
            return carry

        lax.fori_loop(0, groups, one_group, 0)
        pltpu.sync_copy(g_ref, g_hbm.at[k])
        return carry

    lax.fori_loop(0, pass_count(meta_ref, groups), one_pass, 0)
    for i in range(rows_all // LANE):
        tile = row_sum_ref[i * LANE : (i + 1) * LANE, :].T
        inner_ref[i : i + 1, :] = tile[0:1, :]


def likelihood(meta, hidden, shift, y, w, c):
    rows_all, width = hidden.shape
    passes, groups, both, _ = w.shape
    return pl.pallas_call(
        likelihood_kernel,
        in_specs=[smem(), vmem(), vmem(), anywhere(), anywhere(), anywhere()],
        out_specs=[vmem(), vmem(), vmem(), anywhere()],
        out_shape=[
            jax.ShapeDtypeStruct((rows_all, width), f32),
            jax.ShapeDtypeStruct((-(-rows_all // LANE // 8) * 8, LANE), f32),
            jax.ShapeDtypeStruct((8, LANE), f32),
            jax.ShapeDtypeStruct((passes, both + 16, groups * CAP), f32),
        ],
        scratch_shapes=[
            pltpu.VMEM((rows_all, width), f32),
            pltpu.VMEM((rows_all, CAP), bf16),
            pltpu.VMEM((groups, both, CAP), bf16),
            pltpu.VMEM((groups, 8, CAP), f32),
            pltpu.VMEM((RB, 2 * CAP), f32),
            pltpu.VMEM((RB, 2 * CAP), bf16),
            pltpu.VMEM((both + 16, groups * CAP), f32),
        ],
        compiler_params=params(48),
        cost_estimate=cost(20),
        name="likelihood",
    )(meta, hidden, shift, y, w, c)


def expand_kernel(meta_ref, g_ref, pos_ref, row_ref, exp_ref, g_hbm, out_ref, pick_ref, more_ref):
    groups = pos_ref.shape[0]
    both16 = g_ref.shape[1]
    genes = out_ref.shape[1]
    width = (both16 - 16) // 2

    def spread(k, g):
        for d in range(groups):
            column = lax.broadcasted_iota(i32, (CAP, 1), 0) + k * CAP
            pick_ref[d * CAP : (d + 1) * CAP, :] = (
                (column == pos_ref[d : d + 1, :]).astype(f32).astype(bf16)[:, :genes]
            )
        high = g.astype(bf16)
        low = (g - high.astype(f32)).astype(bf16)
        pick = pick_ref[...]
        return jnp.dot(high, pick, preferred_element_type=f32) + jnp.dot(
            low, pick, preferred_element_type=f32
        )

    out_ref[...] = spread(0, g_ref[0])
    drop = jnp.dot(row_ref[...], exp_ref[...], preferred_element_type=f32)
    out_ref[:width, :] -= drop[:width]
    out_ref[2 * width : 2 * width + 1, :] -= drop[width : width + 1]

    def more(k, carry):
        pltpu.sync_copy(g_hbm.at[k], more_ref)
        out_ref[...] += spread(k, more_ref[...])
        return carry

    lax.fori_loop(1, pass_count(meta_ref, groups), more, 0)


def expand(meta, g, pos, rows, exps):
    groups = pos.shape[0]
    both16 = g.shape[1]
    rows_all, genes = exps.shape
    block = 512 if genes % 512 == 0 else genes
    return pl.pallas_call(
        expand_kernel,
        grid=(genes // block,),
        in_specs=[
            smem(),
            pl.BlockSpec((1, both16, groups * CAP), lambda i: (0, 0, 0)),
            pl.BlockSpec((groups, -(-block // LANE) * LANE), lambda i: (0, i)),
            pl.BlockSpec(rows.shape, lambda i: (0, 0)),
            pl.BlockSpec((rows_all, block), lambda i: (0, i)),
            anywhere(),
        ],
        out_specs=pl.BlockSpec((both16, block), lambda i: (0, i)),
        out_shape=jax.ShapeDtypeStruct((both16, genes), f32),
        scratch_shapes=[
            pltpu.VMEM((groups * CAP, block), bf16),
            pltpu.VMEM((both16, groups * CAP), f32),
        ],
        compiler_params=params(56),
        cost_estimate=cost(16),
        name="expand",
    )(meta, g, pos, rows, exps, g)


def norm_parts(x, stats, affine, total):
    center = stats[0:1] * (1.0 / total)
    variance = stats[1:2] * (1.0 / total) - center * center
    inverse = lax.rsqrt(variance + norm_eps)
    normed = (x - center) * inverse
    gated = normed * affine[0:1] + affine[1:2]
    sigma = 0.5 + 0.5 * jnp.tanh(0.5 * gated)
    return normed, inverse, gated, sigma


def two_rows(first, second):
    row = lax.broadcasted_iota(i32, (8, first.shape[1]), 0)
    return jnp.where(row == 0, first, jnp.where(row == 1, second, 0.0))


def sums_of(x):
    return two_rows(
        jnp.sum(x, axis=0, keepdims=True), jnp.sum(x * x, axis=0, keepdims=True)
    )


def exact(a, b, dims):
    return lax.dot_general(a, b, dims, precision=highest, preferred_element_type=f32)


plain = (((1,), (0,)), ((), ()))


def batch_rows(batch_ref, count):
    names = lax.broadcasted_iota(i32, (count, 1), 0)
    return (names == batch_ref[...]).astype(f32)


def latent_kernel(
    total, x_ref, stat_ref, affine_ref, heads_ref, bias_ref, noise_ref, decode_ref, add_ref,
    pre_ref, sums_ref, latent_ref, kl_ref,
):
    _, _, gated, sigma = norm_parts(x_ref[...], stat_ref, affine_ref, total)
    act = gated * sigma
    heads = exact(heads_ref[...], act, by_last) + bias_ref[:, 0:1]
    mean, logvar = heads[:16], heads[16:]
    scale = jnp.exp(0.5 * logvar)
    latent = mean + scale * noise_ref[...]
    latent_ref[0:16, :] = mean
    latent_ref[16:32, :] = logvar
    latent_ref[32:48, :] = latent
    latent_ref[48:64, :] = scale
    terms = jnp.exp(logvar) + mean * mean - 1.0 - logvar
    folded = jnp.zeros((16, LANE), f32)
    for start, width in cuts(terms.shape[1], LANE):
        folded = folded + terms[:, start : start + width]
    kl_ref[...] = 0.5 * (folded[:8] + folded[8:])
    pre = exact(latent, decode_ref[...], by_first) + add_ref[...]
    pre_ref[...] = pre
    sums_ref[...] = sums_of(pre)


def latent_stage(total, x, stat, affine, heads, bias, noise, decode, add):
    cells, width = x.shape
    return pl.pallas_call(
        lambda *refs: latent_kernel(total, *refs),
        in_specs=[vmem()] * 8,
        out_specs=[vmem()] * 4,
        out_shape=[
            jax.ShapeDtypeStruct((cells, width), f32),
            jax.ShapeDtypeStruct((8, width), f32),
            jax.ShapeDtypeStruct((64, cells), f32),
            jax.ShapeDtypeStruct((8, LANE), f32),
        ],
        compiler_params=params(40),
        cost_estimate=cost(2),
        name="latent_stage",
    )(x, stat, affine, heads, bias, noise, decode, add)


def hidden_kernel(total, pre_ref, stat_ref, affine_ref, rank_ref, lib_ref, hidden_ref, sum_ref, carry_ref):
    width = pre_ref.shape[1]
    rows_all = hidden_ref.shape[0]
    _, _, gated, sigma = norm_parts(pre_ref[...], stat_ref, affine_ref, total)
    carry_ref[:, :width] = (gated * sigma).astype(bf16)
    lib = jnp.sum(lib_ref[...], axis=1, keepdims=True)
    lane = lax.broadcasted_iota(i32, (lib.shape[0], LANE), 1)
    high = lib.astype(bf16).astype(f32)
    middle = (lib - high).astype(bf16).astype(f32)
    low = lib - high - middle
    carry_ref[:, width:] = jnp.where(
        lane == 0, high, jnp.where(lane == 1, middle, jnp.where(lane == 2, low, 0.0))
    ).astype(bf16)
    block = row_block(rows_all)

    def body(i, carry):
        first = pl.multiple_of(i * block, ALIGN)
        place = lax.broadcasted_iota(i32, (block, 1), 0) + first
        pick = (place == rank_ref[...]).astype(f32).astype(bf16)
        got = jnp.dot(pick, carry_ref[...], preferred_element_type=f32)
        hidden_ref[pl.ds(first, block), :] = got[:, :width].astype(bf16)
        sum_ref[pl.ds(first, block), :] = jnp.broadcast_to(
            jnp.sum(got[:, width:], axis=1, keepdims=True), (block, LANE)
        )
        return carry

    lax.fori_loop(0, rows_all // block, body, 0)


def hidden_stage(total, pre, stat, affine, rank, lib, rows_all):
    cells, width = pre.shape
    return pl.pallas_call(
        lambda *refs: hidden_kernel(total, *refs),
        in_specs=[vmem()] * 5,
        out_specs=[vmem()] * 2,
        out_shape=[
            jax.ShapeDtypeStruct((rows_all, width), bf16),
            jax.ShapeDtypeStruct((rows_all, LANE), f32),
        ],
        scratch_shapes=[pltpu.VMEM((cells, width + LANE), bf16)],
        compiler_params=params(40),
        cost_estimate=cost(5),
        name="hidden_stage",
    )(pre, stat, affine, rank, lib)


def decoder_back_kernel(
    total, latents, back_ref, exp_back_ref, scale_ref, place_ref, pre_ref, stat_ref, affine_ref,
    decode_ref, latent_ref, batch_ref,
    pull_ref, weight_ref, sorted_ref,
):
    rows_all, width = back_ref.shape
    cells = pre_ref.shape[0]
    names = weight_ref.shape[0] - 16
    for i in range(rows_all // LANE):
        tile = pl.ds(i * LANE, LANE)
        scale = jnp.broadcast_to(scale_ref[i : i + 1, :], (LANE, LANE)).T
        part = back_ref[tile, :] - exp_back_ref[tile, :] * scale
        high = part.astype(bf16)
        sorted_ref[tile, :width] = high
        sorted_ref[tile, width:] = (part - high.astype(f32)).astype(bf16)
    block = 256
    first = jnp.zeros((1, width), f32)
    second = jnp.zeros((1, width), f32)
    weight = jnp.zeros((16 + names, width), f32)
    lane = lax.broadcasted_iota(i32, (1, rows_all), 1)
    for start, tall in cuts(cells, block):
        rows = pl.ds(start, tall)
        place = jnp.concatenate([place_ref[rows, :]] * (rows_all // LANE), axis=1)
        pick = (place == lane).astype(f32).astype(bf16)
        got = jnp.dot(pick, sorted_ref[...], preferred_element_type=f32)
        grad = got[:, :width] + got[:, width:]
        normed, inverse, gated, sigma = norm_parts(pre_ref[rows, :], stat_ref, affine_ref, total)
        inner = grad * sigma * (1.0 + gated * (1.0 - sigma))
        first = first + jnp.sum(inner, axis=0, keepdims=True)
        second = second + jnp.sum(inner * normed, axis=0, keepdims=True)
        pull_ref[:, rows] = exact(decode_ref[...] * (inverse * affine_ref[0:1, :]), inner, by_last)
        hot = (lax.broadcasted_iota(i32, (names, 1), 0) == batch_ref[:, rows]).astype(f32)
        side = jnp.concatenate([latent_ref[32:48, rows], hot], axis=0)
        weight = weight + exact(side, inner, plain)
    weight_ref[...] = weight
    pull_ref[latents : latents + 1, :width] = first
    pull_ref[latents + 1 : latents + 2, :width] = second


def decoder_back(total, latents, back, exp_back, scale, place, pre, stat, affine, decode, latent, batch, names):
    rows_all, width = back.shape
    cells = pre.shape[0]
    return pl.pallas_call(
        lambda *refs: decoder_back_kernel(total, latents, *refs),
        in_specs=[vmem()] * 10,
        out_specs=[vmem()] * 2,
        out_shape=[
            jax.ShapeDtypeStruct((16, cells), f32),
            jax.ShapeDtypeStruct((16 + names, width), f32),
        ],
        scratch_shapes=[pltpu.VMEM((rows_all, 2 * width), bf16)],
        compiler_params=params(48),
        cost_estimate=cost(8),
        name="decoder_back",
    )(back, exp_back, scale, place, pre, stat, affine, decode, latent, batch)


def encoder_back_kernel(
    total, latents, share, pull_ref, inner_ref, pre_ref, stat_ref, affine_ref,
    x_ref, x_stat_ref, x_affine_ref, latent_ref, noise_ref, heads_ref, decode_ref,
    weight_ref, batch_ref, loss_ref, kl_ref,
    inner_out, sums_ref, pack_ref,
):
    width = pre_ref.shape[1]
    names = weight_ref.shape[0] - 16
    normed, inverse, _, _ = norm_parts(pre_ref[...], stat_ref, affine_ref, total)
    factor = inverse * affine_ref[0:1, :]
    shift_mean = inner_ref[0:1, :] * (1.0 / total)
    gain_mean = inner_ref[1:2, :] * (1.0 / total)
    decode = decode_ref[...] * factor
    fixed = jnp.sum(decode * shift_mean, axis=1, keepdims=True)
    moving = exact(decode * gain_mean, normed, by_last)
    row = lax.broadcasted_iota(i32, (16, 1), 0)
    pull = jnp.where(row < latents, pull_ref[...], 0.0) - fixed - moving
    mean, logvar = latent_ref[0:16, :], latent_ref[16:32, :]
    latent, scale = latent_ref[32:48, :], latent_ref[48:64, :]
    grad_mean = pull + mean
    grad_logvar = 0.5 * pull * noise_ref[...] * scale + 0.5 * (jnp.exp(logvar) - 1.0)
    grads = jnp.concatenate([grad_mean, grad_logvar], axis=0)
    grad_act = exact(grads, heads_ref[...], by_first)
    x_normed, _, gated, sigma = norm_parts(x_ref[...], x_stat_ref, x_affine_ref, total)
    inner = grad_act * sigma * (1.0 + gated * (1.0 - sigma))
    inner_out[...] = inner
    sums_ref[...] = two_rows(
        jnp.sum(inner, axis=0, keepdims=True), jnp.sum(inner * x_normed, axis=0, keepdims=True)
    )
    side = jnp.concatenate([latent, batch_rows(batch_ref, names)], axis=0)
    side_sum = jnp.sum(side, axis=1, keepdims=True)
    fix = side_sum * shift_mean + exact(side, normed, plain) * gain_mean
    pack_ref[: 16 + names, :] = factor * (weight_ref[...] - share * fix)
    at = 16 + names
    pack_ref[at : at + 32, :] = share * exact(grads, gated * sigma, plain)
    pack_ref[at + 32 : at + 64, :] = jnp.broadcast_to(
        share * jnp.sum(grads, axis=1, keepdims=True), (32, LANE)
    )
    pack_ref[at + 64 : at + 72, :] = share * kl_ref[...] - loss_ref[...]


def encoder_back(
    total, latents, share, pull, inner, pre, stat, affine, x, x_stat, x_affine, latent, noise,
    heads, decode, weight, batch, loss, kl,
):
    cells, width = pre.shape
    return pl.pallas_call(
        lambda *refs: encoder_back_kernel(total, latents, share, *refs),
        in_specs=[vmem()] * 16,
        out_specs=[vmem()] * 3,
        out_shape=[
            jax.ShapeDtypeStruct((cells, width), f32),
            jax.ShapeDtypeStruct((8, width), f32),
            jax.ShapeDtypeStruct((weight.shape[0] + 72, width), f32),
        ],
        compiler_params=params(48),
        cost_estimate=cost(3),
        name="encoder_back",
    )(
        pull, inner, pre, stat, affine, x, x_stat, x_affine, latent, noise,
        heads, decode, weight, batch, loss, kl,
    )


def encoder_grad_kernel(
    total, inner_ref, x_ref, stat_ref, affine_ref, sums_ref, batch_ref, expr_ref,
    out_ref, grad_ref, batch_out_ref, turned_ref,
):
    @pl.when(pl.program_id(0) == 0)
    def _():
        normed, inverse, _, _ = norm_parts(x_ref[...], stat_ref, affine_ref, total)
        factor = inverse * affine_ref[0:1, :]
        grad = factor * (
            inner_ref[...]
            - sums_ref[0:1, :] * (1.0 / total)
            - normed * (sums_ref[1:2, :] * (1.0 / total))
        )
        low = grad.astype(bf16)
        grad_ref[...] = low
        turned_ref[...] = low.astype(f32).T.astype(bf16)
        hot = batch_rows(batch_ref, batch_out_ref.shape[0])
        batch_out_ref[...] = jnp.dot(hot.astype(bf16), low, preferred_element_type=f32)

    got = jnp.dot(turned_ref[...], expr_ref[...], preferred_element_type=f32)
    out_ref[...] = got.T


def encoder_grad(total, inner, x, stat, affine, sums, batch, names, expr):
    cells, width = x.shape
    genes = expr.shape[1]
    block = 512 if genes % 512 == 0 else genes
    full = lambda v: pl.BlockSpec(v.shape, lambda i: (0, 0))
    return pl.pallas_call(
        lambda *refs: encoder_grad_kernel(total, *refs),
        grid=(genes // block,),
        in_specs=[full(v) for v in (inner, x, stat, affine, sums, batch)]
        + [pl.BlockSpec((cells, block), lambda i: (0, i))],
        out_specs=[
            pl.BlockSpec((block, width), lambda i: (i, 0)),
            pl.BlockSpec((cells, width), lambda i: (0, 0)),
            pl.BlockSpec((names, width), lambda i: (0, 0)),
        ],
        out_shape=[
            jax.ShapeDtypeStruct((genes, width), f32),
            jax.ShapeDtypeStruct((cells, width), bf16),
            jax.ShapeDtypeStruct((names, width), f32),
        ],
        scratch_shapes=[pltpu.VMEM((width, cells), bf16)],
        compiler_params=params(40),
        cost_estimate=cost(4),
        name="encoder_grad",
    )(inner, x, stat, affine, sums, batch, expr)


def input_grad_kernel(grad_ref, weight_ref, out_ref):
    out_ref[...] = lax.dot_general(
        grad_ref[...], weight_ref[...], by_last, preferred_element_type=f32
    )


def input_grad(grad, weight):
    cells, width = grad.shape
    genes = weight.shape[0]
    block = 256
    return pl.pallas_call(
        input_grad_kernel,
        grid=(cells // block,),
        in_specs=[
            pl.BlockSpec((block, width), lambda i: (i, 0)),
            pl.BlockSpec((genes, width), lambda i: (0, 0)),
        ],
        out_specs=pl.BlockSpec((block, genes), lambda i: (i, 0)),
        out_shape=jax.ShapeDtypeStruct((cells, genes), f32),
        compiler_params=params(40),
        cost_estimate=cost(9),
        name="input_grad",
    )(grad, weight)


def body(
    counts,
    batch_ids,
    dataset_ids,
    variable_mask,
    latent_noise,
    encoder_weight,
    encoder_batch,
    encoder_gain,
    encoder_shift,
    mean_weight,
    mean_bias,
    logvar_weight,
    logvar_bias,
    decoder_latent,
    decoder_batch,
    decoder_gain,
    decoder_shift,
    scale_weight,
    scale_bias,
    dropout_weight,
    dropout_bias,
    log_theta,
):
    cells, genes = counts.shape
    groups = variable_mask.shape[0]
    width = encoder_weight.shape[1]
    latents = mean_weight.shape[1]
    names = encoder_batch.shape[0]
    total_cells = cells * lax.axis_size("cells")
    gene_parts = lax.axis_size("genes")
    inverse_cells = 1.0 / total_cells
    pieces = 4 if genes % (4 * LANE) == 0 else 1
    rows_all = -(-(cells + groups * ALIGN) // LANE) * LANE

    partial_pre, lib_lanes, packed = encode(counts, encoder_weight, pieces)
    pre_pieces = rows_pieces(partial_pre, WIRE)

    pos, rank, meta = order_cells(variable_mask, dataset_ids)
    extra = [*split3(scale_bias), *split3(0.5 * dropout_bias), *split3(log_theta)]
    extra = jnp.concatenate([jnp.stack(extra), jnp.zeros((16 - len(extra), genes), bf16)])
    batch_row = batch_ids.reshape(1, cells)
    batch_hot = (batch_ids[:, None] == jnp.arange(names)[None, :]).astype(f32)
    encoder_add = jnp.dot(batch_hot, encoder_batch, precision=highest)
    decoder_add = jnp.dot(batch_hot, decoder_batch, precision=highest)
    pad_rows = lambda v, n=16: jnp.pad(v, ((0, n - v.shape[0]), (0, 0)))
    noise = pad_rows(latent_noise.T)
    heads = jnp.concatenate([pad_rows(mean_weight.T), pad_rows(logvar_weight.T)])
    head_bias = jnp.concatenate([pad_rows(mean_bias[:, None]), pad_rows(logvar_bias[:, None])])
    head_bias = jnp.broadcast_to(head_bias, (32, LANE))
    decode = pad_rows(decoder_latent)
    encoder_affine = pad_rows(jnp.stack([encoder_gain, encoder_shift]), 8)
    decoder_affine = pad_rows(jnp.stack([decoder_gain, decoder_shift]), 8)
    place = jnp.broadcast_to(rank.reshape(cells, 1), (cells, LANE))

    def own_genes(members, rows, before):
        return compact(
            members, meta, rows, pos, scale_weight, dropout_weight, extra, genes, pieces, before
        )

    batches = [[d for d in range(groups) if d * 8 // groups in some] for some in ((0, 1, 2), (3, 4), (5, 6), (7,))]

    pre_pieces, packed = after(pre_pieces, packed)
    pre_parts = exchange(pre_pieces, "genes", 2)
    sorted_rows = sort_rows(rank.reshape(cells), packed, rows_all)
    pre_parts, sorted_rows = after(pre_parts, sorted_rows)
    pre_own, sorted_rows = after(join(pre_parts, WIRE), sorted_rows)
    pre_blocks = spread_out(pre_own, "genes", 2)
    ycw = own_genes(batches[0], sorted_rows, None)
    pre_blocks, ycw = after(pre_blocks, ycw)
    x = rows_whole(assemble(pre_blocks, "genes", 0, 2)) + encoder_add
    x_sums = pad_rows(jnp.stack([jnp.sum(x, axis=0), jnp.sum(x * x, axis=0)]), 8)
    x_sums, sorted_rows = after(x_sums, sorted_rows)
    x_stat = total_direct(x_sums, "cells")
    ycw = own_genes(batches[1], sorted_rows, ycw)
    x_stat, ycw = after(x_stat, ycw)
    pre, sums, latent, kl_lanes = latent_stage(
        total_cells, x, x_stat, encoder_affine, heads, head_bias, noise, decode, decoder_add
    )
    sums, sorted_rows = after(sums, sorted_rows)
    stat = total_direct(sums, "cells")
    ycw = own_genes(batches[2], sorted_rows, ycw)
    stat, ycw = after(stat, ycw)
    hidden, lib_sorted = hidden_stage(
        total_cells, pre, stat, decoder_affine, rank, lib_lanes, rows_all
    )

    exps, own = softmax_part(hidden, lib_sorted, scale_weight, scale_bias.reshape(1, genes))
    own, exps, sorted_rows = after(own, exps, sorted_rows)
    pair = jnp.stack([own, swap(own, "genes", 1)])
    gathered = [pair] + [swap(pair, "genes", 2 * s) for s in range(1, gene_parts // 2)]
    exp_back = exp_times_weight(exps, scale_weight)
    ycw = own_genes(batches[3], sorted_rows, ycw)
    gathered, exp_back, ycw = after(gathered, exp_back, ycw)
    tops = [g[i, 0] for g in gathered for i in range(2)]
    top = tops[0]
    for t in tops[1:]:
        top = jnp.maximum(top, t)
    exp_total = tree_sum(
        [g[0, 1] * jnp.exp(g[0, 0] - top) + g[1, 1] * jnp.exp(g[1, 0] - top) for g in gathered]
    )
    exp_total = jnp.maximum(exp_total, 1e-30)
    library = tree_sum([g[0, 2] + g[1, 2] for g in gathered])
    own_scale = jnp.exp(own[0] - top) / exp_total
    shift = jnp.where(
        library > 0.0,
        jnp.log(jnp.maximum(library, 1.0)) - jnp.log(exp_total) - top,
        -1e30,
    )
    shift = jnp.broadcast_to(shift.reshape(-1)[:rows_all, None], (rows_all, LANE))
    back, inner_rows, loss_lanes, g = likelihood(meta, hidden, shift, *ycw)
    inner_rows, packed = after(inner_rows, packed)
    inner_total = total_genes(inner_rows)
    expr = express(packed, genes, pieces)
    inner_total, expr = after(inner_total, expr)
    row_scale = inner_total * own_scale
    pull, decoder_weight = decoder_back(
        total_cells, latents, back, exp_back, row_scale, place, pre, stat, decoder_affine,
        decode, latent, batch_row, names,
    )
    row_flat = row_scale.reshape(1, -1)[:, :rows_all]
    row_t = jnp.concatenate(
        [
            (hidden.T.astype(f32) * row_flat).astype(bf16),
            row_flat.astype(bf16),
            jnp.zeros((15, rows_all), bf16),
        ]
    )
    pull, row_t = after(pull, row_t)
    pull = total_genes(pull)
    spread = expand(meta, g, pos, row_t, exps)
    pull, spread = after(pull, spread)
    spread_pieces = pieces_for(spread, "cells", 1, bf16)
    spread_pieces, pull = after(spread_pieces, pull)
    spread_parts = exchange(spread_pieces, "cells")
    decoder_sums = total_direct(pad_rows(pull[latents : latents + 2, :width], 8), "cells")
    inner, sums, pack = encoder_back(
        total_cells, latents, 1.0 / gene_parts, pull, decoder_sums, pre, stat, decoder_affine,
        x, x_stat, encoder_affine, latent, noise, heads, decode, decoder_weight, batch_row,
        loss_lanes, kl_lanes,
    )
    spread_parts, sums = after(spread_parts, sums)
    spread_own, sums = after(join(spread_parts, bf16), sums)
    sums = total_direct(sums, "cells")
    spread_blocks = spread_out(spread_own, "cells")
    encoder_weight_grad, grad_pre_low, encoder_batch_grad = encoder_grad(
        total_cells, inner, x, x_stat, encoder_affine, sums, batch_row, names, expr
    )
    encoder_pieces = pieces_for(encoder_weight_grad, "cells", 0, bf16)
    encoder_pieces, spread_blocks, grad_pre_low = after(
        encoder_pieces, spread_blocks, grad_pre_low
    )
    encoder_parts = exchange(encoder_pieces, "cells")
    pack = jnp.concatenate([pack, encoder_batch_grad * (1.0 / gene_parts)])
    pack = total_genes(pack)
    spread = assemble(spread_blocks, "cells", 1).astype(f32)
    input_gradient = input_grad(grad_pre_low, encoder_weight)
    encoder_parts, pack, input_gradient = after(encoder_parts, pack, input_gradient)
    pack = total_direct(pack, "cells") * inverse_cells
    encoder_total = assemble(spread_out(join(encoder_parts, bf16), "cells"), "cells", 0).astype(f32)

    scale_total = spread[:width] * inverse_cells
    dropout_total = spread[width : 2 * width] * (0.5 * inverse_cells)
    scale_bias_total = spread[2 * width] * inverse_cells
    dropout_bias_total = spread[2 * width + 1] * (0.5 * inverse_cells)
    theta_total = -jnp.exp(log_theta) * spread[2 * width + 2] * inverse_cells
    at = 16 + names
    mean_loss = jnp.sum(pack[at + 64 : at + 72])
    return (
        mean_loss,
        input_gradient,
        encoder_total * inverse_cells,
        pack[at + 72 : at + 72 + names],
        sums[1] * inverse_cells,
        sums[0] * inverse_cells,
        pack[at : at + latents].T,
        pack[at + 32 : at + 32 + latents, 0],
        pack[at + 16 : at + 16 + latents].T,
        pack[at + 48 : at + 48 + latents, 0],
        pack[:latents],
        pack[16 : 16 + names],
        decoder_sums[1] * inverse_cells,
        decoder_sums[0] * inverse_cells,
        scale_total,
        scale_bias_total,
        dropout_total,
        dropout_bias_total,
        theta_total,
    )


def solution(mesh):
    return jax.shard_map(
        body,
        mesh=mesh,
        in_specs=(
            P("cells", "genes"),
            P("cells"),
            P("cells"),
            P(None, "genes"),
            P("cells", None),
            P("genes", None),
            P(),
            P(),
            P(),
            P(),
            P(),
            P(),
            P(),
            P(),
            P(),
            P(),
            P(),
            P(None, "genes"),
            P("genes"),
            P(None, "genes"),
            P("genes"),
            P("genes"),
        ),
        out_specs=(
            P(),
            P("cells", "genes"),
            P("genes", None),
            P(),
            P(),
            P(),
            P(),
            P(),
            P(),
            P(),
            P(),
            P(),
            P(),
            P(),
            P(None, "genes"),
            P("genes"),
            P(None, "genes"),
            P("genes"),
            P("genes"),
        ),
        check_vma=False,
    )
```

```python
import jax
import jax.numpy as jnp
from jax import lax
from jax.experimental import pallas as pl
from jax.experimental.pallas import tpu as pltpu
from jax.sharding import PartitionSpec as P

highest = lax.Precision.HIGHEST
norm_eps = 0.001
log_eps = 1e-08
f32 = jnp.float32
bf16 = jnp.bfloat16
i32 = jnp.int32
LANE = 128
ALIGN = 16
CAP = 384
RB = 320
TOP = 24
WIRE = bf16
VMEM_MB = 1 << 20
by_last = (((1,), (1,)), ((), ()))
by_first = (((0,), (0,)), ((), ()))


def cuts(total, width):
    return [(i, min(width, total - i)) for i in range(0, total, width)]


def fit(v, width=LANE):
    return v if v.shape[1] == width else jnp.pad(v, ((0, 0), (0, width - v.shape[1])))


def vmem():
    return pl.BlockSpec(memory_space=pltpu.VMEM)


def smem():
    return pl.BlockSpec(memory_space=pltpu.SMEM)


def anywhere():
    return pl.BlockSpec(memory_space=pl.ANY)


def params(mib):
    return pltpu.CompilerParams(vmem_limit_bytes=mib * VMEM_MB)


def cost(micros):
    return pl.CostEstimate(
        flops=int(micros * 0.01 * 1.1e9), bytes_accessed=int(micros * 0.01 * 3.6e6), transcendentals=0
    )


def split3(v):
    high = lax.reduce_precision(v, 8, 7)
    rest = v - high
    middle = lax.reduce_precision(rest, 8, 7)
    return high.astype(bf16), middle.astype(bf16), (rest - middle).astype(bf16)


def swap(v, axis, bits):
    n = lax.axis_size(axis)
    return lax.ppermute(v, axis, [(i, i ^ bits) for i in range(n)])


def tree_sum(parts):
    while len(parts) > 1:
        parts = [parts[i] + parts[i + 1] for i in range(0, len(parts), 2)]
    return parts[0]


def total_direct(v, axis, unit=1):
    n = lax.axis_size(axis)
    return tree_sum([v] + [swap(v, axis, s) for s in range(unit, n, unit)])


def total_genes(v):
    return total_direct(v + swap(v, "genes", 1), "genes", 2)


def piece_of(v, i, size, axis):
    return lax.dynamic_slice_in_dim(v, i * size, size, axis)


def pieces_for(v, axis, dim, wire, unit=1):
    groups = lax.axis_size(axis) // unit
    spot = lax.axis_index(axis) // unit
    size = v.shape[dim] // groups
    low = v.astype(wire)
    own = piece_of(v, spot, size, dim).astype(f32)
    return [own] + [piece_of(low, spot ^ s, size, dim) for s in range(1, groups)]


def exchange(pieces, axis, unit=1):
    return pieces[:1] + [swap(piece, axis, unit * s) for s, piece in enumerate(pieces) if s]


def axis_scatter(v, axis, dim, wire, unit=1):
    return exchange(pieces_for(v, axis, dim, wire, unit), axis, unit)


def join(parts, wire):
    return tree_sum([part.astype(f32) for part in parts]).astype(wire)


def spread_out(own, axis, unit=1):
    groups = lax.axis_size(axis) // unit
    return [own] + [swap(own, axis, unit * s) for s in range(1, groups)]


def assemble(pieces, axis, dim, unit=1):
    spot = lax.axis_index(axis) // unit
    size = pieces[0].shape[dim]
    shape = list(pieces[0].shape)
    shape[dim] = size * len(pieces)
    whole = jnp.zeros(shape, pieces[0].dtype)
    for s, piece in enumerate(pieces):
        whole = lax.dynamic_update_slice_in_dim(whole, piece, (spot ^ s) * size, dim)
    return whole


def rows_pieces(v, wire):
    core = lax.axis_index("genes") % 2
    half = v.shape[0] // 2
    mine = piece_of(v, core, half, 0)
    other = piece_of(v, 1 - core, half, 0)
    summed = mine + swap(other.astype(wire), "genes", 1).astype(f32)
    return pieces_for(summed, "genes", 0, wire, 2)


def rows_whole(block):
    core = lax.axis_index("genes") % 2
    far = swap(block, "genes", 1)
    first = jnp.where(core == 0, block, far)
    second = jnp.where(core == 0, far, block)
    return jnp.concatenate([first, second], axis=0).astype(f32)


def after(value, *earlier):
    return lax.optimization_barrier((value, *earlier))


def arriving(source, target, arrived, blocks):
    block = target.shape[0] // blocks
    rows = [pl.ds(i * block, block) for i in range(blocks)]
    copies = [
        pltpu.make_async_copy(source.at[rows[i], :], target.at[rows[i], :], arrived.at[i])
        for i in range(blocks)
    ]
    for copy in copies:
        copy.start()
    return rows, copies


def encode_kernel(blocks, counts_hbm, weight_ref, part_ref, lib_ref, counts_ref, arrived):
    cells, genes = counts_ref.shape
    block = cells // blocks
    rows, copies = arriving(counts_hbm, counts_ref, arrived, blocks)
    for i in range(blocks):
        copies[i].wait()
        lib = jnp.zeros((block, LANE), f32)
        part = jnp.zeros((block, part_ref.shape[1]), f32)
        for start, width in cuts(genes, 2 * LANE):
            at = pl.ds(start, width)
            real = counts_ref[rows[i], at].astype(f32)
            expr = jnp.log(1.0 + real).astype(bf16)
            part = part + jnp.dot(expr, weight_ref[at, :], preferred_element_type=f32)
            for first, wide in cuts(width, LANE):
                lib = lib + fit(real[:, first : first + wide])
        part_ref[rows[i], :] = part
        lib_ref[rows[i], :] = lib


def encode(counts, weight):
    cells, genes = counts.shape
    hidden = weight.shape[1]
    blocks = 8
    return pl.pallas_call(
        lambda *refs: encode_kernel(blocks, *refs),
        in_specs=[anywhere(), vmem()],
        out_specs=[vmem(), vmem()],
        out_shape=[
            jax.ShapeDtypeStruct((cells, hidden), f32),
            jax.ShapeDtypeStruct((cells, LANE), f32),
        ],
        scratch_shapes=[pltpu.VMEM((cells, genes), i32), pltpu.SemaphoreType.DMA((blocks,))],
        compiler_params=params(32),
        cost_estimate=cost(8),
        name="encode",
    )(counts, weight)


def order_kernel(mask_ref, data_ref, pos_ref, rank_ref, meta_ref):
    groups, genes = mask_ref.shape
    cells = data_ref.shape[1]
    row = lax.broadcasted_iota(i32, (LANE, LANE), 0)
    col = lax.broadcasted_iota(i32, (LANE, LANE), 1)
    upto = (row <= col).astype(bf16)
    group = lax.broadcasted_iota(i32, (groups, LANE), 0)

    def running(hot, so_far, width):
        inside = jnp.dot(hot.astype(bf16), upto[:width, :width], preferred_element_type=f32)
        return so_far + inside, so_far + jnp.sum(hot, axis=1, keepdims=True)

    so_far = jnp.zeros((groups, 1), f32)
    for start, width in cuts(genes, LANE):
        hot = mask_ref[:, pl.ds(start, width)].astype(f32)
        count, so_far = running(hot, so_far, width)
        place = jnp.where(hot > 0.5, count - 1.0, -1.0).astype(i32)
        if width < LANE:
            place = jnp.pad(place, ((0, 0), (0, LANE - width)), constant_values=-1)
        pos_ref[:, pl.ds(start, LANE)] = place
    gene_count = so_far

    so_far = jnp.zeros((groups, 1), f32)
    kept = []
    for start, width in cuts(cells, LANE):
        data = data_ref[:, pl.ds(start, width)]
        hot = (group[:, :width] == data).astype(f32)
        count, so_far = running(hot, so_far, width)
        kept.append((start, width, hot, count))
    cell_count = so_far
    padded = jnp.floor((cell_count + (ALIGN - 1)) * (1.0 / ALIGN))
    before = lax.broadcasted_iota(i32, (groups, groups), 1) < lax.broadcasted_iota(
        i32, (groups, groups), 0
    )
    spread = jnp.broadcast_to(padded, (groups, LANE))
    begin = ALIGN * jnp.dot(
        before.astype(f32), spread, precision=highest, preferred_element_type=f32
    )
    for start, width, hot, count in kept:
        place = hot * (begin[:, :width] + count - 1.0)
        rank_ref[:, pl.ds(start, width)] = jnp.sum(place, axis=0, keepdims=True).astype(i32)
    lane = lax.broadcasted_iota(i32, (groups, LANE), 1)
    meta = jnp.where(lane == 0, cell_count, jnp.where(lane == 1, begin, gene_count))
    meta_ref[...] = meta.astype(i32)


def order_cells(mask, data):
    groups, genes = mask.shape
    cells = data.shape[0]
    pos, rank, meta = pl.pallas_call(
        order_kernel,
        in_specs=[vmem(), vmem()],
        out_specs=[vmem(), vmem(), vmem()],
        out_shape=[
            jax.ShapeDtypeStruct((groups, -(-genes // LANE) * LANE), i32),
            jax.ShapeDtypeStruct((1, cells), i32),
            jax.ShapeDtypeStruct((groups, LANE), i32),
        ],
        cost_estimate=cost(2),
        name="order_cells",
    )(mask, data.reshape(1, cells))
    return pos, rank, meta[:, :3].reshape(-1)


def pass_count(meta_ref, groups):
    most = meta_ref[2]
    for d in range(1, groups):
        most = jnp.maximum(most, meta_ref[3 * d + 2])
    return jnp.maximum((most + CAP - 1) // CAP, 1)


def chunk_of(meta_ref, d, i, rows_all):
    count = meta_ref[3 * d]
    begin = meta_ref[3 * d + 1]
    low = begin + i * RB
    first = pl.multiple_of(jnp.minimum(low, rows_all - RB), ALIGN)
    return first, low, begin + count


def pack_width(genes, pieces):
    return -(-genes // pieces // LANE) * LANE


def sort_kernel(
    blocks, pieces, rank_ref, counts_hbm, sorted_hbm, counts_ref, pack_ref, sorted_ref, came, gone
):
    cells, genes = counts_ref.shape
    rows_all = sorted_ref.shape[0]
    block = cells // blocks
    unroll = 32
    rows, copies = arriving(counts_hbm, counts_ref, came, blocks)
    for i in range(blocks):
        copies[i].wait()
        for start, width in cuts(genes // pieces, LANE):
            packed = None
            for piece in range(pieces):
                one = counts_ref[rows[i], pl.ds(pieces * start + piece * width, width)]
                packed = one if piece == 0 else packed | (one << (8 * piece))
            pack_ref[:, pl.ds(start, width)] = packed

        def move(j, carry):
            base = pl.multiple_of(j * unroll, unroll)
            tile = pack_ref[pl.ds(base, unroll), :]
            for u in range(unroll):
                sorted_ref[pl.ds(rank_ref[i * block + base + u], 1), :] = tile[u : u + 1, :]
            return carry

        lax.fori_loop(0, block // unroll, move, 0)
    copy = pltpu.make_async_copy(sorted_ref, sorted_hbm.at[pl.ds(0, rows_all), :], gone)
    copy.start()
    copy.wait()


def sort_rows(rank, counts, pieces, rows_all):
    cells, genes = counts.shape
    narrow = pack_width(genes, pieces)
    blocks = 8
    return pl.pallas_call(
        lambda *refs: sort_kernel(blocks, pieces, *refs),
        in_specs=[smem(), anywhere()],
        out_specs=anywhere(),
        out_shape=jax.ShapeDtypeStruct((rows_all + RB, narrow), i32),
        scratch_shapes=[
            pltpu.VMEM((cells, genes), i32),
            pltpu.VMEM((cells // blocks, narrow), i32),
            pltpu.VMEM((rows_all, narrow), i32),
            pltpu.SemaphoreType.DMA((blocks,)),
            pltpu.SemaphoreType.DMA,
        ],
        compiler_params=params(58),
        cost_estimate=cost(11),
        name="sort_rows",
    )(rank, counts)


def compact_kernel(
    pieces, genes, members, first_call, meta_ref, sorted_hbm, pos_ref, scale_ref, dropout_ref,
    extra_ref, *rest,
):
    if not first_call:
        rest = rest[3:]
    y_hbm, w_hbm, c_hbm, rows_ref, stack_ref, pick_ref, found_ref, table_ref, y_ref, w_ref, c_ref, came, gone = rest
    width = w_ref.shape[1]
    both = 2 * width
    quarter = genes // pieces
    groups = pos_ref.shape[0]
    stack_ref[RB : RB + both // 2, :] = scale_ref[...]
    stack_ref[RB + both // 2 : RB + both, :] = dropout_ref[...] * jnp.asarray(0.5, bf16)
    stack_ref[RB + both :, :] = extra_ref[...]

    def rows_of(d, i):
        low = pl.multiple_of(meta_ref[3 * d + 1] + i * RB, ALIGN)
        return low, meta_ref[3 * d + 1] + meta_ref[3 * d]

    def bring(n, d, i):
        low, _ = rows_of(d, i)
        return pltpu.make_async_copy(sorted_hbm.at[pl.ds(low, RB), :], rows_ref.at[n], came.at[n])

    def widen(n):
        for start, wide in cuts(quarter, LANE):
            raw = rows_ref[n, :, pl.ds(start, wide)]
            for piece in range(pieces):
                part = raw if pieces == 1 else (raw >> (8 * piece)) & 255
                stack_ref[:RB, pl.ds(pieces * start + piece * wide, wide)] = part.astype(f32).astype(bf16)

    def look(n, d, i, k, sums):
        low, high = rows_of(d, i)

        def step(j, sums):
            gamma_in, digamma_in = sums
            src = pl.ds(pl.multiple_of(j * 16, 16), 16)
            row = lax.broadcasted_iota(i32, (16, CAP), 0) + (low + j * 16)
            col = lax.broadcasted_iota(i32, (16, CAP), 1) + k * CAP
            own = (row < high) & (col < meta_ref[3 * d + 2])
            value = jnp.where(own, found_ref[src, :], -1.0)
            y_ref[n, src, :] = value.astype(bf16)
            index = jnp.maximum(value, 0.0).astype(i32)
            for h in (0, 8):
                here = index[h : h + 8]
                inner = here & 7
                got = []
                for base in (0, TOP):
                    g0 = jnp.take_along_axis(table_ref[base : base + 8, :], inner, axis=0)
                    g1 = jnp.take_along_axis(table_ref[base + 8 : base + 16, :], inner, axis=0)
                    g2 = jnp.take_along_axis(table_ref[base + 16 : base + 24, :], inner, axis=0)
                    got.append(jnp.where(here < 8, g0, jnp.where(here < 16, g1, g2)))
                gamma_in = gamma_in + got[0]
                digamma_in = digamma_in + got[1]
            return gamma_in, digamma_in

        return lax.fori_loop(0, RB // 16, step, sums, unroll=2)

    def leave(n, d, i, k):
        low, _ = rows_of(d, i)
        return pltpu.make_async_copy(y_ref.at[n], y_hbm.at[k, pl.ds(low, RB), :], gone.at[3 * n])

    def one_pass(k, carry):
        for n, d in enumerate(members):
            bring(n, d, 0).start()
        pending = []
        for n, d in enumerate(members):
            column = lax.broadcasted_iota(i32, (CAP, 1), 0) + k * CAP
            for start, wide in cuts(genes, 2 * LANE):
                place = pos_ref[d : d + 1, pl.ds(start, -(-wide // LANE) * LANE)]
                pick = (column == place).astype(f32).astype(bf16)
                pick_ref[:, pl.ds(start, wide)] = pick[:, :wide]
            bring(n, d, 0).wait()
            widen(n)
            found_ref[...] = lax.dot_general(
                stack_ref[...], pick_ref[...], by_last, preferred_element_type=f32
            )
            w_ref[n, :, :CAP] = found_ref[RB : RB + width, :].astype(bf16)
            w_ref[n, :, CAP:] = found_ref[RB + width : RB + both, :].astype(bf16)
            side = [found_ref[RB + both + j : RB + both + j + 1, :] for j in range(9)]
            scale_bias = side[0] + side[1] + side[2]
            dropout_bias = side[3] + side[4] + side[5]
            log_theta = side[6] + side[7] + side[8]
            used = lax.broadcasted_iota(i32, (1, CAP), 1) + k * CAP < meta_ref[3 * d + 2]
            scale_bias = jnp.where(used, scale_bias, -1e30)
            theta = jnp.exp(log_theta)
            gamma_sum = jnp.zeros((1, CAP), f32)
            digamma_sum = jnp.zeros((1, CAP), f32)
            table_ref[...] = jnp.zeros_like(table_ref)
            for x in range(1, TOP):
                base = theta + float(x - 1)
                gamma_sum = gamma_sum + jnp.log(base * (1.0 / x))
                digamma_sum = digamma_sum + 1.0 / base
                table_ref[x : x + 1, :] = gamma_sum
                table_ref[TOP + x : TOP + x + 1, :] = digamma_sum
            zero = jnp.zeros((8, CAP), f32)
            sums = look(n, d, 0, k, (zero, zero))
            if pending:
                pending[-1].wait()
                pending.pop()
            last = leave(n, d, 0, k)
            last.start()

            def more(i, sums):
                leave(n, d, i - 1, k).wait()
                bring(n, d, i).start()
                bring(n, d, i).wait()
                widen(n)
                found_ref[:RB, :] = lax.dot_general(
                    stack_ref[:RB, :], pick_ref[...], by_last, preferred_element_type=f32
                )
                sums = look(n, d, i, k, sums)
                leave(n, d, i, k).start()
                return sums

            chunks = (meta_ref[3 * d] + RB - 1) // RB
            gammas, digammas = lax.fori_loop(1, chunks, more, sums)
            pending.append(last)
            c_ref[n] = jnp.zeros((8, CAP), f32)
            c_ref[n, 0:1, :] = scale_bias
            c_ref[n, 1:2, :] = dropout_bias
            c_ref[n, 2:3, :] = theta
            c_ref[n, 5:6, :] = theta + log_eps
            c_ref[n, 6:7, :] = jnp.log(theta + log_eps)
            c_ref[n, 7:8, :] = theta / (theta + log_eps)
            c_ref[n, 3:4, :] = jnp.sum(gammas, axis=0, keepdims=True)
            c_ref[n, 4:5, :] = jnp.sum(digammas, axis=0, keepdims=True)
            for copy in sides(n, d, k):
                copy.start()
        pending.pop().wait()
        for n, d in enumerate(members):
            for copy in sides(n, d, k):
                copy.wait()
        return carry

    def sides(n, d, k):
        return [
            pltpu.make_async_copy(w_ref.at[n], w_hbm.at[k, d], gone.at[3 * n + 1]),
            pltpu.make_async_copy(c_ref.at[n], c_hbm.at[k, d], gone.at[3 * n + 2]),
        ]

    lax.fori_loop(0, pass_count(meta_ref, groups), one_pass, 0)


def compact(members, meta, sorted_rows, pos, scale_weight, dropout_weight, extra, genes, pieces, before):
    groups = pos.shape[0]
    tall, narrow = sorted_rows.shape
    passes = -(-genes // CAP)
    both = 2 * scale_weight.shape[0]
    count = len(members)
    first_call = before is None
    return pl.pallas_call(
        lambda *refs: compact_kernel(pieces, genes, members, first_call, *refs),
        in_specs=[smem(), anywhere(), vmem(), vmem(), vmem(), vmem()]
        + ([] if first_call else [anywhere()] * 3),
        out_specs=[anywhere()] * 3,
        out_shape=[
            jax.ShapeDtypeStruct((passes, tall, CAP), bf16),
            jax.ShapeDtypeStruct((passes, groups, both // 2, 2 * CAP), bf16),
            jax.ShapeDtypeStruct((passes, groups, 8, CAP), f32),
        ],
        input_output_aliases={} if first_call else {6: 0, 7: 1, 8: 2},
        scratch_shapes=[
            pltpu.VMEM((count, RB, narrow), i32),
            pltpu.VMEM((RB + both + 16, genes), bf16),
            pltpu.VMEM((CAP, genes), bf16),
            pltpu.VMEM((RB + both + 16, CAP), f32),
            pltpu.VMEM((2 * TOP, CAP), f32),
            pltpu.VMEM((count, RB, CAP), bf16),
            pltpu.VMEM((count, both // 2, 2 * CAP), bf16),
            pltpu.VMEM((count, 8, CAP), f32),
            pltpu.SemaphoreType.DMA((count,)),
            pltpu.SemaphoreType.DMA((3 * count,)),
        ],
        compiler_params=params(58),
        cost_estimate=cost(4 * count),
        name="compact",
    )(meta, sorted_rows, pos, scale_weight, dropout_weight, extra, *(before or ()))


def softmax_kernel(
    hidden_ref, lib_ref, weight_ref, bias_ref, stat_ref, top_out_ref, back_ref,
    even_ref, odd_ref, even_top_ref, odd_top_ref, column_ref,
):
    rows, genes = even_ref.shape
    blocks = back_ref.shape[0] // rows
    columns = cuts(genes, 2 * LANE)

    def place(i):
        return pl.ds(pl.multiple_of(i * rows, ALIGN), rows)

    def logits(i, c, logit_ref, top_ref):
        start, width = columns[c]
        at = pl.ds(start, width)
        logit = (
            jnp.dot(hidden_ref[place(i), :], weight_ref[:, at], preferred_element_type=f32)
            + bias_ref[:, at]
        )
        logit_ref[:, at] = logit
        top = None if c == 0 else top_ref[...]
        for first, wide in cuts(width, LANE):
            piece = logit[:, first : first + wide]
            if wide < LANE:
                piece = jnp.broadcast_to(jnp.max(piece, axis=1, keepdims=True), (rows, LANE))
            top = piece if top is None else jnp.maximum(top, piece)
        top_ref[...] = top

    def one(i, logit_ref, top_ref, next_ref, next_top_ref):
        here = place(i)
        after_this = jnp.minimum(i + 1, blocks - 1)
        top = jnp.max(top_ref[...], axis=1, keepdims=True)
        total = jnp.zeros((rows, LANE), f32)
        for c, (start, width) in enumerate(columns):
            logits(after_this, c, next_ref, next_top_ref)
            at = pl.ds(start, width)
            value = jnp.exp(logit_ref[:, at] - top)
            for first, wide in cuts(width, LANE):
                total = total + fit(value[:, first : first + wide])
            back = lax.dot_general(
                value.astype(bf16), weight_ref[:, at], by_last, preferred_element_type=f32
            )
            if c == 0:
                back_ref[here, :] = back
            else:
                back_ref[here, :] += back
        total = jnp.sum(total, axis=1, keepdims=True)
        lane = lax.broadcasted_iota(i32, (rows, LANE), 1)
        top_out_ref[here, :] = jnp.broadcast_to(top, (rows, LANE))
        column_ref[here, :] = jnp.where(lane == 0, top, jnp.where(lane == 1, total, lib_ref[here, :]))

    for c in range(len(columns)):
        logits(0, c, even_ref, even_top_ref)

    def pair(j, carry):
        one(2 * j, even_ref, even_top_ref, odd_ref, odd_top_ref)
        one(2 * j + 1, odd_ref, odd_top_ref, even_ref, even_top_ref)
        return carry

    lax.fori_loop(0, blocks // 2, pair, 0)
    stat_ref[...] = jnp.zeros_like(stat_ref)
    for i in range(column_ref.shape[0] // LANE):
        tile = column_ref[i * LANE : (i + 1) * LANE, :].T
        for j in range(3):
            stat_ref[j, i : i + 1, :] = tile[j : j + 1, :]


def row_block(rows_all):
    return rows_all // 8 if rows_all % 128 == 0 else rows_all


def softmax_part(hidden, lib, weight, bias):
    rows_all, width = hidden.shape
    genes = weight.shape[1]
    block = row_block(rows_all)
    tall = -(-rows_all // LANE // 8) * 8
    return pl.pallas_call(
        softmax_kernel,
        in_specs=[vmem()] * 4,
        out_specs=[vmem()] * 3,
        out_shape=[
            jax.ShapeDtypeStruct((3, tall, LANE), f32),
            jax.ShapeDtypeStruct((rows_all, LANE), f32),
            jax.ShapeDtypeStruct((rows_all, width), f32),
        ],
        scratch_shapes=[
            pltpu.VMEM((block, genes), f32),
            pltpu.VMEM((block, genes), f32),
            pltpu.VMEM((block, LANE), f32),
            pltpu.VMEM((block, LANE), f32),
            pltpu.VMEM((rows_all, LANE), f32),
        ],
        compiler_params=params(24),
        cost_estimate=cost(10),
        name="softmax_part",
    )(hidden, lib, weight, bias)


def likelihood_kernel(
    meta_ref, hidden_ref, shift_ref, y_hbm, w_hbm, c_hbm,
    back_ref, inner_ref, loss_ref, g_hbm,
    row_sum_ref, y_ref, w_ref, c_ref, logit_ref, grad_ref, g_ref, came, gone,
):
    rows_all, width = hidden_ref.shape
    groups = w_ref.shape[0]
    both = 2 * width
    step = 32
    back_ref[...] = jnp.zeros_like(back_ref)
    row_sum_ref[...] = jnp.zeros_like(row_sum_ref)
    inner_ref[...] = jnp.zeros_like(inner_ref)
    loss_ref[...] = jnp.zeros_like(loss_ref)
    w_ref[:, width:, :CAP] = jnp.ones((groups, width, CAP), bf16)
    w_ref[:, width:, CAP:] = jnp.zeros((groups, width, CAP), bf16)

    def one_pass(k, carry):
        def bring(d):
            first, _, _ = chunk_of(meta_ref, d, 0, rows_all)
            return (
                pltpu.make_async_copy(w_hbm.at[k, d], w_ref.at[d, pl.ds(0, width), :], came.at[d]),
                pltpu.make_async_copy(
                    y_hbm.at[k, pl.ds(first, RB), :], y_ref.at[d], came.at[groups + d]
                ),
            )

        def leave(d):
            at = pl.ds(pl.multiple_of(d * CAP, LANE), CAP)
            return pltpu.make_async_copy(g_ref.at[:, at], g_hbm.at[k, :, at], gone.at[d])

        consts = pltpu.make_async_copy(c_hbm.at[k], c_ref, came.at[2 * groups])
        consts.start()
        for d in range(groups):
            for copy in bring(d):
                copy.start()
        consts.wait()

        def one_group(d, carry):
            for copy in bring(d):
                copy.wait()
            weight = w_ref[d]
            const = c_ref[d]
            at = pl.ds(pl.multiple_of(d * CAP, LANE), CAP)
            g_ref[:, at] = jnp.zeros((both + 16, CAP), f32)
            lower = width + 8

            def one_chunk(i, sums):
                first, low, high = chunk_of(meta_ref, d, i, rows_all)
                rows = pl.ds(first, RB)
                hidden = hidden_ref[rows, :]

                @pl.when(i > 0)
                def _():
                    pltpu.sync_copy(y_hbm.at[k, rows, :], y_ref.at[d])

                logit_ref[...] = jnp.dot(hidden, weight[:width], preferred_element_type=f32)

                def element(j, sums):
                    src = pl.ds(pl.multiple_of(j * step, step), step)
                    row = pl.ds(pl.multiple_of(first + j * step, 16), step)
                    shift = shift_ref[row, :]
                    halves, powers, num, den = sums[:4]
                    place = lax.broadcasted_iota(i32, (step, LANE), 0) + (first + j * step)
                    inside = (place >= low) & (place < high)
                    columns = []
                    for n, (start, wide) in enumerate(cuts(CAP, LANE)):
                        here = pl.ds(start, wide)
                        there = pl.ds(CAP + start, wide)
                        own = lambda k: c_ref[d, k : k + 1, start : start + wide]
                        theta = own(2)
                        y = jnp.where(inside, y_ref[d, src, here].astype(f32), -1.0)
                        mean = jnp.exp(logit_ref[src, here] + (own(0) + shift))
                        t = mean + own(5)
                        log_t = jnp.log(t)
                        inv_t = pl.reciprocal(t, approx=False)
                        down = own(6) - log_t
                        weighted_in = y >= 0.0
                        half = jnp.where(weighted_in, logit_ref[src, there] + own(1), 0.0)
                        joint = jnp.where(y == 0.0, (0.5 * theta) * down - half, 32.0 * y)
                        joint = jnp.where(weighted_in, joint, 0.0)
                        count = jnp.maximum(y, 0.0)
                        tan_drop = jnp.tanh(half)
                        tan_joint = jnp.tanh(joint)
                        one = jnp.where(weighted_in, 1.0, 0.0)
                        chance = one + tan_joint
                        pull = ((0.5 * theta) * chance + count) * inv_t
                        me = mean + log_eps
                        drift = (pull - count * pl.reciprocal(me, approx=False)) * mean
                        twice = tan_joint + tan_drop
                        grad_ref[src, here] = drift.astype(bf16)
                        grad_ref[src, there] = twice.astype(bf16)
                        slope = chance * (0.5 * (down + own(7))) - pull
                        fold = lambda v: jnp.sum(v.reshape(step // 8, 8, wide), axis=0)
                        old = sums[4 + n]
                        columns.append(
                            (
                                old[0] + fold(slope),
                                old[1] + fold(drift),
                                old[2] + fold(twice),
                                old[3] + fold(one * down),
                            )
                        )
                        halves = halves + (jnp.minimum(joint, 0.0) + jnp.maximum(half, 0.0))
                        powers = powers + count * (jnp.log(me) - log_t)
                        num = num + num * jnp.abs(tan_drop)
                        den = den + den * jnp.abs(tan_joint)
                    return (halves, powers, num, den, *columns)

                def clear(j, carry):
                    src = pl.ds(pl.multiple_of(j * step, step), step)
                    grad_ref[src, :] = jnp.zeros((step, 2 * CAP), bf16)
                    return carry

                steps = jnp.minimum((high - first + step - 1) // step, RB // step)
                one_rows = jnp.ones((step, LANE), f32)
                got = lax.fori_loop(
                    0, steps, element, (sums[0], sums[1], one_rows, one_rows, *sums[2:])
                )
                lax.fori_loop(steps, RB // step, clear, 0)
                halves, powers, num, den = got[:4]
                powers = powers + (jnp.log(num) - jnp.log(den))
                grads = grad_ref[...]
                outer = lax.dot_general(hidden, grads, by_first, preferred_element_type=f32)
                g_ref[:width, at] += outer[:, :CAP]
                g_ref[lower : lower + width, at] += outer[:, CAP:]
                sums_both = lax.dot_general(grads, weight, by_last, preferred_element_type=f32)
                back_ref[rows, :] += sums_both[:, :width]
                row_sum_ref[rows, :] += sums_both[:, width:]
                return (halves, powers, *got[4:])

            zero = jnp.zeros((8, LANE), f32)
            start_sums = (jnp.zeros((step, LANE), f32),) * 2 + tuple(
                (zero,) * 4 for _ in cuts(CAP, LANE)
            )
            chunks = (meta_ref[3 * d] + RB - 1) // RB
            got = lax.fori_loop(0, chunks, one_chunk, start_sums)
            count_sum = const[3:4, :LANE]
            for start, wide in cuts(CAP, LANE)[1:]:
                count_sum = count_sum + const[3:4, start : start + wide]
            parts = (got[1] - 2.0 * got[0]).reshape(step // 8, 8, LANE)
            total = jnp.sum(parts, axis=0) + jnp.where(
                lax.broadcasted_iota(i32, (8, LANE), 0) == 0, count_sum, 0.0
            )
            for n, (start, wide) in enumerate(cuts(CAP, LANE)):
                total = total + got[2 + n][3] * const[2:3, start : start + wide]
            loss_ref[...] += total
            for n, (start, wide) in enumerate(cuts(CAP, LANE)):
                here = pl.ds(pl.multiple_of(d * CAP + start, LANE), wide)
                slope, drift, twice = (
                    jnp.sum(v, axis=0, keepdims=True) for v in got[2 + n][:3]
                )
                g_ref[width : width + 1, here] = drift
                g_ref[both + 8 : both + 9, here] = twice
                g_ref[both + 9 : both + 10, here] = slope + const[4:5, start : start + wide]
            leave(d).start()
            return carry

        lax.fori_loop(0, groups, one_group, 0)
        for d in range(groups):
            leave(d).wait()
        return carry

    lax.fori_loop(0, pass_count(meta_ref, groups), one_pass, 0)
    for i in range(rows_all // LANE):
        tile = row_sum_ref[i * LANE : (i + 1) * LANE, :].T
        inner_ref[i : i + 1, :] = tile[0:1, :]


def likelihood(meta, hidden, shift, y, w, c):
    rows_all, width = hidden.shape
    passes, groups = w.shape[:2]
    both = 2 * width
    return pl.pallas_call(
        likelihood_kernel,
        in_specs=[smem(), vmem(), vmem(), anywhere(), anywhere(), anywhere()],
        out_specs=[vmem(), vmem(), vmem(), anywhere()],
        out_shape=[
            jax.ShapeDtypeStruct((rows_all, width), f32),
            jax.ShapeDtypeStruct((-(-rows_all // LANE // 8) * 8, LANE), f32),
            jax.ShapeDtypeStruct((8, LANE), f32),
            jax.ShapeDtypeStruct((passes, both + 16, groups * CAP), f32),
        ],
        scratch_shapes=[
            pltpu.VMEM((rows_all, width), f32),
            pltpu.VMEM((groups, RB, CAP), bf16),
            pltpu.VMEM((groups, both, 2 * CAP), bf16),
            pltpu.VMEM((groups, 8, CAP), f32),
            pltpu.VMEM((RB, 2 * CAP), f32),
            pltpu.VMEM((RB, 2 * CAP), bf16),
            pltpu.VMEM((both + 16, groups * CAP), f32),
            pltpu.SemaphoreType.DMA((2 * groups + 1,)),
            pltpu.SemaphoreType.DMA((groups,)),
        ],
        compiler_params=params(58),
        cost_estimate=cost(20),
        name="likelihood",
    )(meta, hidden, shift, y, w, c)


def expand_kernel(use_rows, first, tall, meta_ref, g_ref, pos_ref, *rest):
    if use_rows:
        row_ref, hidden_ref, top_ref, weight_ref, bias_ref = rest[:5]
        g_hbm, out_ref, pick_ref, more_ref, logit_ref, total_ref = rest[5:]
    else:
        g_hbm, out_ref, pick_ref, more_ref, _, total_ref = rest
    groups = pos_ref.shape[0]
    genes = out_ref.shape[1]

    def choose(k, d):
        column = lax.broadcasted_iota(i32, (CAP, 1), 0) + k * CAP
        pick_ref[d * CAP : (d + 1) * CAP, :] = (
            (column == pos_ref[d : d + 1, :]).astype(f32).astype(bf16)[:, :genes]
        )

    def spread(k, g):
        for d in range(groups):
            choose(k, d)
        return jnp.dot(g.astype(bf16), pick_ref[...], preferred_element_type=f32)

    if use_rows:
        for d in range(groups):
            choose(0, d)
        logit_ref[...] = jnp.dot(hidden_ref[...], weight_ref[...], preferred_element_type=f32)
        sparse = jnp.dot(g_ref[0].astype(bf16), pick_ref[...], preferred_element_type=f32)
        total_ref[...] = sparse
        pieces = cuts(hidden_ref.shape[0], 2 * LANE)
        got = None
        for start, high in pieces:
            here = pl.ds(start, high)
            value = jnp.exp(logit_ref[here, :] + (bias_ref[...] - top_ref[here, 0:1]))
            more = jnp.dot(
                row_ref[:, start : start + high], value.astype(bf16), preferred_element_type=f32
            )
            got = more if got is None else got + more
        total_ref[...] -= got
    else:
        total_ref[...] = spread(0, g_ref[0])

    def more(k, carry):
        pltpu.sync_copy(g_hbm.at[k, pl.ds(first, tall), :], more_ref)
        total_ref[...] += spread(k, more_ref[...])
        return carry

    lax.fori_loop(1, pass_count(meta_ref, groups), more, 0)
    out_ref[...] = total_ref[...].astype(bf16)


def expand(meta, g, pos, genes, part, rows=None, hidden=None, top=None, weight=None, bias=None):
    groups = pos.shape[0]
    tall = g.shape[1] // 2
    block = 512 if genes % 512 == 0 else genes
    extra = [] if rows is None else [rows, hidden, top, weight, bias]
    extra_specs = []
    if extra:
        extra_specs = [pl.BlockSpec(v.shape, lambda i: (0, 0)) for v in (rows, hidden, top)]
        extra_specs += [pl.BlockSpec((v.shape[0], block), lambda i: (0, i)) for v in (weight, bias)]
    return pl.pallas_call(
        lambda *refs: expand_kernel(bool(extra), part * tall, tall, *refs),
        grid=(genes // block,),
        in_specs=[
            smem(),
            pl.BlockSpec((1, tall, groups * CAP), lambda i: (0, part, 0)),
            pl.BlockSpec((groups, -(-block // LANE) * LANE), lambda i: (0, i)),
            *extra_specs,
            anywhere(),
        ],
        out_specs=pl.BlockSpec((tall, block), lambda i: (0, i)),
        out_shape=jax.ShapeDtypeStruct((tall, genes), bf16),
        scratch_shapes=[
            pltpu.VMEM((groups * CAP, block), bf16),
            pltpu.VMEM((tall, groups * CAP), f32),
            pltpu.VMEM((8 if rows is None else hidden.shape[0], block), f32),
            pltpu.VMEM((tall, block), f32),
        ],
        compiler_params=params(58),
        cost_estimate=cost(8),
        name="expand",
    )(meta, g, pos, *extra, g)


def norm_parts(x, stats, affine, total):
    center = stats[0:1] * (1.0 / total)
    variance = stats[1:2] * (1.0 / total) - center * center
    inverse = lax.rsqrt(variance + norm_eps)
    normed = (x - center) * inverse
    gated = normed * affine[0:1] + affine[1:2]
    sigma = 0.5 + 0.5 * jnp.tanh(0.5 * gated)
    return normed, inverse, gated, sigma


def two_rows(first, second):
    row = lax.broadcasted_iota(i32, (8, first.shape[1]), 0)
    return jnp.where(row == 0, first, jnp.where(row == 1, second, 0.0))


def sums_of(x):
    return two_rows(
        jnp.sum(x, axis=0, keepdims=True), jnp.sum(x * x, axis=0, keepdims=True)
    )


def exact(a, b, dims):
    return lax.dot_general(a, b, dims, precision=highest, preferred_element_type=f32)


plain = (((1,), (0,)), ((), ()))


def batch_rows(batch_ref, count):
    names = lax.broadcasted_iota(i32, (count, 1), 0)
    return (names == batch_ref[...]).astype(f32)


def latent_kernel(
    total, x_ref, stat_ref, affine_ref, heads_ref, bias_ref, noise_ref, decode_ref, add_ref,
    pre_ref, sums_ref, latent_ref, kl_ref,
):
    _, _, gated, sigma = norm_parts(x_ref[...], stat_ref, affine_ref, total)
    act = gated * sigma
    heads = exact(heads_ref[...], act, by_last) + bias_ref[:, 0:1]
    mean, logvar = heads[:16], heads[16:]
    scale = jnp.exp(0.5 * logvar)
    latent = mean + scale * noise_ref[...]
    latent_ref[0:16, :] = mean
    latent_ref[16:32, :] = logvar
    latent_ref[32:48, :] = latent
    latent_ref[48:64, :] = scale
    terms = jnp.exp(logvar) + mean * mean - 1.0 - logvar
    folded = jnp.zeros((16, LANE), f32)
    for start, width in cuts(terms.shape[1], LANE):
        folded = folded + terms[:, start : start + width]
    kl_ref[...] = 0.5 * (folded[:8] + folded[8:])
    pre = exact(latent, decode_ref[...], by_first) + add_ref[...]
    pre_ref[...] = pre
    sums_ref[...] = sums_of(pre)


def latent_stage(total, x, stat, affine, heads, bias, noise, decode, add):
    cells, width = x.shape
    return pl.pallas_call(
        lambda *refs: latent_kernel(total, *refs),
        in_specs=[vmem()] * 8,
        out_specs=[vmem()] * 4,
        out_shape=[
            jax.ShapeDtypeStruct((cells, width), f32),
            jax.ShapeDtypeStruct((8, width), f32),
            jax.ShapeDtypeStruct((64, cells), f32),
            jax.ShapeDtypeStruct((8, LANE), f32),
        ],
        compiler_params=params(18),
        cost_estimate=cost(2),
        name="latent_stage",
    )(x, stat, affine, heads, bias, noise, decode, add)


def hidden_kernel(total, pre_ref, stat_ref, affine_ref, rank_ref, lib_ref, hidden_ref, sum_ref, carry_ref):
    width = pre_ref.shape[1]
    rows_all = hidden_ref.shape[0]
    _, _, gated, sigma = norm_parts(pre_ref[...], stat_ref, affine_ref, total)
    carry_ref[:, :width] = (gated * sigma).astype(bf16)
    lib = jnp.sum(lib_ref[...], axis=1, keepdims=True)
    lane = lax.broadcasted_iota(i32, (lib.shape[0], LANE), 1)
    high = lib.astype(bf16).astype(f32)
    middle = (lib - high).astype(bf16).astype(f32)
    low = lib - high - middle
    carry_ref[:, width:] = jnp.where(
        lane == 0, high, jnp.where(lane == 1, middle, jnp.where(lane == 2, low, 0.0))
    ).astype(bf16)
    block = 2 * row_block(rows_all) if rows_all % 128 == 0 else rows_all

    def body(i, carry):
        first = pl.multiple_of(i * block, ALIGN)
        place = lax.broadcasted_iota(i32, (block, 1), 0) + first
        pick = (place == rank_ref[...]).astype(f32).astype(bf16)
        got = jnp.dot(pick, carry_ref[...], preferred_element_type=f32)
        hidden_ref[pl.ds(first, block), :] = got[:, :width].astype(bf16)
        sum_ref[pl.ds(first, block), :] = jnp.broadcast_to(
            jnp.sum(got[:, width:], axis=1, keepdims=True), (block, LANE)
        )
        return carry

    lax.fori_loop(0, rows_all // block, body, 0)


def hidden_stage(total, pre, stat, affine, rank, lib, rows_all):
    cells, width = pre.shape
    return pl.pallas_call(
        lambda *refs: hidden_kernel(total, *refs),
        in_specs=[vmem()] * 5,
        out_specs=[vmem()] * 2,
        out_shape=[
            jax.ShapeDtypeStruct((rows_all, width), bf16),
            jax.ShapeDtypeStruct((rows_all, LANE), f32),
        ],
        scratch_shapes=[pltpu.VMEM((cells, width + LANE), bf16)],
        compiler_params=params(18),
        cost_estimate=cost(5),
        name="hidden_stage",
    )(pre, stat, affine, rank, lib)


def decoder_back_kernel(
    total, latents, rank_ref, back_ref, exp_back_ref, scale_ref, pre_ref, stat_ref, affine_ref,
    decode_ref, latent_ref, batch_ref, loss_ref,
    pull_ref, sorted_ref, grad_ref,
):
    rows_all, width = back_ref.shape
    cells = pre_ref.shape[0]
    lines = cells // LANE
    fixed = -(-latents * lines // 8) * 8
    names = pull_ref.shape[0] - fixed - 24
    for i in range(rows_all // LANE):
        tile = pl.ds(i * LANE, LANE)
        scale = jnp.broadcast_to(scale_ref[i : i + 1, :], (LANE, LANE)).T
        sorted_ref[tile, :] = back_ref[tile, :] - exp_back_ref[tile, :] * scale
    block = 512
    unroll = 32

    def move(j, carry):
        base = pl.multiple_of(j * unroll, unroll)
        rows = [sorted_ref[pl.ds(rank_ref[base + u], 1), :] for u in range(unroll)]
        grad_ref[pl.ds(base, unroll), :] = jnp.concatenate(rows, axis=0)
        return carry

    lax.fori_loop(0, cells // unroll, move, 0)
    first = jnp.zeros((1, width), f32)
    second = jnp.zeros((1, width), f32)
    weight = jnp.zeros((16 + names, width), f32)
    for start, tall in cuts(cells, block):
        rows = pl.ds(start, tall)
        grad = grad_ref[rows, :]
        normed, inverse, gated, sigma = norm_parts(pre_ref[rows, :], stat_ref, affine_ref, total)
        inner = grad * sigma * (1.0 + gated * (1.0 - sigma))
        first = first + jnp.sum(inner, axis=0, keepdims=True)
        second = second + jnp.sum(inner * normed, axis=0, keepdims=True)
        pull = exact(decode_ref[...] * (inverse * affine_ref[0:1, :]), inner, by_last)
        for l in range(latents):
            for j in range(tall // LANE):
                at = l * lines + start // LANE + j
                pull_ref[at : at + 1, :] = pull[l : l + 1, j * LANE : (j + 1) * LANE]
        hot = (lax.broadcasted_iota(i32, (names, 1), 0) == batch_ref[:, rows]).astype(f32)
        side = jnp.concatenate([latent_ref[32:48, rows], hot], axis=0)
        weight = weight + exact(side, inner, plain)
    if fixed > latents * lines:
        pull_ref[latents * lines : fixed, :] = jnp.zeros((fixed - latents * lines, LANE), f32)
    loss = jnp.sum(loss_ref[...], axis=0, keepdims=True)
    row = lax.broadcasted_iota(i32, (8, LANE), 0)
    pull_ref[fixed : fixed + 8, :] = jnp.where(row == 2, loss, two_rows(first, second))
    pull_ref[fixed + 8 :, :] = weight


def decoder_back(
    total, latents, rank, back, exp_back, scale, pre, stat, affine, decode, latent, batch, loss, names
):
    rows_all, width = back.shape
    cells = pre.shape[0]
    return pl.pallas_call(
        lambda *refs: decoder_back_kernel(total, latents, *refs),
        in_specs=[smem()] + [vmem()] * 10,
        out_specs=vmem(),
        out_shape=jax.ShapeDtypeStruct(
            (-(-latents * (cells // LANE) // 8) * 8 + 24 + names, LANE), f32
        ),
        scratch_shapes=[pltpu.VMEM((rows_all, width), f32), pltpu.VMEM((cells, width), f32)],
        compiler_params=params(22),
        cost_estimate=cost(8),
        name="decoder_back",
    )(rank, back, exp_back, scale, pre, stat, affine, decode, latent, batch, loss)


def encoder_back_kernel(
    total, latents, pull_ref, inner_ref, pre_ref, stat_ref, affine_ref,
    x_ref, x_stat_ref, x_affine_ref, latent_ref, noise_ref, heads_ref, decode_ref,
    batch_ref, kl_ref,
    inner_out, sums_ref, pack_ref,
):
    cells, width = pre_ref.shape
    lines = cells // LANE
    fixed_rows = -(-latents * lines // 8) * 8
    names = pull_ref.shape[0] - fixed_rows - 24
    normed, inverse, _, _ = norm_parts(pre_ref[...], stat_ref, affine_ref, total)
    factor = inverse * affine_ref[0:1, :]
    shift_mean = inner_ref[0:1, :] * (1.0 / total)
    gain_mean = inner_ref[1:2, :] * (1.0 / total)
    decode = decode_ref[...] * factor
    fixed = jnp.sum(decode * shift_mean, axis=1, keepdims=True)
    moving = exact(decode * gain_mean, normed, by_last)
    pulls = []
    for l in range(latents):
        pieces = [pull_ref[l * lines + j : l * lines + j + 1, :] for j in range(lines)]
        pulls.append(jnp.concatenate(pieces, axis=1))
    pulls.append(jnp.zeros((16 - latents, cells), f32))
    pull = jnp.concatenate(pulls, axis=0) - fixed - moving
    mean, logvar = latent_ref[0:16, :], latent_ref[16:32, :]
    latent, scale = latent_ref[32:48, :], latent_ref[48:64, :]
    grad_mean = pull + mean
    grad_logvar = 0.5 * pull * noise_ref[...] * scale + 0.5 * (jnp.exp(logvar) - 1.0)
    grads = jnp.concatenate([grad_mean, grad_logvar], axis=0)
    grad_act = exact(grads, heads_ref[...], by_first)
    x_normed, _, gated, sigma = norm_parts(x_ref[...], x_stat_ref, x_affine_ref, total)
    inner = grad_act * sigma * (1.0 + gated * (1.0 - sigma))
    inner_out[...] = inner
    loss = jnp.sum(kl_ref[...], axis=0, keepdims=True) - pull_ref[fixed_rows + 2 : fixed_rows + 3, :]
    sums_ref[...] = two_rows(
        jnp.sum(inner, axis=0, keepdims=True), jnp.sum(inner * x_normed, axis=0, keepdims=True)
    ) + jnp.where(lax.broadcasted_iota(i32, (8, LANE), 0) == 2, loss, 0.0)
    side = jnp.concatenate([latent, batch_rows(batch_ref, names)], axis=0)
    side_sum = jnp.sum(side, axis=1, keepdims=True)
    fix = side_sum * shift_mean + exact(side, normed, plain) * gain_mean
    at = 16 + names
    pack_ref[:at, :] = factor * (pull_ref[fixed_rows + 8 :, :] - fix)
    pack_ref[at : at + 32, :] = exact(grads, gated * sigma, plain)
    pack_ref[at + 32 : at + 64, :] = jnp.broadcast_to(jnp.sum(grads, axis=1, keepdims=True), (32, LANE))


def encoder_back(
    total, latents, pull, inner, pre, stat, affine, x, x_stat, x_affine, latent, noise,
    heads, decode, batch, kl, names,
):
    cells, width = pre.shape
    return pl.pallas_call(
        lambda *refs: encoder_back_kernel(total, latents, *refs),
        in_specs=[vmem()] * 14,
        out_specs=[vmem()] * 3,
        out_shape=[
            jax.ShapeDtypeStruct((cells, width), f32),
            jax.ShapeDtypeStruct((8, width), f32),
            jax.ShapeDtypeStruct((names + 80, width), f32),
        ],
        compiler_params=params(22),
        cost_estimate=cost(3),
        name="encoder_back",
    )(pull, inner, pre, stat, affine, x, x_stat, x_affine, latent, noise, heads, decode, batch, kl)


def encoder_grad_kernel(
    total, block, inner_ref, x_ref, stat_ref, affine_ref, sums_ref, batch_ref, pack_ref, counts_hbm,
    out_ref, grad_ref, counts_ref, expr_ref, came,
):
    cells, genes = counts_ref.shape
    packed = pack_ref.shape[0]
    names = packed - 80
    columns = [pl.ds(i * block, block) for i in range(genes // block)]
    copies = [
        pltpu.make_async_copy(counts_hbm.at[:, at], counts_ref.at[:, at], came.at[i])
        for i, at in enumerate(columns)
    ]
    for copy in copies:
        copy.start()
    normed, inverse, _, _ = norm_parts(x_ref[...], stat_ref, affine_ref, total)
    factor = inverse * affine_ref[0:1, :]
    grad = factor * (
        inner_ref[...]
        - sums_ref[0:1, :] * (1.0 / total)
        - normed * (sums_ref[1:2, :] * (1.0 / total))
    )
    low = grad.astype(bf16)
    grad_ref[...] = low
    turned = low.astype(f32).T.astype(bf16)
    out_ref[genes : genes + packed, :] = pack_ref[...].astype(bf16)
    hot = batch_rows(batch_ref, names).astype(bf16)
    got = jnp.dot(hot, low, preferred_element_type=f32)
    out_ref[genes + packed : genes + packed + names, :] = got.astype(bf16)
    rest = out_ref.shape[0] - genes - packed - names
    if rest:
        out_ref[genes + packed + names :, :] = jnp.zeros((rest, out_ref.shape[1]), bf16)
    chunk = 256
    for i in range(len(columns) + 1):
        if i < len(columns):
            copies[i].wait()
        got = None
        for first in range(0, cells, chunk):
            rows = pl.ds(first, chunk)
            if i < len(columns):
                real = counts_ref[rows, columns[i]].astype(f32)
                expr_ref[i % 2, rows, :] = jnp.log(1.0 + real).astype(bf16)
            if i > 0:
                more = jnp.dot(
                    turned[:, first : first + chunk],
                    expr_ref[(i - 1) % 2, rows, :],
                    preferred_element_type=f32,
                )
                got = more if got is None else got + more
        if i > 0:
            out_ref[columns[i - 1], :] = got.T.astype(bf16)


def encoder_grad(total, inner, x, stat, affine, sums, batch, pack, counts, shares):
    cells, width = x.shape
    genes = counts.shape[1]
    block = 512 if genes % 512 == 0 else genes
    rows = genes + 2 * pack.shape[0] - 80
    rows = -(-rows // (ALIGN * shares)) * ALIGN * shares
    return pl.pallas_call(
        lambda *refs: encoder_grad_kernel(total, block, *refs),
        in_specs=[vmem()] * 7 + [anywhere()],
        out_specs=[vmem()] * 2,
        out_shape=[
            jax.ShapeDtypeStruct((rows, width), bf16),
            jax.ShapeDtypeStruct((cells, width), bf16),
        ],
        scratch_shapes=[
            pltpu.VMEM((cells, genes), i32),
            pltpu.VMEM((2, cells, block), bf16),
            pltpu.SemaphoreType.DMA((genes // block,)),
        ],
        compiler_params=params(48),
        cost_estimate=cost(7),
        name="encoder_grad",
    )(inner, x, stat, affine, sums, batch, pack, counts)


def input_grad_kernel(grad_ref, weight_ref, out_ref):
    out_ref[...] = lax.dot_general(
        grad_ref[...], weight_ref[...], by_last, preferred_element_type=f32
    )


def input_grad(grad, weight):
    cells, width = grad.shape
    genes = weight.shape[0]
    block = 256
    return pl.pallas_call(
        input_grad_kernel,
        grid=(cells // block,),
        in_specs=[
            pl.BlockSpec((block, width), lambda i: (i, 0)),
            pl.BlockSpec((genes, width), lambda i: (0, 0)),
        ],
        out_specs=pl.BlockSpec((block, genes), lambda i: (i, 0)),
        out_shape=jax.ShapeDtypeStruct((cells, genes), f32),
        compiler_params=params(14),
        cost_estimate=cost(9),
        name="input_grad",
    )(grad, weight)


def body(
    counts,
    batch_ids,
    dataset_ids,
    variable_mask,
    latent_noise,
    encoder_weight,
    encoder_batch,
    encoder_gain,
    encoder_shift,
    mean_weight,
    mean_bias,
    logvar_weight,
    logvar_bias,
    decoder_latent,
    decoder_batch,
    decoder_gain,
    decoder_shift,
    scale_weight,
    scale_bias,
    dropout_weight,
    dropout_bias,
    log_theta,
):
    cells, genes = counts.shape
    groups = variable_mask.shape[0]
    width = encoder_weight.shape[1]
    latents = mean_weight.shape[1]
    names = encoder_batch.shape[0]
    total_cells = cells * lax.axis_size("cells")
    gene_parts = lax.axis_size("genes")
    inverse_cells = 1.0 / total_cells
    pieces = 4 if genes % (4 * LANE) == 0 else 1
    rows_all = -(-(cells + groups * ALIGN) // LANE) * LANE

    partial_pre, lib_lanes = encode(counts, encoder_weight)
    pre_pieces = rows_pieces(partial_pre, WIRE)

    pos, rank, meta = order_cells(variable_mask, dataset_ids)
    extra = [*split3(scale_bias), *split3(0.5 * dropout_bias), *split3(log_theta)]
    extra = jnp.concatenate([jnp.stack(extra), jnp.zeros((16 - len(extra), genes), bf16)])
    batch_row = batch_ids.reshape(1, cells)
    batch_hot = (batch_ids[:, None] == jnp.arange(names)[None, :]).astype(f32)
    encoder_add = jnp.dot(batch_hot, encoder_batch, precision=highest)
    decoder_add = jnp.dot(batch_hot, decoder_batch, precision=highest)
    pad_rows = lambda v, n=16: jnp.pad(v, ((0, n - v.shape[0]), (0, 0)))
    noise = pad_rows(latent_noise.T)
    heads = jnp.concatenate([pad_rows(mean_weight.T), pad_rows(logvar_weight.T)])
    head_bias = jnp.concatenate([pad_rows(mean_bias[:, None]), pad_rows(logvar_bias[:, None])])
    head_bias = jnp.broadcast_to(head_bias, (32, LANE))
    decode = pad_rows(decoder_latent)
    encoder_affine = pad_rows(jnp.stack([encoder_gain, encoder_shift]), 8)
    decoder_affine = pad_rows(jnp.stack([decoder_gain, decoder_shift]), 8)

    def own_genes(members, rows, before):
        return compact(
            members, meta, rows, pos, scale_weight, dropout_weight, extra, genes, pieces, before
        )

    batches = [[d for d in range(groups) if d * 8 // groups in some] for some in ((0, 1, 2), (3, 4), (5, 6), (7,))]

    pre_pieces, rank = after(pre_pieces, rank)
    pre_parts = exchange(pre_pieces, "genes", 2)
    sorted_rows = sort_rows(rank.reshape(cells), counts, pieces, rows_all)
    pre_parts, sorted_rows = after(pre_parts, sorted_rows)
    pre_own, sorted_rows = after(join(pre_parts, WIRE), sorted_rows)
    pre_blocks = spread_out(pre_own, "genes", 2)
    ycw = own_genes(batches[0], sorted_rows, None)
    pre_blocks, ycw = after(pre_blocks, ycw)
    x = rows_whole(assemble(pre_blocks, "genes", 0, 2)) + encoder_add
    x_sums = pad_rows(jnp.stack([jnp.sum(x, axis=0), jnp.sum(x * x, axis=0)]), 8)
    x_sums, sorted_rows = after(x_sums, sorted_rows)
    x_stat = total_direct(x_sums, "cells")
    ycw = own_genes(batches[1], sorted_rows, ycw)
    x_stat, ycw = after(x_stat, ycw)
    pre, sums, latent, kl_lanes = latent_stage(
        total_cells, x, x_stat, encoder_affine, heads, head_bias, noise, decode, decoder_add
    )
    sums, sorted_rows = after(sums, sorted_rows)
    stat = total_direct(sums, "cells")
    ycw = own_genes(batches[2], sorted_rows, ycw)
    stat, ycw = after(stat, ycw)
    hidden, lib_sorted = hidden_stage(
        total_cells, pre, stat, decoder_affine, rank, lib_lanes, rows_all
    )

    own, own_top, exp_back = softmax_part(hidden, lib_sorted, scale_weight, scale_bias.reshape(1, genes))
    own, sorted_rows = after(own, sorted_rows)
    pair = jnp.stack([own, swap(own, "genes", 1)])
    pair, sorted_rows = after(pair, sorted_rows)
    gathered = [pair] + [swap(pair, "genes", 2 * s) for s in range(1, gene_parts // 2)]
    ycw = own_genes(batches[3], sorted_rows, ycw)
    gathered, ycw = after(gathered, ycw)
    tops = [g[i, 0] for g in gathered for i in range(2)]
    top = tops[0]
    for t in tops[1:]:
        top = jnp.maximum(top, t)
    exp_total = tree_sum(
        [g[0, 1] * jnp.exp(g[0, 0] - top) + g[1, 1] * jnp.exp(g[1, 0] - top) for g in gathered]
    )
    exp_total = jnp.maximum(exp_total, 1e-30)
    library = tree_sum([g[0, 2] + g[1, 2] for g in gathered])
    own_scale = jnp.exp(own[0] - top) / exp_total
    shift = jnp.where(
        library > 0.0,
        jnp.log(jnp.maximum(library, 1.0)) - jnp.log(exp_total) - top,
        -1e30,
    )
    shift = jnp.broadcast_to(shift.reshape(-1)[:rows_all, None], (rows_all, LANE))
    back, inner_rows, loss_lanes, g = likelihood(meta, hidden, shift, *ycw)
    inner_rows = inner_rows + swap(inner_rows, "genes", 1)
    inner_rows, g = after(inner_rows, g)
    inner_total = total_direct(inner_rows, "genes", 2)
    dropout_spread = expand(meta, g, pos, genes, 1)
    inner_total, dropout_spread = after(inner_total, dropout_spread)
    row_scale = inner_total * own_scale
    dropout_pieces = pieces_for(dropout_spread, "cells", 1, bf16)
    dropout_pieces, row_scale = after(dropout_pieces, row_scale)
    dropout_parts = exchange(dropout_pieces, "cells")
    pull = decoder_back(
        total_cells, latents, rank.reshape(cells), back, exp_back, row_scale, pre, stat, decoder_affine,
        decode, latent, batch_row, loss_lanes, names,
    )
    row_flat = row_scale.reshape(1, -1)[:, :rows_all]
    row_scaled = jnp.concatenate(
        [
            (hidden.T.astype(f32) * row_flat).astype(bf16),
            row_flat.astype(bf16),
            jnp.zeros((7, rows_all), bf16),
        ]
    )
    pull = pull + swap(pull, "genes", 1)
    pull, row_scaled = after(pull, row_scaled)
    pull = total_direct(pull, "genes", 2)
    row_scaled, dropout_parts = after(row_scaled, dropout_parts)
    dropout_own, row_scaled = after(join(dropout_parts, bf16), row_scaled)
    scale_spread = expand(
        meta, g, pos, genes, 0, row_scaled, hidden, own_top, scale_weight, scale_bias.reshape(1, genes)
    )
    dropout_blocks = spread_out(dropout_own, "cells")
    pull, scale_spread = after(pull, scale_spread)
    sums_at = -(-latents * (cells // LANE) // 8) * 8
    decoder_sums = total_direct(pull[sums_at : sums_at + 8], "cells")
    decoder_sums, dropout_blocks = after(decoder_sums, dropout_blocks)
    inner, sums, pack = encoder_back(
        total_cells, latents, pull, decoder_sums, pre, stat, decoder_affine,
        x, x_stat, encoder_affine, latent, noise, heads, decode, batch_row, kl_lanes, names,
    )
    sums = total_direct(sums, "cells")
    scale_pieces = pieces_for(scale_spread, "cells", 1, bf16)
    scale_pieces, sums = after(scale_pieces, sums)
    scale_parts = exchange(scale_pieces, "cells")
    encoder_weight_grad, grad_pre_low = encoder_grad(
        total_cells, inner, x, x_stat, encoder_affine, sums, batch_row, pack, counts,
        lax.axis_size("cells"),
    )
    encoder_weight_grad, scale_parts = after(encoder_weight_grad, scale_parts)
    encoder_pieces = pieces_for(encoder_weight_grad, "cells", 0, bf16)
    encoder_pieces, grad_pre_low = after(encoder_pieces, grad_pre_low)
    encoder_parts = exchange(encoder_pieces, "cells")
    input_gradient = input_grad(grad_pre_low, encoder_weight)
    encoder_parts, input_gradient, scale_parts = after(encoder_parts, input_gradient, scale_parts)
    encoder_blocks = spread_out(join(encoder_parts, bf16), "cells")
    scale_blocks = spread_out(join(scale_parts, bf16), "cells")
    dropout_spread = assemble(dropout_blocks, "cells", 1).astype(f32)
    scale_spread = assemble(scale_blocks, "cells", 1).astype(f32)
    encoder_total = assemble(encoder_blocks, "cells", 0).astype(f32) * inverse_cells
    pack = encoder_total[genes:]

    scale_total = scale_spread[:width] * inverse_cells
    dropout_total = dropout_spread[:width] * (0.5 * inverse_cells)
    scale_bias_total = scale_spread[width] * inverse_cells
    dropout_bias_total = dropout_spread[width] * (0.5 * inverse_cells)
    theta_total = -jnp.exp(log_theta) * dropout_spread[width + 1] * inverse_cells
    at = 16 + names
    mean_loss = jnp.sum(sums[2]) * inverse_cells
    return (
        mean_loss,
        input_gradient,
        encoder_total[:genes],
        pack[at + 64 : at + 64 + names],
        sums[1] * inverse_cells,
        sums[0] * inverse_cells,
        pack[at : at + latents].T,
        pack[at + 32 : at + 32 + latents, 0],
        pack[at + 16 : at + 16 + latents].T,
        pack[at + 48 : at + 48 + latents, 0],
        pack[:latents],
        pack[16 : 16 + names],
        decoder_sums[1] * inverse_cells,
        decoder_sums[0] * inverse_cells,
        scale_total,
        scale_bias_total,
        dropout_total,
        dropout_bias_total,
        theta_total,
    )


def solution(mesh):
    return jax.shard_map(
        body,
        mesh=mesh,
        in_specs=(
            P("cells", "genes"),
            P("cells"),
            P("cells"),
            P(None, "genes"),
            P("cells", None),
            P("genes", None),
            P(),
            P(),
            P(),
            P(),
            P(),
            P(),
            P(),
            P(),
            P(),
            P(),
            P(),
            P(None, "genes"),
            P("genes"),
            P(None, "genes"),
            P("genes"),
            P("genes"),
        ),
        out_specs=(
            P(),
            P("cells", "genes"),
            P("genes", None),
            P(),
            P(),
            P(),
            P(),
            P(),
            P(),
            P(),
            P(),
            P(),
            P(),
            P(),
            P(None, "genes"),
            P("genes"),
            P(None, "genes"),
            P("genes"),
            P("genes"),
        ),
        check_vma=False,
    )
```

```python
import jax
import jax.numpy as jnp
from jax import lax
from jax.experimental import pallas as pl
from jax.experimental.pallas import tpu as pltpu
from jax.sharding import PartitionSpec as P

highest = lax.Precision.HIGHEST
norm_eps = 0.001
log_eps = 1e-08
f32 = jnp.float32
bf16 = jnp.bfloat16
i32 = jnp.int32
LANE = 128
ALIGN = 16
CAP = 384
RB = 320
TOP = 24
WIRE = bf16
VMEM_MB = 1 << 20
by_last = (((1,), (1,)), ((), ()))
by_first = (((0,), (0,)), ((), ()))


def cuts(total, width):
    return [(i, min(width, total - i)) for i in range(0, total, width)]


def fit(v, width=LANE):
    return v if v.shape[1] == width else jnp.pad(v, ((0, 0), (0, width - v.shape[1])))


def vmem():
    return pl.BlockSpec(memory_space=pltpu.VMEM)


def smem():
    return pl.BlockSpec(memory_space=pltpu.SMEM)


def anywhere():
    return pl.BlockSpec(memory_space=pl.ANY)


def params(mib):
    return pltpu.CompilerParams(vmem_limit_bytes=mib * VMEM_MB)


def cost(micros):
    return pl.CostEstimate(
        flops=int(micros * 1.1e9), bytes_accessed=int(micros * 3.6e6), transcendentals=0
    )


def split3(v):
    high = lax.reduce_precision(v, 8, 7)
    rest = v - high
    middle = lax.reduce_precision(rest, 8, 7)
    return high.astype(bf16), middle.astype(bf16), (rest - middle).astype(bf16)


def swap(v, axis, bits):
    n = lax.axis_size(axis)
    return lax.ppermute(v, axis, [(i, i ^ bits) for i in range(n)])


def tree_sum(parts):
    while len(parts) > 1:
        parts = [parts[i] + parts[i + 1] for i in range(0, len(parts), 2)]
    return parts[0]


def total_direct(v, axis, unit=1):
    n = lax.axis_size(axis)
    return tree_sum([v] + [swap(v, axis, s) for s in range(unit, n, unit)])


def total_genes(v):
    return total_direct(v + swap(v, "genes", 1), "genes", 2)


def piece_of(v, i, size, axis):
    return lax.dynamic_slice_in_dim(v, i * size, size, axis)


def pieces_for(v, axis, dim, wire, unit=1):
    groups = lax.axis_size(axis) // unit
    spot = lax.axis_index(axis) // unit
    size = v.shape[dim] // groups
    low = v.astype(wire)
    own = piece_of(v, spot, size, dim).astype(f32)
    return [own] + [piece_of(low, spot ^ s, size, dim) for s in range(1, groups)]


def exchange(pieces, axis, unit=1):
    return pieces[:1] + [swap(piece, axis, unit * s) for s, piece in enumerate(pieces) if s]


def axis_scatter(v, axis, dim, wire, unit=1):
    return exchange(pieces_for(v, axis, dim, wire, unit), axis, unit)


def join(parts, wire):
    return tree_sum([part.astype(f32) for part in parts]).astype(wire)


def spread_out(own, axis, unit=1):
    groups = lax.axis_size(axis) // unit
    return [own] + [swap(own, axis, unit * s) for s in range(1, groups)]


def assemble(pieces, axis, dim, unit=1):
    spot = lax.axis_index(axis) // unit
    size = pieces[0].shape[dim]
    shape = list(pieces[0].shape)
    shape[dim] = size * len(pieces)
    whole = jnp.zeros(shape, pieces[0].dtype)
    for s, piece in enumerate(pieces):
        whole = lax.dynamic_update_slice_in_dim(whole, piece, (spot ^ s) * size, dim)
    return whole


def rows_pieces(v, wire):
    core = lax.axis_index("genes") % 2
    half = v.shape[0] // 2
    mine = piece_of(v, core, half, 0)
    other = piece_of(v, 1 - core, half, 0)
    summed = mine + swap(other.astype(wire), "genes", 1).astype(f32)
    return pieces_for(summed, "genes", 0, wire, 2)


def rows_whole(block):
    core = lax.axis_index("genes") % 2
    far = swap(block, "genes", 1)
    first = jnp.where(core == 0, block, far)
    second = jnp.where(core == 0, far, block)
    return jnp.concatenate([first, second], axis=0).astype(f32)


def after(value, *earlier):
    return lax.optimization_barrier((value, *earlier))


def arriving(source, target, arrived, blocks):
    block = target.shape[0] // blocks
    rows = [pl.ds(i * block, block) for i in range(blocks)]
    copies = [
        pltpu.make_async_copy(source.at[rows[i], :], target.at[rows[i], :], arrived.at[i])
        for i in range(blocks)
    ]
    for copy in copies:
        copy.start()
    return rows, copies


def encode_kernel(blocks, counts_hbm, weight_ref, part_ref, lib_ref, counts_ref, arrived):
    cells, genes = counts_ref.shape
    block = cells // blocks
    rows, copies = arriving(counts_hbm, counts_ref, arrived, blocks)
    for i in range(blocks):
        copies[i].wait()
        lib = jnp.zeros((block, LANE), f32)
        part = jnp.zeros((block, part_ref.shape[1]), f32)
        for start, width in cuts(genes, 2 * LANE):
            at = pl.ds(start, width)
            real = counts_ref[rows[i], at].astype(f32)
            expr = jnp.log(1.0 + real).astype(bf16)
            part = part + jnp.dot(expr, weight_ref[at, :], preferred_element_type=f32)
            for first, wide in cuts(width, LANE):
                lib = lib + fit(real[:, first : first + wide])
        part_ref[rows[i], :] = part
        lib_ref[rows[i], :] = lib


def encode(counts, weight):
    cells, genes = counts.shape
    hidden = weight.shape[1]
    blocks = 8
    return pl.pallas_call(
        lambda *refs: encode_kernel(blocks, *refs),
        in_specs=[anywhere(), vmem()],
        out_specs=[vmem(), vmem()],
        out_shape=[
            jax.ShapeDtypeStruct((cells, hidden), f32),
            jax.ShapeDtypeStruct((cells, LANE), f32),
        ],
        scratch_shapes=[pltpu.VMEM((cells, genes), i32), pltpu.SemaphoreType.DMA((blocks,))],
        compiler_params=params(32),
        cost_estimate=cost(8),
        name="encode",
    )(counts, weight)


def order_kernel(mask_ref, data_ref, pos_ref, rank_ref, meta_ref):
    groups, genes = mask_ref.shape
    cells = data_ref.shape[1]
    row = lax.broadcasted_iota(i32, (LANE, LANE), 0)
    col = lax.broadcasted_iota(i32, (LANE, LANE), 1)
    upto = (row <= col).astype(bf16)
    group = lax.broadcasted_iota(i32, (groups, LANE), 0)

    def running(hot, so_far, width):
        inside = jnp.dot(hot.astype(bf16), upto[:width, :width], preferred_element_type=f32)
        return so_far + inside, so_far + jnp.sum(hot, axis=1, keepdims=True)

    so_far = jnp.zeros((groups, 1), f32)
    for start, width in cuts(genes, LANE):
        hot = mask_ref[:, pl.ds(start, width)].astype(f32)
        count, so_far = running(hot, so_far, width)
        place = jnp.where(hot > 0.5, count - 1.0, -1.0).astype(i32)
        if width < LANE:
            place = jnp.pad(place, ((0, 0), (0, LANE - width)), constant_values=-1)
        pos_ref[:, pl.ds(start, LANE)] = place
    gene_count = so_far

    so_far = jnp.zeros((groups, 1), f32)
    kept = []
    for start, width in cuts(cells, LANE):
        data = data_ref[:, pl.ds(start, width)]
        hot = (group[:, :width] == data).astype(f32)
        count, so_far = running(hot, so_far, width)
        kept.append((start, width, hot, count))
    cell_count = so_far
    padded = jnp.floor((cell_count + (ALIGN - 1)) * (1.0 / ALIGN))
    before = lax.broadcasted_iota(i32, (groups, groups), 1) < lax.broadcasted_iota(
        i32, (groups, groups), 0
    )
    spread = jnp.broadcast_to(padded, (groups, LANE))
    begin = ALIGN * jnp.dot(
        before.astype(f32), spread, precision=highest, preferred_element_type=f32
    )
    for start, width, hot, count in kept:
        place = hot * (begin[:, :width] + count - 1.0)
        rank_ref[:, pl.ds(start, width)] = jnp.sum(place, axis=0, keepdims=True).astype(i32)
    lane = lax.broadcasted_iota(i32, (groups, LANE), 1)
    meta = jnp.where(lane == 0, cell_count, jnp.where(lane == 1, begin, gene_count))
    meta_ref[...] = meta.astype(i32)


def order_cells(mask, data):
    groups, genes = mask.shape
    cells = data.shape[0]
    pos, rank, meta = pl.pallas_call(
        order_kernel,
        in_specs=[vmem(), vmem()],
        out_specs=[vmem(), vmem(), vmem()],
        out_shape=[
            jax.ShapeDtypeStruct((groups, -(-genes // LANE) * LANE), i32),
            jax.ShapeDtypeStruct((1, cells), i32),
            jax.ShapeDtypeStruct((groups, LANE), i32),
        ],
        cost_estimate=cost(2),
        name="order_cells",
    )(mask, data.reshape(1, cells))
    return pos, rank, meta[:, :3].reshape(-1)


def pass_count(meta_ref, groups):
    most = meta_ref[2]
    for d in range(1, groups):
        most = jnp.maximum(most, meta_ref[3 * d + 2])
    return jnp.maximum((most + CAP - 1) // CAP, 1)


def chunk_of(meta_ref, d, i, rows_all):
    count = meta_ref[3 * d]
    begin = meta_ref[3 * d + 1]
    low = begin + i * RB
    first = pl.multiple_of(jnp.minimum(low, rows_all - RB), ALIGN)
    return first, low, begin + count


def pack_width(genes, pieces):
    return -(-genes // pieces // LANE) * LANE


def sort_kernel(
    blocks, pieces, rank_ref, counts_hbm, sorted_hbm, counts_ref, pack_ref, sorted_ref, came, gone
):
    cells, genes = counts_ref.shape
    rows_all = sorted_ref.shape[0]
    block = cells // blocks
    unroll = 32
    rows, copies = arriving(counts_hbm, counts_ref, came, blocks)
    for i in range(blocks):
        copies[i].wait()
        for start, width in cuts(genes // pieces, LANE):
            packed = None
            for piece in range(pieces):
                one = counts_ref[rows[i], pl.ds(pieces * start + piece * width, width)]
                packed = one if piece == 0 else packed | (one << (8 * piece))
            pack_ref[:, pl.ds(start, width)] = packed

        def move(j, carry):
            base = pl.multiple_of(j * unroll, unroll)
            tile = pack_ref[pl.ds(base, unroll), :]
            for u in range(unroll):
                sorted_ref[pl.ds(rank_ref[i * block + base + u], 1), :] = tile[u : u + 1, :]
            return carry

        lax.fori_loop(0, block // unroll, move, 0)
    copy = pltpu.make_async_copy(sorted_ref, sorted_hbm.at[pl.ds(0, rows_all), :], gone)
    copy.start()
    copy.wait()


def sort_rows(rank, counts, pieces, rows_all):
    cells, genes = counts.shape
    narrow = pack_width(genes, pieces)
    blocks = 8
    return pl.pallas_call(
        lambda *refs: sort_kernel(blocks, pieces, *refs),
        in_specs=[smem(), anywhere()],
        out_specs=anywhere(),
        out_shape=jax.ShapeDtypeStruct((rows_all + RB, narrow), i32),
        scratch_shapes=[
            pltpu.VMEM((cells, genes), i32),
            pltpu.VMEM((cells // blocks, narrow), i32),
            pltpu.VMEM((rows_all, narrow), i32),
            pltpu.SemaphoreType.DMA((blocks,)),
            pltpu.SemaphoreType.DMA,
        ],
        compiler_params=params(58),
        cost_estimate=cost(11),
        name="sort_rows",
    )(rank, counts)


def compact_kernel(
    pieces, genes, members, first_call, meta_ref, sorted_hbm, pos_ref, scale_ref, dropout_ref,
    extra_ref, *rest,
):
    if not first_call:
        rest = rest[3:]
    y_hbm, w_hbm, c_hbm, rows_ref, stack_ref, pick_ref, found_ref, table_ref, y_ref, w_ref, c_ref, came, gone = rest
    width = w_ref.shape[1]
    both = 2 * width
    quarter = genes // pieces
    groups = pos_ref.shape[0]
    stack_ref[RB : RB + both // 2, :] = scale_ref[...]
    stack_ref[RB + both // 2 : RB + both, :] = dropout_ref[...] * jnp.asarray(0.5, bf16)
    stack_ref[RB + both :, :] = extra_ref[...]

    def rows_of(d, i):
        low = pl.multiple_of(meta_ref[3 * d + 1] + i * RB, ALIGN)
        return low, meta_ref[3 * d + 1] + meta_ref[3 * d]

    def bring(n, d, i):
        low, _ = rows_of(d, i)
        return pltpu.make_async_copy(sorted_hbm.at[pl.ds(low, RB), :], rows_ref.at[n], came.at[n])

    def widen(n):
        for start, wide in cuts(quarter, LANE):
            raw = rows_ref[n, :, pl.ds(start, wide)]
            for piece in range(pieces):
                part = raw if pieces == 1 else (raw >> (8 * piece)) & 255
                stack_ref[:RB, pl.ds(pieces * start + piece * wide, wide)] = part.astype(f32).astype(bf16)

    def look(n, d, i, k, sums):
        low, high = rows_of(d, i)

        def step(j, sums):
            gamma_in, digamma_in = sums
            src = pl.ds(pl.multiple_of(j * 16, 16), 16)
            row = lax.broadcasted_iota(i32, (16, CAP), 0) + (low + j * 16)
            col = lax.broadcasted_iota(i32, (16, CAP), 1) + k * CAP
            own = (row < high) & (col < meta_ref[3 * d + 2])
            value = jnp.where(own, found_ref[src, :], -1.0)
            y_ref[n, src, :] = value.astype(bf16)
            index = jnp.maximum(value, 0.0).astype(i32)
            for h in (0, 8):
                here = index[h : h + 8]
                inner = here & 7
                got = []
                for base in (0, TOP):
                    g0 = jnp.take_along_axis(table_ref[base : base + 8, :], inner, axis=0)
                    g1 = jnp.take_along_axis(table_ref[base + 8 : base + 16, :], inner, axis=0)
                    g2 = jnp.take_along_axis(table_ref[base + 16 : base + 24, :], inner, axis=0)
                    got.append(jnp.where(here < 8, g0, jnp.where(here < 16, g1, g2)))
                gamma_in = gamma_in + got[0]
                digamma_in = digamma_in + got[1]
            return gamma_in, digamma_in

        return lax.fori_loop(0, RB // 16, step, sums, unroll=2)

    def leave(n, d, i, k):
        low, _ = rows_of(d, i)
        return pltpu.make_async_copy(y_ref.at[n], y_hbm.at[k, pl.ds(low, RB), :], gone.at[3 * n])

    def one_pass(k, carry):
        for n, d in enumerate(members):
            bring(n, d, 0).start()
        pending = []
        for n, d in enumerate(members):
            column = lax.broadcasted_iota(i32, (CAP, 1), 0) + k * CAP
            for start, wide in cuts(genes, 2 * LANE):
                place = pos_ref[d : d + 1, pl.ds(start, -(-wide // LANE) * LANE)]
                pick = (column == place).astype(f32).astype(bf16)
                pick_ref[:, pl.ds(start, wide)] = pick[:, :wide]
            bring(n, d, 0).wait()
            widen(n)
            found_ref[...] = lax.dot_general(
                stack_ref[...], pick_ref[...], by_last, preferred_element_type=f32
            )
            w_ref[n, :, :CAP] = found_ref[RB : RB + width, :].astype(bf16)
            w_ref[n, :, CAP:] = found_ref[RB + width : RB + both, :].astype(bf16)
            side = [found_ref[RB + both + j : RB + both + j + 1, :] for j in range(9)]
            scale_bias = side[0] + side[1] + side[2]
            dropout_bias = side[3] + side[4] + side[5]
            log_theta = side[6] + side[7] + side[8]
            used = lax.broadcasted_iota(i32, (1, CAP), 1) + k * CAP < meta_ref[3 * d + 2]
            scale_bias = jnp.where(used, scale_bias, -1e30)
            theta = jnp.exp(log_theta)
            gamma_sum = jnp.zeros((1, CAP), f32)
            digamma_sum = jnp.zeros((1, CAP), f32)
            table_ref[...] = jnp.zeros_like(table_ref)
            for x in range(1, TOP):
                base = theta + float(x - 1)
                gamma_sum = gamma_sum + jnp.log(base * (1.0 / x))
                digamma_sum = digamma_sum + 1.0 / base
                table_ref[x : x + 1, :] = gamma_sum
                table_ref[TOP + x : TOP + x + 1, :] = digamma_sum
            zero = jnp.zeros((8, CAP), f32)
            sums = look(n, d, 0, k, (zero, zero))
            if pending:
                pending[-1].wait()
                pending.pop()
            last = leave(n, d, 0, k)
            last.start()

            def more(i, sums):
                leave(n, d, i - 1, k).wait()
                bring(n, d, i).start()
                bring(n, d, i).wait()
                widen(n)
                found_ref[:RB, :] = lax.dot_general(
                    stack_ref[:RB, :], pick_ref[...], by_last, preferred_element_type=f32
                )
                sums = look(n, d, i, k, sums)
                leave(n, d, i, k).start()
                return sums

            chunks = (meta_ref[3 * d] + RB - 1) // RB
            gammas, digammas = lax.fori_loop(1, chunks, more, sums)
            pending.append(last)
            c_ref[n] = jnp.zeros((8, CAP), f32)
            c_ref[n, 0:1, :] = scale_bias
            c_ref[n, 1:2, :] = dropout_bias
            c_ref[n, 2:3, :] = theta
            c_ref[n, 5:6, :] = theta + log_eps
            c_ref[n, 6:7, :] = jnp.log(theta + log_eps)
            c_ref[n, 7:8, :] = theta / (theta + log_eps)
            c_ref[n, 3:4, :] = jnp.sum(gammas, axis=0, keepdims=True)
            c_ref[n, 4:5, :] = jnp.sum(digammas, axis=0, keepdims=True)
            for copy in sides(n, d, k):
                copy.start()
        pending.pop().wait()
        for n, d in enumerate(members):
            for copy in sides(n, d, k):
                copy.wait()
        return carry

    def sides(n, d, k):
        return [
            pltpu.make_async_copy(w_ref.at[n], w_hbm.at[k, d], gone.at[3 * n + 1]),
            pltpu.make_async_copy(c_ref.at[n], c_hbm.at[k, d], gone.at[3 * n + 2]),
        ]

    lax.fori_loop(0, pass_count(meta_ref, groups), one_pass, 0)


def compact(members, meta, sorted_rows, pos, scale_weight, dropout_weight, extra, genes, pieces, before):
    groups = pos.shape[0]
    tall, narrow = sorted_rows.shape
    passes = -(-genes // CAP)
    both = 2 * scale_weight.shape[0]
    count = len(members)
    first_call = before is None
    return pl.pallas_call(
        lambda *refs: compact_kernel(pieces, genes, members, first_call, *refs),
        in_specs=[smem(), anywhere(), vmem(), vmem(), vmem(), vmem()]
        + ([] if first_call else [anywhere()] * 3),
        out_specs=[anywhere()] * 3,
        out_shape=[
            jax.ShapeDtypeStruct((passes, tall, CAP), bf16),
            jax.ShapeDtypeStruct((passes, groups, both // 2, 2 * CAP), bf16),
            jax.ShapeDtypeStruct((passes, groups, 8, CAP), f32),
        ],
        input_output_aliases={} if first_call else {6: 0, 7: 1, 8: 2},
        scratch_shapes=[
            pltpu.VMEM((count, RB, narrow), i32),
            pltpu.VMEM((RB + both + 16, genes), bf16),
            pltpu.VMEM((CAP, genes), bf16),
            pltpu.VMEM((RB + both + 16, CAP), f32),
            pltpu.VMEM((2 * TOP, CAP), f32),
            pltpu.VMEM((count, RB, CAP), bf16),
            pltpu.VMEM((count, both // 2, 2 * CAP), bf16),
            pltpu.VMEM((count, 8, CAP), f32),
            pltpu.SemaphoreType.DMA((count,)),
            pltpu.SemaphoreType.DMA((3 * count,)),
        ],
        compiler_params=params(58),
        cost_estimate=cost(4 * count),
        name="compact",
    )(meta, sorted_rows, pos, scale_weight, dropout_weight, extra, *(before or ()))


def softmax_kernel(
    hidden_ref, lib_ref, weight_ref, bias_ref, stat_ref, back_ref,
    even_ref, odd_ref, even_top_ref, odd_top_ref, column_ref,
):
    rows, genes = even_ref.shape
    blocks = back_ref.shape[0] // rows
    columns = cuts(genes, 2 * LANE)

    def place(i):
        return pl.ds(pl.multiple_of(i * rows, ALIGN), rows)

    def logits(i, c, logit_ref, top_ref):
        start, width = columns[c]
        at = pl.ds(start, width)
        logit = (
            jnp.dot(hidden_ref[place(i), :], weight_ref[:, at], preferred_element_type=f32)
            + bias_ref[:, at]
        )
        logit_ref[:, at] = logit
        top = None if c == 0 else top_ref[...]
        for first, wide in cuts(width, LANE):
            piece = logit[:, first : first + wide]
            if wide < LANE:
                piece = jnp.broadcast_to(jnp.max(piece, axis=1, keepdims=True), (rows, LANE))
            top = piece if top is None else jnp.maximum(top, piece)
        top_ref[...] = top

    def one(i, logit_ref, top_ref, next_ref, next_top_ref):
        here = place(i)
        after_this = jnp.minimum(i + 1, blocks - 1)
        top = jnp.max(top_ref[...], axis=1, keepdims=True)
        total = jnp.zeros((rows, LANE), f32)
        for c, (start, width) in enumerate(columns):
            logits(after_this, c, next_ref, next_top_ref)
            at = pl.ds(start, width)
            value = jnp.exp(logit_ref[:, at] - top)
            for first, wide in cuts(width, LANE):
                total = total + fit(value[:, first : first + wide])
            back = lax.dot_general(
                value.astype(bf16), weight_ref[:, at], by_last, preferred_element_type=f32
            )
            if c == 0:
                back_ref[here, :] = back
            else:
                back_ref[here, :] += back
        total = jnp.sum(total, axis=1, keepdims=True)
        lane = lax.broadcasted_iota(i32, (rows, LANE), 1)
        column_ref[here, :] = jnp.where(lane == 0, top, jnp.where(lane == 1, total, lib_ref[here, :]))

    for c in range(len(columns)):
        logits(0, c, even_ref, even_top_ref)

    def pair(j, carry):
        one(2 * j, even_ref, even_top_ref, odd_ref, odd_top_ref)
        one(2 * j + 1, odd_ref, odd_top_ref, even_ref, even_top_ref)
        return carry

    lax.fori_loop(0, blocks // 2, pair, 0)
    stat_ref[...] = jnp.zeros_like(stat_ref)
    for i in range(column_ref.shape[0] // LANE):
        tile = column_ref[i * LANE : (i + 1) * LANE, :].T
        for j in range(3):
            stat_ref[j, i : i + 1, :] = tile[j : j + 1, :]


def row_block(rows_all):
    return rows_all // 8 if rows_all % 128 == 0 else rows_all


def softmax_part(hidden, lib, weight, bias):
    rows_all, width = hidden.shape
    genes = weight.shape[1]
    block = row_block(rows_all)
    tall = -(-rows_all // LANE // 8) * 8
    return pl.pallas_call(
        softmax_kernel,
        in_specs=[vmem()] * 4,
        out_specs=[vmem()] * 2,
        out_shape=[
            jax.ShapeDtypeStruct((3, tall, LANE), f32),
            jax.ShapeDtypeStruct((rows_all, width), f32),
        ],
        scratch_shapes=[
            pltpu.VMEM((block, genes), f32),
            pltpu.VMEM((block, genes), f32),
            pltpu.VMEM((block, LANE), f32),
            pltpu.VMEM((block, LANE), f32),
            pltpu.VMEM((rows_all, LANE), f32),
        ],
        compiler_params=params(24),
        cost_estimate=cost(10),
        name="softmax_part",
    )(hidden, lib, weight, bias)


def likelihood_kernel(
    meta_ref, hidden_ref, line_ref, y_hbm, w_hbm, c_hbm,
    back_ref, inner_ref, loss_ref, g_hbm,
    shift_ref, row_sum_ref, y_ref, w_ref, c_ref, logit_ref, grad_ref, g_ref, came, gone,
):
    rows_all, width = hidden_ref.shape
    groups = w_ref.shape[0]
    both = 2 * width
    step = 32
    for i in range(rows_all // LANE):
        line = jnp.broadcast_to(line_ref[i : i + 1, :], (LANE, LANE))
        shift_ref[i * LANE : (i + 1) * LANE, :] = line.T
    back_ref[...] = jnp.zeros_like(back_ref)
    row_sum_ref[...] = jnp.zeros_like(row_sum_ref)
    inner_ref[...] = jnp.zeros_like(inner_ref)
    loss_ref[...] = jnp.zeros_like(loss_ref)
    w_ref[:, width:, :CAP] = jnp.ones((groups, width, CAP), bf16)
    w_ref[:, width:, CAP:] = jnp.zeros((groups, width, CAP), bf16)

    def one_pass(k, carry):
        def bring(d):
            first, _, _ = chunk_of(meta_ref, d, 0, rows_all)
            return (
                pltpu.make_async_copy(w_hbm.at[k, d], w_ref.at[d, pl.ds(0, width), :], came.at[d]),
                pltpu.make_async_copy(
                    y_hbm.at[k, pl.ds(first, RB), :], y_ref.at[d], came.at[groups + d]
                ),
            )

        def leave(d):
            at = pl.ds(pl.multiple_of(d * CAP, LANE), CAP)
            return pltpu.make_async_copy(g_ref.at[:, at], g_hbm.at[k, :, at], gone.at[d])

        consts = pltpu.make_async_copy(c_hbm.at[k], c_ref, came.at[2 * groups])
        consts.start()
        for d in range(groups):
            for copy in bring(d):
                copy.start()
        consts.wait()

        def one_group(d, carry):
            for copy in bring(d):
                copy.wait()
            weight = w_ref[d]
            const = c_ref[d]
            at = pl.ds(pl.multiple_of(d * CAP, LANE), CAP)
            g_ref[:, at] = jnp.zeros((both + 16, CAP), f32)
            lower = width + 8

            def one_chunk(i, sums):
                first, low, high = chunk_of(meta_ref, d, i, rows_all)
                rows = pl.ds(first, RB)
                hidden = hidden_ref[rows, :]

                @pl.when(i > 0)
                def _():
                    pltpu.sync_copy(y_hbm.at[k, rows, :], y_ref.at[d])

                logit_ref[...] = jnp.dot(hidden, weight[:width], preferred_element_type=f32)

                def element(j, sums):
                    src = pl.ds(pl.multiple_of(j * step, step), step)
                    row = pl.ds(pl.multiple_of(first + j * step, 16), step)
                    shift = shift_ref[row, :]
                    halves, powers, num, den = sums[:4]
                    place = lax.broadcasted_iota(i32, (step, LANE), 0) + (first + j * step)
                    inside = (place >= low) & (place < high)
                    columns = []
                    for n, (start, wide) in enumerate(cuts(CAP, LANE)):
                        here = pl.ds(start, wide)
                        there = pl.ds(CAP + start, wide)
                        own = lambda k: c_ref[d, k : k + 1, start : start + wide]
                        theta = own(2)
                        y = jnp.where(inside, y_ref[d, src, here].astype(f32), -1.0)
                        mean = jnp.exp(logit_ref[src, here] + (own(0) + shift))
                        t = mean + own(5)
                        log_t = jnp.log(t)
                        inv_t = pl.reciprocal(t, approx=False)
                        down = own(6) - log_t
                        weighted_in = y >= 0.0
                        half = jnp.where(weighted_in, logit_ref[src, there] + own(1), 0.0)
                        joint = jnp.where(y == 0.0, (0.5 * theta) * down - half, 32.0 * y)
                        joint = jnp.where(weighted_in, joint, 0.0)
                        count = jnp.maximum(y, 0.0)
                        tan_drop = jnp.tanh(half)
                        tan_joint = jnp.tanh(joint)
                        one = jnp.where(weighted_in, 1.0, 0.0)
                        chance = one + tan_joint
                        pull = ((0.5 * theta) * chance + count) * inv_t
                        me = mean + log_eps
                        drift = (pull - count * pl.reciprocal(me, approx=False)) * mean
                        twice = tan_joint + tan_drop
                        grad_ref[src, here] = drift.astype(bf16)
                        grad_ref[src, there] = twice.astype(bf16)
                        slope = chance * (0.5 * (down + own(7))) - pull
                        fold = lambda v: jnp.sum(v.reshape(step // 8, 8, wide), axis=0)
                        old = sums[4 + n]
                        columns.append(
                            (
                                old[0] + fold(slope),
                                old[1] + fold(drift),
                                old[2] + fold(twice),
                                old[3] + fold(one * down),
                            )
                        )
                        halves = halves + (jnp.minimum(joint, 0.0) + jnp.maximum(half, 0.0))
                        powers = powers + count * (jnp.log(me) - log_t)
                        num = num + num * jnp.abs(tan_drop)
                        den = den + den * jnp.abs(tan_joint)
                    return (halves, powers, num, den, *columns)

                def clear(j, carry):
                    src = pl.ds(pl.multiple_of(j * step, step), step)
                    grad_ref[src, :] = jnp.zeros((step, 2 * CAP), bf16)
                    return carry

                steps = jnp.minimum((high - first + step - 1) // step, RB // step)
                one_rows = jnp.ones((step, LANE), f32)
                got = lax.fori_loop(
                    0, steps, element, (sums[0], sums[1], one_rows, one_rows, *sums[2:])
                )
                lax.fori_loop(steps, RB // step, clear, 0)
                halves, powers, num, den = got[:4]
                powers = powers + (jnp.log(num) - jnp.log(den))
                grads = grad_ref[...]
                outer = lax.dot_general(hidden, grads, by_first, preferred_element_type=f32)
                g_ref[:width, at] += outer[:, :CAP]
                g_ref[lower : lower + width, at] += outer[:, CAP:]
                sums_both = lax.dot_general(grads, weight, by_last, preferred_element_type=f32)
                back_ref[rows, :] += sums_both[:, :width]
                row_sum_ref[rows, :] += sums_both[:, width:]
                return (halves, powers, *got[4:])

            zero = jnp.zeros((8, LANE), f32)
            start_sums = (jnp.zeros((step, LANE), f32),) * 2 + tuple(
                (zero,) * 4 for _ in cuts(CAP, LANE)
            )
            chunks = (meta_ref[3 * d] + RB - 1) // RB
            got = lax.fori_loop(0, chunks, one_chunk, start_sums)
            count_sum = const[3:4, :LANE]
            for start, wide in cuts(CAP, LANE)[1:]:
                count_sum = count_sum + const[3:4, start : start + wide]
            parts = (got[1] - 2.0 * got[0]).reshape(step // 8, 8, LANE)
            total = jnp.sum(parts, axis=0) + jnp.where(
                lax.broadcasted_iota(i32, (8, LANE), 0) == 0, count_sum, 0.0
            )
            for n, (start, wide) in enumerate(cuts(CAP, LANE)):
                total = total + got[2 + n][3] * const[2:3, start : start + wide]
            loss_ref[...] += total
            for n, (start, wide) in enumerate(cuts(CAP, LANE)):
                here = pl.ds(pl.multiple_of(d * CAP + start, LANE), wide)
                slope, drift, twice = (
                    jnp.sum(v, axis=0, keepdims=True) for v in got[2 + n][:3]
                )
                g_ref[width : width + 1, here] = drift
                g_ref[both + 8 : both + 9, here] = twice
                g_ref[both + 9 : both + 10, here] = slope + const[4:5, start : start + wide]
            leave(d).start()
            return carry

        lax.fori_loop(0, groups, one_group, 0)
        for d in range(groups):
            leave(d).wait()
        return carry

    lax.fori_loop(0, pass_count(meta_ref, groups), one_pass, 0)
    for i in range(rows_all // LANE):
        tile = row_sum_ref[i * LANE : (i + 1) * LANE, :].T
        inner_ref[i : i + 1, :] = tile[0:1, :]


def likelihood(meta, hidden, shift, y, w, c):
    rows_all, width = hidden.shape
    passes, groups = w.shape[:2]
    both = 2 * width
    return pl.pallas_call(
        likelihood_kernel,
        in_specs=[smem(), vmem(), vmem(), anywhere(), anywhere(), anywhere()],
        out_specs=[vmem(), vmem(), vmem(), anywhere()],
        out_shape=[
            jax.ShapeDtypeStruct((rows_all, width), f32),
            jax.ShapeDtypeStruct((-(-rows_all // LANE // 8) * 8, LANE), f32),
            jax.ShapeDtypeStruct((8, LANE), f32),
            jax.ShapeDtypeStruct((passes, both + 16, groups * CAP), f32),
        ],
        scratch_shapes=[
            pltpu.VMEM((rows_all, LANE), f32),
            pltpu.VMEM((rows_all, width), f32),
            pltpu.VMEM((groups, RB, CAP), bf16),
            pltpu.VMEM((groups, both, 2 * CAP), bf16),
            pltpu.VMEM((groups, 8, CAP), f32),
            pltpu.VMEM((RB, 2 * CAP), f32),
            pltpu.VMEM((RB, 2 * CAP), bf16),
            pltpu.VMEM((both + 16, groups * CAP), f32),
            pltpu.SemaphoreType.DMA((2 * groups + 1,)),
            pltpu.SemaphoreType.DMA((groups,)),
        ],
        compiler_params=params(58),
        cost_estimate=cost(20),
        name="likelihood",
    )(meta, hidden, shift, y, w, c)


def expand_kernel(use_rows, first, tall, meta_ref, g_ref, pos_ref, *rest):
    if use_rows:
        row_ref, hidden_ref, line_ref, weight_ref, bias_ref = rest[:5]
        g_hbm, out_ref, pick_ref, more_ref, logit_ref, top_ref, total_ref = rest[5:]
    else:
        g_hbm, out_ref, pick_ref, more_ref, _, _, total_ref = rest
    groups = pos_ref.shape[0]
    genes = out_ref.shape[1]

    def choose(k, d):
        column = lax.broadcasted_iota(i32, (CAP, 1), 0) + k * CAP
        pick_ref[d * CAP : (d + 1) * CAP, :] = (
            (column == pos_ref[d : d + 1, :]).astype(f32).astype(bf16)[:, :genes]
        )

    def spread(k, g):
        for d in range(groups):
            choose(k, d)
        return jnp.dot(g.astype(bf16), pick_ref[...], preferred_element_type=f32)

    if use_rows:
        @pl.when(pl.program_id(0) == 0)
        def _():
            for i in range(hidden_ref.shape[0] // LANE):
                line = jnp.broadcast_to(line_ref[i : i + 1, :], (LANE, LANE))
                top_ref[i * LANE : (i + 1) * LANE, :] = line.T

        for d in range(groups):
            choose(0, d)
        logit_ref[...] = jnp.dot(hidden_ref[...], weight_ref[...], preferred_element_type=f32)
        sparse = jnp.dot(g_ref[0].astype(bf16), pick_ref[...], preferred_element_type=f32)
        total_ref[...] = sparse
        pieces = cuts(hidden_ref.shape[0], 2 * LANE)
        got = None
        for start, high in pieces:
            here = pl.ds(start, high)
            value = jnp.exp(logit_ref[here, :] + (bias_ref[...] - top_ref[here, 0:1]))
            more = jnp.dot(
                row_ref[:, start : start + high], value.astype(bf16), preferred_element_type=f32
            )
            got = more if got is None else got + more
        total_ref[...] -= got
    else:
        total_ref[...] = spread(0, g_ref[0])

    def more(k, carry):
        pltpu.sync_copy(g_hbm.at[k, pl.ds(first, tall), :], more_ref)
        total_ref[...] += spread(k, more_ref[...])
        return carry

    lax.fori_loop(1, pass_count(meta_ref, groups), more, 0)
    out_ref[...] = total_ref[...].astype(bf16)


def expand(meta, g, pos, genes, part, rows=None, hidden=None, top=None, weight=None, bias=None):
    groups = pos.shape[0]
    tall = g.shape[1] // 2
    block = 512 if genes % 512 == 0 else genes
    extra = [] if rows is None else [rows, hidden, top, weight, bias]
    extra_specs = []
    if extra:
        extra_specs = [pl.BlockSpec(v.shape, lambda i: (0, 0)) for v in (rows, hidden, top)]
        extra_specs += [pl.BlockSpec((v.shape[0], block), lambda i: (0, i)) for v in (weight, bias)]
    return pl.pallas_call(
        lambda *refs: expand_kernel(bool(extra), part * tall, tall, *refs),
        grid=(genes // block,),
        in_specs=[
            smem(),
            pl.BlockSpec((1, tall, groups * CAP), lambda i: (0, part, 0)),
            pl.BlockSpec((groups, -(-block // LANE) * LANE), lambda i: (0, i)),
            *extra_specs,
            anywhere(),
        ],
        out_specs=pl.BlockSpec((tall, block), lambda i: (0, i)),
        out_shape=jax.ShapeDtypeStruct((tall, genes), bf16),
        scratch_shapes=[
            pltpu.VMEM((groups * CAP, block), bf16),
            pltpu.VMEM((tall, groups * CAP), f32),
            pltpu.VMEM((8 if rows is None else hidden.shape[0], block), f32),
            pltpu.VMEM((8 if rows is None else hidden.shape[0], LANE), f32),
            pltpu.VMEM((tall, block), f32),
        ],
        compiler_params=params(58),
        cost_estimate=cost(8),
        name="expand",
    )(meta, g, pos, *extra, g)


def norm_parts(x, stats, affine, total):
    center = stats[0:1] * (1.0 / total)
    variance = stats[1:2] * (1.0 / total) - center * center
    inverse = lax.rsqrt(variance + norm_eps)
    normed = (x - center) * inverse
    gated = normed * affine[0:1] + affine[1:2]
    sigma = 0.5 + 0.5 * jnp.tanh(0.5 * gated)
    return normed, inverse, gated, sigma


def two_rows(first, second):
    row = lax.broadcasted_iota(i32, (8, first.shape[1]), 0)
    return jnp.where(row == 0, first, jnp.where(row == 1, second, 0.0))


def sums_of(x):
    return two_rows(
        jnp.sum(x, axis=0, keepdims=True), jnp.sum(x * x, axis=0, keepdims=True)
    )


def exact(a, b, dims):
    return lax.dot_general(a, b, dims, precision=highest, preferred_element_type=f32)


plain = (((1,), (0,)), ((), ()))


def batch_rows(batch_ref, count):
    names = lax.broadcasted_iota(i32, (count, 1), 0)
    return (names == batch_ref[...]).astype(f32)


def latent_kernel(
    total, x_ref, stat_ref, affine_ref, heads_ref, bias_ref, noise_ref, decode_ref, add_ref,
    pre_ref, sums_ref, latent_ref, kl_ref,
):
    _, _, gated, sigma = norm_parts(x_ref[...], stat_ref, affine_ref, total)
    act = gated * sigma
    heads = exact(heads_ref[...], act, by_last) + bias_ref[:, 0:1]
    mean, logvar = heads[:16], heads[16:]
    scale = jnp.exp(0.5 * logvar)
    latent = mean + scale * noise_ref[...]
    latent_ref[0:16, :] = mean
    latent_ref[16:32, :] = logvar
    latent_ref[32:48, :] = latent
    latent_ref[48:64, :] = scale
    terms = jnp.exp(logvar) + mean * mean - 1.0 - logvar
    folded = jnp.zeros((16, LANE), f32)
    for start, width in cuts(terms.shape[1], LANE):
        folded = folded + terms[:, start : start + width]
    kl_ref[...] = 0.5 * (folded[:8] + folded[8:])
    pre = exact(latent, decode_ref[...], by_first) + add_ref[...]
    pre_ref[...] = pre
    sums_ref[...] = sums_of(pre)


def latent_stage(total, x, stat, affine, heads, bias, noise, decode, add):
    cells, width = x.shape
    return pl.pallas_call(
        lambda *refs: latent_kernel(total, *refs),
        in_specs=[vmem()] * 8,
        out_specs=[vmem()] * 4,
        out_shape=[
            jax.ShapeDtypeStruct((cells, width), f32),
            jax.ShapeDtypeStruct((8, width), f32),
            jax.ShapeDtypeStruct((64, cells), f32),
            jax.ShapeDtypeStruct((8, LANE), f32),
        ],
        compiler_params=params(18),
        cost_estimate=cost(2),
        name="latent_stage",
    )(x, stat, affine, heads, bias, noise, decode, add)


def hidden_kernel(total, pre_ref, stat_ref, affine_ref, rank_ref, lib_ref, hidden_ref, sum_ref, carry_ref):
    width = pre_ref.shape[1]
    rows_all = hidden_ref.shape[0]
    _, _, gated, sigma = norm_parts(pre_ref[...], stat_ref, affine_ref, total)
    carry_ref[:, :width] = (gated * sigma).astype(bf16)
    lib = jnp.sum(lib_ref[...], axis=1, keepdims=True)
    lane = lax.broadcasted_iota(i32, (lib.shape[0], LANE), 1)
    high = lib.astype(bf16).astype(f32)
    middle = (lib - high).astype(bf16).astype(f32)
    low = lib - high - middle
    carry_ref[:, width:] = jnp.where(
        lane == 0, high, jnp.where(lane == 1, middle, jnp.where(lane == 2, low, 0.0))
    ).astype(bf16)
    block = 2 * row_block(rows_all) if rows_all % 128 == 0 else rows_all

    def body(i, carry):
        first = pl.multiple_of(i * block, ALIGN)
        place = lax.broadcasted_iota(i32, (block, 1), 0) + first
        pick = (place == rank_ref[...]).astype(f32).astype(bf16)
        got = jnp.dot(pick, carry_ref[...], preferred_element_type=f32)
        hidden_ref[pl.ds(first, block), :] = got[:, :width].astype(bf16)
        sum_ref[pl.ds(first, block), :] = jnp.broadcast_to(
            jnp.sum(got[:, width:], axis=1, keepdims=True), (block, LANE)
        )
        return carry

    lax.fori_loop(0, rows_all // block, body, 0)


def hidden_stage(total, pre, stat, affine, rank, lib, rows_all):
    cells, width = pre.shape
    return pl.pallas_call(
        lambda *refs: hidden_kernel(total, *refs),
        in_specs=[vmem()] * 5,
        out_specs=[vmem()] * 2,
        out_shape=[
            jax.ShapeDtypeStruct((rows_all, width), bf16),
            jax.ShapeDtypeStruct((rows_all, LANE), f32),
        ],
        scratch_shapes=[pltpu.VMEM((cells, width + LANE), bf16)],
        compiler_params=params(18),
        cost_estimate=cost(5),
        name="hidden_stage",
    )(pre, stat, affine, rank, lib)


def decoder_back_kernel(
    total, latents, rank_ref, back_ref, exp_back_ref, scale_ref, pre_ref, stat_ref, affine_ref,
    decode_ref, latent_ref, batch_ref, loss_ref,
    pull_ref, sorted_ref, grad_ref,
):
    rows_all, width = back_ref.shape
    cells = pre_ref.shape[0]
    lines = cells // LANE
    fixed = -(-latents * lines // 8) * 8
    names = pull_ref.shape[0] - fixed - 24
    for i in range(rows_all // LANE):
        tile = pl.ds(i * LANE, LANE)
        scale = jnp.broadcast_to(scale_ref[i : i + 1, :], (LANE, LANE)).T
        sorted_ref[tile, :] = back_ref[tile, :] - exp_back_ref[tile, :] * scale
    block = 512
    unroll = 32

    def move(j, carry):
        base = pl.multiple_of(j * unroll, unroll)
        rows = [sorted_ref[pl.ds(rank_ref[base + u], 1), :] for u in range(unroll)]
        grad_ref[pl.ds(base, unroll), :] = jnp.concatenate(rows, axis=0)
        return carry

    lax.fori_loop(0, cells // unroll, move, 0)
    first = jnp.zeros((1, width), f32)
    second = jnp.zeros((1, width), f32)
    weight = jnp.zeros((16 + names, width), f32)
    for start, tall in cuts(cells, block):
        rows = pl.ds(start, tall)
        grad = grad_ref[rows, :]
        normed, inverse, gated, sigma = norm_parts(pre_ref[rows, :], stat_ref, affine_ref, total)
        inner = grad * sigma * (1.0 + gated * (1.0 - sigma))
        first = first + jnp.sum(inner, axis=0, keepdims=True)
        second = second + jnp.sum(inner * normed, axis=0, keepdims=True)
        pull = exact(decode_ref[...] * (inverse * affine_ref[0:1, :]), inner, by_last)
        for l in range(latents):
            for j in range(tall // LANE):
                at = l * lines + start // LANE + j
                pull_ref[at : at + 1, :] = pull[l : l + 1, j * LANE : (j + 1) * LANE]
        hot = (lax.broadcasted_iota(i32, (names, 1), 0) == batch_ref[:, rows]).astype(f32)
        side = jnp.concatenate([latent_ref[32:48, rows], hot], axis=0)
        weight = weight + exact(side, inner, plain)
    if fixed > latents * lines:
        pull_ref[latents * lines : fixed, :] = jnp.zeros((fixed - latents * lines, LANE), f32)
    loss = jnp.sum(loss_ref[...], axis=0, keepdims=True)
    row = lax.broadcasted_iota(i32, (8, LANE), 0)
    pull_ref[fixed : fixed + 8, :] = jnp.where(row == 2, loss, two_rows(first, second))
    pull_ref[fixed + 8 :, :] = weight


def decoder_back(
    total, latents, rank, back, exp_back, scale, pre, stat, affine, decode, latent, batch, loss, names
):
    rows_all, width = back.shape
    cells = pre.shape[0]
    return pl.pallas_call(
        lambda *refs: decoder_back_kernel(total, latents, *refs),
        in_specs=[smem()] + [vmem()] * 10,
        out_specs=vmem(),
        out_shape=jax.ShapeDtypeStruct(
            (-(-latents * (cells // LANE) // 8) * 8 + 24 + names, LANE), f32
        ),
        scratch_shapes=[pltpu.VMEM((rows_all, width), f32), pltpu.VMEM((cells, width), f32)],
        compiler_params=params(22),
        cost_estimate=cost(8),
        name="decoder_back",
    )(rank, back, exp_back, scale, pre, stat, affine, decode, latent, batch, loss)


def encoder_back_kernel(
    total, latents, pull_ref, inner_ref, pre_ref, stat_ref, affine_ref,
    x_ref, x_stat_ref, x_affine_ref, latent_ref, noise_ref, heads_ref, decode_ref,
    batch_ref, kl_ref,
    inner_out, sums_ref, pack_ref,
):
    cells, width = pre_ref.shape
    lines = cells // LANE
    fixed_rows = -(-latents * lines // 8) * 8
    names = pull_ref.shape[0] - fixed_rows - 24
    normed, inverse, _, _ = norm_parts(pre_ref[...], stat_ref, affine_ref, total)
    factor = inverse * affine_ref[0:1, :]
    shift_mean = inner_ref[0:1, :] * (1.0 / total)
    gain_mean = inner_ref[1:2, :] * (1.0 / total)
    decode = decode_ref[...] * factor
    fixed = jnp.sum(decode * shift_mean, axis=1, keepdims=True)
    moving = exact(decode * gain_mean, normed, by_last)
    pulls = []
    for l in range(latents):
        pieces = [pull_ref[l * lines + j : l * lines + j + 1, :] for j in range(lines)]
        pulls.append(jnp.concatenate(pieces, axis=1))
    pulls.append(jnp.zeros((16 - latents, cells), f32))
    pull = jnp.concatenate(pulls, axis=0) - fixed - moving
    mean, logvar = latent_ref[0:16, :], latent_ref[16:32, :]
    latent, scale = latent_ref[32:48, :], latent_ref[48:64, :]
    grad_mean = pull + mean
    grad_logvar = 0.5 * pull * noise_ref[...] * scale + 0.5 * (jnp.exp(logvar) - 1.0)
    grads = jnp.concatenate([grad_mean, grad_logvar], axis=0)
    grad_act = exact(grads, heads_ref[...], by_first)
    x_normed, _, gated, sigma = norm_parts(x_ref[...], x_stat_ref, x_affine_ref, total)
    inner = grad_act * sigma * (1.0 + gated * (1.0 - sigma))
    inner_out[...] = inner
    loss = jnp.sum(kl_ref[...], axis=0, keepdims=True) - pull_ref[fixed_rows + 2 : fixed_rows + 3, :]
    sums_ref[...] = two_rows(
        jnp.sum(inner, axis=0, keepdims=True), jnp.sum(inner * x_normed, axis=0, keepdims=True)
    ) + jnp.where(lax.broadcasted_iota(i32, (8, LANE), 0) == 2, loss, 0.0)
    side = jnp.concatenate([latent, batch_rows(batch_ref, names)], axis=0)
    side_sum = jnp.sum(side, axis=1, keepdims=True)
    fix = side_sum * shift_mean + exact(side, normed, plain) * gain_mean
    at = 16 + names
    pack_ref[:at, :] = factor * (pull_ref[fixed_rows + 8 :, :] - fix)
    pack_ref[at : at + 32, :] = exact(grads, gated * sigma, plain)
    pack_ref[at + 32 : at + 64, :] = jnp.broadcast_to(jnp.sum(grads, axis=1, keepdims=True), (32, LANE))


def encoder_back(
    total, latents, pull, inner, pre, stat, affine, x, x_stat, x_affine, latent, noise,
    heads, decode, batch, kl, names,
):
    cells, width = pre.shape
    return pl.pallas_call(
        lambda *refs: encoder_back_kernel(total, latents, *refs),
        in_specs=[vmem()] * 14,
        out_specs=[vmem()] * 3,
        out_shape=[
            jax.ShapeDtypeStruct((cells, width), f32),
            jax.ShapeDtypeStruct((8, width), f32),
            jax.ShapeDtypeStruct((names + 80, width), f32),
        ],
        compiler_params=params(22),
        cost_estimate=cost(3),
        name="encoder_back",
    )(pull, inner, pre, stat, affine, x, x_stat, x_affine, latent, noise, heads, decode, batch, kl)


def encoder_grad_kernel(
    total, block, inner_ref, x_ref, stat_ref, affine_ref, sums_ref, batch_ref, pack_ref, counts_hbm,
    out_ref, grad_ref, counts_ref, expr_ref, came,
):
    cells, genes = counts_ref.shape
    packed = pack_ref.shape[0]
    names = packed - 80
    columns = [pl.ds(i * block, block) for i in range(genes // block)]
    copies = [
        pltpu.make_async_copy(counts_hbm.at[:, at], counts_ref.at[:, at], came.at[i])
        for i, at in enumerate(columns)
    ]
    for copy in copies:
        copy.start()
    normed, inverse, _, _ = norm_parts(x_ref[...], stat_ref, affine_ref, total)
    factor = inverse * affine_ref[0:1, :]
    grad = factor * (
        inner_ref[...]
        - sums_ref[0:1, :] * (1.0 / total)
        - normed * (sums_ref[1:2, :] * (1.0 / total))
    )
    low = grad.astype(bf16)
    grad_ref[...] = low
    turned = low.astype(f32).T.astype(bf16)
    hot = batch_rows(batch_ref, names).astype(bf16)
    got = jnp.dot(hot, low, preferred_element_type=f32)
    small = jnp.concatenate([pack_ref[...], got], axis=0)
    tall = packed + names
    high = small.astype(bf16)
    out_ref[genes : genes + tall, :] = high
    out_ref[genes + tall : genes + 2 * tall, :] = (small - high.astype(f32)).astype(bf16)
    rest = out_ref.shape[0] - genes - 2 * tall
    if rest:
        out_ref[genes + 2 * tall :, :] = jnp.zeros((rest, out_ref.shape[1]), bf16)
    chunk = 256
    for i in range(len(columns) + 1):
        if i < len(columns):
            copies[i].wait()
        got = None
        for first in range(0, cells, chunk):
            rows = pl.ds(first, chunk)
            if i < len(columns):
                real = counts_ref[rows, columns[i]].astype(f32)
                expr_ref[i % 2, rows, :] = jnp.log(1.0 + real).astype(bf16)
            if i > 0:
                more = jnp.dot(
                    turned[:, first : first + chunk],
                    expr_ref[(i - 1) % 2, rows, :],
                    preferred_element_type=f32,
                )
                got = more if got is None else got + more
        if i > 0:
            out_ref[columns[i - 1], :] = got.T.astype(bf16)


def encoder_grad(total, inner, x, stat, affine, sums, batch, pack, counts, shares):
    cells, width = x.shape
    genes = counts.shape[1]
    block = 512 if genes % 512 == 0 else genes
    rows = genes + 2 * (2 * pack.shape[0] - 80)
    rows = -(-rows // (ALIGN * shares)) * ALIGN * shares
    return pl.pallas_call(
        lambda *refs: encoder_grad_kernel(total, block, *refs),
        in_specs=[vmem()] * 7 + [anywhere()],
        out_specs=[vmem()] * 2,
        out_shape=[
            jax.ShapeDtypeStruct((rows, width), bf16),
            jax.ShapeDtypeStruct((cells, width), bf16),
        ],
        scratch_shapes=[
            pltpu.VMEM((cells, genes), i32),
            pltpu.VMEM((2, cells, block), bf16),
            pltpu.SemaphoreType.DMA((genes // block,)),
        ],
        compiler_params=params(48),
        cost_estimate=cost(7),
        name="encoder_grad",
    )(inner, x, stat, affine, sums, batch, pack, counts)


def input_grad_kernel(grad_ref, weight_ref, out_ref):
    out_ref[...] = lax.dot_general(
        grad_ref[...], weight_ref[...], by_last, preferred_element_type=f32
    )


def input_grad(grad, weight):
    cells, width = grad.shape
    genes = weight.shape[0]
    block = 256
    return pl.pallas_call(
        input_grad_kernel,
        grid=(cells // block,),
        in_specs=[
            pl.BlockSpec((block, width), lambda i: (i, 0)),
            pl.BlockSpec((genes, width), lambda i: (0, 0)),
        ],
        out_specs=pl.BlockSpec((block, genes), lambda i: (i, 0)),
        out_shape=jax.ShapeDtypeStruct((cells, genes), f32),
        compiler_params=params(14),
        cost_estimate=cost(9),
        name="input_grad",
    )(grad, weight)


def body(
    counts,
    batch_ids,
    dataset_ids,
    variable_mask,
    latent_noise,
    encoder_weight,
    encoder_batch,
    encoder_gain,
    encoder_shift,
    mean_weight,
    mean_bias,
    logvar_weight,
    logvar_bias,
    decoder_latent,
    decoder_batch,
    decoder_gain,
    decoder_shift,
    scale_weight,
    scale_bias,
    dropout_weight,
    dropout_bias,
    log_theta,
):
    cells, genes = counts.shape
    groups = variable_mask.shape[0]
    width = encoder_weight.shape[1]
    latents = mean_weight.shape[1]
    names = encoder_batch.shape[0]
    total_cells = cells * lax.axis_size("cells")
    gene_parts = lax.axis_size("genes")
    inverse_cells = 1.0 / total_cells
    pieces = 4 if genes % (4 * LANE) == 0 else 1
    rows_all = -(-(cells + groups * ALIGN) // LANE) * LANE

    partial_pre, lib_lanes = encode(counts, encoder_weight)
    pre_pieces = rows_pieces(partial_pre, WIRE)

    pos, rank, meta = order_cells(variable_mask, dataset_ids)
    extra = [*split3(scale_bias), *split3(0.5 * dropout_bias), *split3(log_theta)]
    extra = jnp.concatenate([jnp.stack(extra), jnp.zeros((16 - len(extra), genes), bf16)])
    batch_row = batch_ids.reshape(1, cells)
    batch_hot = (batch_ids[:, None] == jnp.arange(names)[None, :]).astype(f32)
    encoder_add = jnp.dot(batch_hot, encoder_batch, precision=highest)
    decoder_add = jnp.dot(batch_hot, decoder_batch, precision=highest)
    pad_rows = lambda v, n=16: jnp.pad(v, ((0, n - v.shape[0]), (0, 0)))
    noise = pad_rows(latent_noise.T)
    heads = jnp.concatenate([pad_rows(mean_weight.T), pad_rows(logvar_weight.T)])
    head_bias = jnp.concatenate([pad_rows(mean_bias[:, None]), pad_rows(logvar_bias[:, None])])
    head_bias = jnp.broadcast_to(head_bias, (32, LANE))
    decode = pad_rows(decoder_latent)
    encoder_affine = pad_rows(jnp.stack([encoder_gain, encoder_shift]), 8)
    decoder_affine = pad_rows(jnp.stack([decoder_gain, decoder_shift]), 8)

    def own_genes(members, rows, before):
        return compact(
            members, meta, rows, pos, scale_weight, dropout_weight, extra, genes, pieces, before
        )

    batches = [[d for d in range(groups) if d * 8 // groups in some] for some in ((0, 1, 2), (3, 4), (5, 6), (7,))]

    pre_pieces, rank = after(pre_pieces, rank)
    pre_parts = exchange(pre_pieces, "genes", 2)
    sorted_rows = sort_rows(rank.reshape(cells), counts, pieces, rows_all)
    pre_parts, sorted_rows = after(pre_parts, sorted_rows)
    pre_own, sorted_rows = after(join(pre_parts, WIRE), sorted_rows)
    pre_blocks = spread_out(pre_own, "genes", 2)
    ycw = own_genes(batches[0], sorted_rows, None)
    pre_blocks, ycw = after(pre_blocks, ycw)
    x = rows_whole(assemble(pre_blocks, "genes", 0, 2)) + encoder_add
    x_sums = pad_rows(jnp.stack([jnp.sum(x, axis=0), jnp.sum(x * x, axis=0)]), 8)
    x_sums, sorted_rows = after(x_sums, sorted_rows)
    x_stat = total_direct(x_sums, "cells")
    ycw = own_genes(batches[1], sorted_rows, ycw)
    x_stat, ycw = after(x_stat, ycw)
    pre, sums, latent, kl_lanes = latent_stage(
        total_cells, x, x_stat, encoder_affine, heads, head_bias, noise, decode, decoder_add
    )
    sums, sorted_rows = after(sums, sorted_rows)
    stat = total_direct(sums, "cells")
    ycw = own_genes(batches[2], sorted_rows, ycw)
    stat, ycw = after(stat, ycw)
    hidden, lib_sorted = hidden_stage(
        total_cells, pre, stat, decoder_affine, rank, lib_lanes, rows_all
    )

    own, exp_back = softmax_part(hidden, lib_sorted, scale_weight, scale_bias.reshape(1, genes))
    own, sorted_rows = after(own, sorted_rows)
    pair = jnp.stack([own, swap(own, "genes", 1)])
    pair, sorted_rows = after(pair, sorted_rows)
    gathered = [pair] + [swap(pair, "genes", 2 * s) for s in range(1, gene_parts // 2)]
    ycw = own_genes(batches[3], sorted_rows, ycw)
    gathered, ycw = after(gathered, ycw)
    tops = [g[i, 0] for g in gathered for i in range(2)]
    top = tops[0]
    for t in tops[1:]:
        top = jnp.maximum(top, t)
    exp_total = tree_sum(
        [g[0, 1] * jnp.exp(g[0, 0] - top) + g[1, 1] * jnp.exp(g[1, 0] - top) for g in gathered]
    )
    exp_total = jnp.maximum(exp_total, 1e-30)
    library = tree_sum([g[0, 2] + g[1, 2] for g in gathered])
    own_scale = jnp.exp(own[0] - top) / exp_total
    shift = jnp.where(
        library > 0.0,
        jnp.log(jnp.maximum(library, 1.0)) - jnp.log(exp_total) - top,
        -1e30,
    )
    back, inner_rows, loss_lanes, g = likelihood(meta, hidden, shift, *ycw)
    inner_rows = inner_rows + swap(inner_rows, "genes", 1)
    inner_rows, g = after(inner_rows, g)
    inner_total = total_direct(inner_rows, "genes", 2)
    dropout_spread = expand(meta, g, pos, genes, 1)
    inner_total, dropout_spread = after(inner_total, dropout_spread)
    row_scale = inner_total * own_scale
    dropout_pieces = pieces_for(dropout_spread, "cells", 1, bf16)
    dropout_pieces, row_scale = after(dropout_pieces, row_scale)
    dropout_parts = exchange(dropout_pieces, "cells")
    pull = decoder_back(
        total_cells, latents, rank.reshape(cells), back, exp_back, row_scale, pre, stat, decoder_affine,
        decode, latent, batch_row, loss_lanes, names,
    )
    row_flat = row_scale.reshape(1, -1)[:, :rows_all]
    row_scaled = jnp.concatenate(
        [
            (hidden.T.astype(f32) * row_flat).astype(bf16),
            row_flat.astype(bf16),
            jnp.zeros((7, rows_all), bf16),
        ]
    )
    pull = pull + swap(pull, "genes", 1)
    pull, row_scaled = after(pull, row_scaled)
    pull = total_direct(pull, "genes", 2)
    row_scaled, dropout_parts = after(row_scaled, dropout_parts)
    dropout_own, row_scaled = after(join(dropout_parts, bf16), row_scaled)
    scale_spread = expand(
        meta, g, pos, genes, 0, row_scaled, hidden, own[0], scale_weight, scale_bias.reshape(1, genes)
    )
    dropout_blocks = spread_out(dropout_own, "cells")
    pull, scale_spread = after(pull, scale_spread)
    sums_at = -(-latents * (cells // LANE) // 8) * 8
    decoder_sums = total_direct(pull[sums_at : sums_at + 8], "cells")
    inner, sums, pack = encoder_back(
        total_cells, latents, pull, decoder_sums, pre, stat, decoder_affine,
        x, x_stat, encoder_affine, latent, noise, heads, decode, batch_row, kl_lanes, names,
    )
    sums = total_direct(sums, "cells")
    scale_pieces = pieces_for(scale_spread, "cells", 1, bf16)
    scale_pieces, sums, dropout_blocks = after(scale_pieces, sums, dropout_blocks)
    scale_parts = exchange(scale_pieces, "cells")
    encoder_weight_grad, grad_pre_low = encoder_grad(
        total_cells, inner, x, x_stat, encoder_affine, sums, batch_row, pack, counts,
        lax.axis_size("cells"),
    )
    encoder_weight_grad, scale_parts = after(encoder_weight_grad, scale_parts)
    encoder_pieces = pieces_for(encoder_weight_grad, "cells", 0, bf16)
    encoder_pieces, grad_pre_low = after(encoder_pieces, grad_pre_low)
    encoder_parts = exchange(encoder_pieces, "cells")
    input_gradient = input_grad(grad_pre_low, encoder_weight)
    encoder_parts, input_gradient, scale_parts = after(encoder_parts, input_gradient, scale_parts)
    encoder_blocks = spread_out(join(encoder_parts, bf16), "cells")
    scale_blocks = spread_out(join(scale_parts, bf16), "cells")
    encoder_blocks[1], dropout_blocks = after(encoder_blocks[1], dropout_blocks)
    dropout_spread = assemble(dropout_blocks, "cells", 1).astype(f32)
    scale_spread = assemble(scale_blocks, "cells", 1).astype(f32)
    encoder_low = assemble(encoder_blocks, "cells", 0)
    encoder_total = encoder_low[:genes].astype(f32) * inverse_cells
    tall = 2 * pack.shape[0] - 80
    pack = encoder_low[genes : genes + tall].astype(f32) + encoder_low[
        genes + tall : genes + 2 * tall
    ].astype(f32)
    pack = pack * inverse_cells

    scale_total = scale_spread[:width] * inverse_cells
    dropout_total = dropout_spread[:width] * (0.5 * inverse_cells)
    scale_bias_total = scale_spread[width] * inverse_cells
    dropout_bias_total = dropout_spread[width] * (0.5 * inverse_cells)
    theta_total = -jnp.exp(log_theta) * dropout_spread[width + 1] * inverse_cells
    at = 16 + names
    mean_loss = jnp.sum(sums[2]) * inverse_cells
    return (
        mean_loss,
        input_gradient,
        encoder_total,
        pack[at + 64 : at + 64 + names],
        sums[1] * inverse_cells,
        sums[0] * inverse_cells,
        pack[at : at + latents].T,
        pack[at + 32 : at + 32 + latents, 0],
        pack[at + 16 : at + 16 + latents].T,
        pack[at + 48 : at + 48 + latents, 0],
        pack[:latents],
        pack[16 : 16 + names],
        decoder_sums[1] * inverse_cells,
        decoder_sums[0] * inverse_cells,
        scale_total,
        scale_bias_total,
        dropout_total,
        dropout_bias_total,
        theta_total,
    )


def solution(mesh):
    return jax.shard_map(
        body,
        mesh=mesh,
        in_specs=(
            P("cells", "genes"),
            P("cells"),
            P("cells"),
            P(None, "genes"),
            P("cells", None),
            P("genes", None),
            P(),
            P(),
            P(),
            P(),
            P(),
            P(),
            P(),
            P(),
            P(),
            P(),
            P(),
            P(None, "genes"),
            P("genes"),
            P(None, "genes"),
            P("genes"),
            P("genes"),
        ),
        out_specs=(
            P(),
            P("cells", "genes"),
            P("genes", None),
            P(),
            P(),
            P(),
            P(),
            P(),
            P(),
            P(),
            P(),
            P(),
            P(),
            P(),
            P(None, "genes"),
            P("genes"),
            P(None, "genes"),
            P("genes"),
            P("genes"),
        ),
        check_vma=False,
    )
```
